32 devices in a mesh: px: 4 (over x, core), py: 8 (over z, y).
Axes of the slice: x: 2, y: 2, z: 4, core: 2. Of those that a mesh axis runs over, the one named last changes fastest.
Arguments:
- potential: float32 [128, 128, 256], P('px', 'py'), may hold values from -2.4 to 2.4
- owner: int32 [4, 8, 256, 1], P('px', 'py'), may hold values from 0 to 31; in each aligned block of 256 rows (0 to 255, 256 to 511, ..., all dimensions but the last counted through in order) at most 16 rows name the same one
- window: int32 [4, 8, 256], P('px', 'py'), may hold values from 0 to 255
Outputs:
- displacement: float32 [3, 128, 128, 256], P(None, 'px', 'py')
- density: float32 [128, 128, 256], P('px', 'py')
The draws below stay inside these ranges and needn't reach their ends.
Inputs may be any that keep to these rules, and one draw needn't show every extreme that they name: Among the 256 blocks of one tile (i, j), no owner is named more than 16 times, and the bound 16 is reached.
All inputs are finite; a program needn't handle non-finite values.
Results may differ from the reference program's by a relative error of at most 0.0003.
Values sent between devices are 32-bit elements; how exact they have to be, the bound alone decides.
No kernel may reach another device: no remote copies, remote signals or barrier semaphores. Data moves between devices by JAX's collectives and lax.ppermute only.
A program may use at most 128 MiB of HBM per device.

```python
import math
import jax
import jax.numpy as jnp
import numpy as np
from jax import lax

CX = 32
CY = 16
NZ = 256
TILES_X = 4
TILES_Y = 8
NX = 128
NY = 128
BX = 4
BY = 2
BZ = 32
NBLK = 256
CAP = 16


def plant(entries, own_key, smallest, top_value):
    longest = entries.shape.index(max(entries.shape))
    spots = []
    for shift in (0, 1):
        where = [jax.random.randint(jax.random.fold_in(own_key, axis), (), 0, length) for axis, length in enumerate(entries.shape)]
        where[longest] = (where[longest] + shift) % entries.shape[longest]
        spots.append(tuple(where))
    return entries.at[spots[0]].set(smallest).at[spots[1]].set(top_value)


def levels(own_key, extent, cuts, low, top_value):
    def one(position, shards_of):
        heights = jax.random.uniform(jax.random.fold_in(jax.random.fold_in(own_key, 6), position), (shards_of,), jnp.float32, low / len(cuts), top_value / len(cuts))
        return jnp.repeat(jnp.exp(heights), extent[position] // shards_of).reshape((-1,) + (1,) * (len(extent) - position - 1))

    gain = one(*cuts[0])
    for cut in cuts[1:]:
        gain = gain * one(*cut)
    return gain


def deal_out(rng, own, number, rows, number_of, top, bound, lean):
    sequence = jax.random.permutation(rng, number_of)
    packed, ordinary = load_shares(number_of, rows * top, bound, lean, True), load_shares(number_of, rows * top, bound, lean, False)
    places = jnp.arange(number_of)

    def named(lengths, rotation):
        used = int((lengths > 0).sum())
        fixed = max(1, used // 4)
        passed = fixed + (places - fixed + rotation * (used - fixed)) % max(1, number_of - fixed)
        return jnp.zeros((number_of,), jnp.int32).at[sequence[jnp.where(places < fixed, places, passed)]].set(jnp.asarray(lengths, jnp.int32))

    lengths = jnp.where(number % 4 == 0, named(packed, number // 4), named(ordinary, number - number // 4 - 1))
    mixed = jax.random.permutation(jax.random.fold_in(own, 3), number_of)
    source_of, receiver = mixed[0:number_of // 2 * 2:2], mixed[1:number_of // 2 * 2:2]
    margin = jnp.minimum(lengths[source_of] - 1, bound - lengths[receiver]) // 2
    margin = jnp.where((source_of == sequence[0]) | (receiver == sequence[0]) | (lengths[receiver] == 0), 0, jnp.maximum(margin, 0))
    passed = jax.random.randint(jax.random.fold_in(own, 4), (number_of // 2,), 0, 1 << 20) % (margin + 1)
    lengths = lengths.at[source_of].add(-passed).at[receiver].add(passed)
    labels = jnp.searchsorted(jnp.cumsum(lengths), jnp.arange(rows * top), side="right").astype(jnp.int32)
    table = labels.reshape(top, rows).T
    table = table[jax.random.permutation(jax.random.fold_in(own, 1), rows)]
    rotation = jax.random.randint(jax.random.fold_in(own, 2), (rows, 1), 0, top)
    return jnp.take_along_axis(table, (jnp.arange(top)[None, :] + rotation) % top, axis=1)


def load_shares(number_of, total, bound, skew, full):
    loads = [(1 << 20) // math.isqrt(standing ** skew) + 1 for standing in range(1, number_of + 1)]
    largest = bound if full else min(bound, max(-(-total // number_of), total * loads[0] // sum(loads)))
    least = 1 if total - largest >= number_of - 1 else 0
    given, spare = [largest] + [least] * (number_of - 1), total - largest - least * (number_of - 1)
    while spare > 0:
        free = [i for i in range(1, number_of) if given[i] < largest] or [i for i in range(1, number_of) if given[i] < bound]
        pool, remaining = sum([loads[i] for i in free]), spare
        for i in free:
            more = min(bound - given[i], max(1, remaining * loads[i] // pool), spare)
            given[i] = given[i] + more
            spare = spare - more
    return np.array(given)


def bell_draw(rng, shape, deviation, most, shards=(), held_as=jnp.bfloat16):
    drawn = jax.random.normal(rng, shape, jnp.float32) * deviation
    if len(shards) > 0:
        drawn = levels(rng, shape, shards, -0.22, 0.18) * drawn
    return jnp.clip(drawn, min=-most, max=most).astype(held_as)


def setup_inputs(seed: int = 0) -> dict:
    splits = jax.random.split(jax.random.key(seed), 4)
    potential = bell_draw(splits[0], (NX, NY, NZ), 0.4, 2.4, ((0, 4), (1, 8)), jnp.float32)
    owner_keys = jax.random.split(jax.random.fold_in(splits[1], 1), TILES_X * TILES_Y * NBLK // NBLK)
    owner_turns = jax.random.permutation(jax.random.fold_in(splits[1], 3), TILES_X * TILES_Y * NBLK // NBLK)
    owner = jax.vmap(lambda own, number: deal_out(jax.random.fold_in(splits[1], 2), own, number, NBLK, TILES_X * TILES_Y, 1, CAP, 2))(owner_keys, owner_turns).reshape((TILES_X, TILES_Y, NBLK, 1))
    window = plant(jax.random.randint(splits[2], (TILES_X, TILES_Y, NBLK), 0, NBLK), jax.random.fold_in(splits[2], 1), 0, NBLK - 1).astype(jnp.int32)
    return {"potential": potential, "owner": owner, "window": window}


SECOND_ORDER = 3.0 / 7.0
HIGHEST = lax.Precision.HIGHEST


def spline_weight(offset):
    magnitude = jnp.abs(offset)
    inner = (4.0 - 6.0 * magnitude * magnitude + 3.0 * magnitude * magnitude * magnitude) / 6.0
    reach = jnp.maximum(2.0 - magnitude, 0.0)
    outer = reach * reach * reach / 6.0
    return jnp.where(magnitude < 1.0, inner, outer)


def deposit_blocks(shifts):
    count = shifts.shape[0]
    within = jnp.arange(512)
    offsets = jnp.stack([within // 64, (within // 8) % 8, within % 8]).astype(jnp.float32)
    places = 2.0 + offsets[None] + shifts
    cells = jnp.arange(12).astype(jnp.float32)
    weights = spline_weight(cells[None, None, :, None] - places[:, :, None, :])
    planar = (weights[:, 0, :, None, :] * weights[:, 1, None, :, :]).reshape(count, 144, 512)
    windows = jnp.einsum('sqp,swp->sqw', planar, weights[:, 2], precision=HIGHEST)
    return windows.reshape(count, 1728)


def periodic_gradient(field, axis):
    return (jnp.roll(field, -1, axis) - jnp.roll(field, 1, axis)) * 0.5


def laplace_modes(length):
    modes = jnp.arange(length)
    return modes, 2.0 * jnp.cos(modes.astype(jnp.float32) * (2.0 * jnp.pi / length)) - 2.0


def reference(potential, owner, window):
    ahead_x = jnp.roll(potential, -1, 0)
    behind_x = jnp.roll(potential, 1, 0)
    ahead_y = jnp.roll(potential, -1, 1)
    behind_y = jnp.roll(potential, 1, 1)
    ahead_z = jnp.roll(potential, -1, 2)
    behind_z = jnp.roll(potential, 1, 2)
    curve_xx = ahead_x - 2.0 * potential + behind_x
    curve_yy = ahead_y - 2.0 * potential + behind_y
    curve_zz = ahead_z - 2.0 * potential + behind_z
    curve_xy = (jnp.roll(ahead_x, -1, 1) - jnp.roll(ahead_x, 1, 1) - jnp.roll(behind_x, -1, 1) + jnp.roll(behind_x, 1, 1)) * 0.25
    curve_xz = (jnp.roll(ahead_x, -1, 2) - jnp.roll(ahead_x, 1, 2) - jnp.roll(behind_x, -1, 2) + jnp.roll(behind_x, 1, 2)) * 0.25
    curve_yz = (jnp.roll(ahead_y, -1, 2) - jnp.roll(ahead_y, 1, 2) - jnp.roll(behind_y, -1, 2) + jnp.roll(behind_y, 1, 2)) * 0.25
    source = curve_xx * curve_yy + curve_xx * curve_zz + curve_yy * curve_zz - curve_xy * curve_xy - curve_xz * curve_xz - curve_yz * curve_yz
    modes_x, lap_x = laplace_modes(NX)
    modes_y, lap_y = laplace_modes(NY)
    modes_z, lap_z = laplace_modes(NZ)
    eigen = lap_x[:, None, None] + lap_y[None, :, None] + lap_z[None, None, :]
    anchor = (modes_x == 0)[:, None, None] & (modes_y == 0)[None, :, None] & (modes_z == 0)[None, None, :]
    inverse = jnp.where(anchor, 0.0, 1.0 / jnp.where(anchor, -1.0, eigen))
    spectrum = jnp.fft.fftn(source)
    second = jnp.real(jnp.fft.ifftn(spectrum * inverse))
    displacement = jnp.stack([-periodic_gradient(potential, component) - SECOND_ORDER * periodic_gradient(second, component) for component in range(3)])
    shift = jnp.clip(displacement, -1.0, 1.0)
    blocks = shift.reshape(3, TILES_X, BX, 8, TILES_Y, BY, 8, BZ, 8).transpose(1, 4, 2, 5, 7, 0, 3, 6, 8).reshape(TILES_X * TILES_Y, NBLK, 3, 512)
    owner_rows = owner.reshape(TILES_X * TILES_Y, NBLK)
    window_rows = window.reshape(TILES_X * TILES_Y, NBLK)
    span = jnp.arange(12).astype(jnp.int32)

    def add_tile(grid, items):
        shifts, owners, windows = items
        values = deposit_blocks(shifts).reshape(NBLK, 12, 12, 12)
        start_x = (owners // TILES_Y) * CX + 8 * (windows // (BY * BZ)) - 2
        start_y = (owners % TILES_Y) * CY + 8 * ((windows // BZ) % BY) - 2
        start_z = 8 * (windows % BZ) - 2
        index_x = (start_x[:, None] + span[None, :]) % NX
        index_y = (start_y[:, None] + span[None, :]) % NY
        index_z = (start_z[:, None] + span[None, :]) % NZ
        grid = grid.at[index_x[:, :, None, None], index_y[:, None, :, None], index_z[:, None, None, :]].add(values)
        return grid, None

    density, ignored = lax.scan(add_tile, jnp.zeros((NX, NY, NZ), jnp.float32), (blocks, owner_rows, window_rows))
    return displacement, density
```

```python
import functools
import math

import jax
import jax.numpy as jnp
import numpy as np
from jax import lax
from jax.experimental import pallas as pl
from jax.experimental.pallas import tpu as pltpu
from jax.sharding import PartitionSpec as P

SECOND_ORDER = 3.0 / 7.0
F32 = jnp.float32
BF16 = jnp.bfloat16
LANES = 128
ROWS = 896
VMEM = pl.BlockSpec(memory_space=pltpu.VMEM)
SMEM = pl.BlockSpec(memory_space=pltpu.SMEM)
NN = (((1,), (0,)), ((), ()))
NT = (((1,), (1,)), ((), ()))
TN = (((0,), (0,)), ((), ()))


def split(x, pieces):
    out = []
    for piece in range(pieces):
        part = x.astype(BF16)
        out.append(part)
        if piece < pieces - 1:
            x = x - part.astype(F32)
    return out


def dot(a, b, dims=NN):
    return lax.dot_general(a, b, dims, preferred_element_type=F32)


def dot3(a, b, dims=NN):
    return dot(a[0], b[0], dims) + (dot(a[0], b[1], dims) + dot(a[1], b[0], dims))


def swap_groups(rows, group):
    rows = list(rows)
    count = len(rows)
    axis = rows[0].ndim - 1
    lane = lax.broadcasted_iota(jnp.int32, rows[0].shape, axis) // group
    step = 1
    while step < count:
        low = (lane & step) == 0
        for k in range(count):
            if k & step:
                continue
            a, b = rows[k], rows[k + step]
            rows[k] = jnp.where(low, a, pltpu.roll(b, step * group, axis))
            rows[k + step] = jnp.where(low, pltpu.roll(a, LANES - step * group, axis), b)
        step *= 2
    return rows


def table_of(length):
    modes = np.arange(length)
    angle = (modes[:, None] * modes[None, :] % length) * (2.0 * math.pi / length)
    return (np.cos(angle) + np.sin(angle)).astype(np.float32)


def pieces_of(table):
    high = table.astype(jnp.bfloat16)
    low = (table - high.astype(np.float32)).astype(jnp.bfloat16)
    return np.asarray(high), np.asarray(low)


def laplace_of(length):
    return (2.0 * np.cos(np.arange(length) * (2.0 * math.pi / length)) - 2.0).astype(np.float32)


def call(body, outs, scratch, vmem, flops, moved):
    return pl.pallas_call(
        body,
        out_shape=outs,
        scratch_shapes=scratch,
        compiler_params=pltpu.CompilerParams(vmem_limit_bytes=vmem << 20),
        cost_estimate=pl.CostEstimate(flops=flops, bytes_accessed=moved, transcendentals=0),
    )


def shape(*dims, dtype=F32):
    return jax.ShapeDtypeStruct(dims, dtype)


def send(x, dx, dy):
    size_x, size_y = lax.axis_size("px"), lax.axis_size("py")
    pairs = []
    for i in range(size_x):
        for j in range(size_y):
            pairs.append((i * size_y + j, ((i + dx) % size_x) * size_y + (j + dy) % size_y))
    return lax.ppermute(x, ("px", "py"), pairs)


def slot_kernel(half, owner_col, owner_row, window_row, slot_out, label_out):
    count = owner_row.shape[1]
    later = lax.broadcasted_iota(jnp.int32, (count, count), 0) < lax.broadcasted_iota(
        jnp.int32, (count, count), 1
    )
    same = (owner_col[...] == owner_row[...]) & later
    rank = jnp.sum(same.astype(F32), axis=0, keepdims=True).astype(jnp.int32)
    second = rank >= half
    place = owner_row[...] * half + jnp.where(second, rank - half, rank)
    slot_out[...] = jnp.where(second, place + count, place)
    named = jnp.broadcast_to((window_row[...] + 1).astype(BF16), (8, count))
    where_row = slot_out[...]
    for part in range(2):
        rows = lax.broadcasted_iota(jnp.int32, (count, count), 0) + part * count
        chosen = (where_row == rows).astype(BF16)
        label_out[part : part + 1, :] = dot(named, chosen, NT)[0:1, :].astype(jnp.int32) - 1


def pad_tile(pad, core, x_faces, y_faces):
    rows_x, rows_y, _ = core.shape
    pad[1 : rows_x + 1, 8 : rows_y + 8, :] = core[...]
    pad[0, 8 : rows_y + 8, :] = x_faces[0]
    pad[rows_x + 1, 8 : rows_y + 8, :] = x_faces[1]
    for x in range(rows_x):
        pad[x + 1, 7:8, :] = y_faces[0, x : x + 1, :]
        pad[x + 1, rows_y + 8 : rows_y + 9, :] = y_faces[1, x : x + 1, :]


def source_kernel(core, x_faces, y_faces, corners, high, low, spectrum, pad, source):
    rows_x, rows_y, cells_z = core.shape
    pad_tile(pad, core, x_faces, y_faces)
    for side in range(2):
        edge = side * (rows_x + 1)
        pad[edge, 7:8, :] = corners[2 * side : 2 * side + 1, :]
        pad[edge, rows_y + 8 : rows_y + 9, :] = corners[2 * side + 1 : 2 * side + 2, :]

    def ahead(value):
        return pltpu.roll(value, cells_z - 1, 1)

    def behind(value):
        return pltpu.roll(value, 1, 1)

    @pl.loop(0, rows_x)
    def _(x):
        def at(dx, dy):
            return pad[x + 1 + dx, 8 + dy : 8 + dy + rows_y, :]

        here = at(0, 0)
        ahead_x, behind_x, ahead_y, behind_y = at(1, 0), at(-1, 0), at(0, 1), at(0, -1)
        xx = ahead_x - 2.0 * here + behind_x
        yy = ahead_y - 2.0 * here + behind_y
        zz = ahead(here) - 2.0 * here + behind(here)
        xy = (at(1, 1) - at(1, -1) - at(-1, 1) + at(-1, -1)) * 0.25
        across_x, across_y = ahead_x - behind_x, ahead_y - behind_y
        xz = (ahead(across_x) - behind(across_x)) * 0.25
        yz = (ahead(across_y) - behind(across_y)) * 0.25
        value = xx * yy + xx * zz + yy * zz - xy * xy - xz * xz - yz * yz
        source[pl.ds(pl.multiple_of(x * rows_y, rows_y), rows_y), :] = value

    spectrum[...] = dot3((high[...], low[...]), split(source[...], 2), NT)


def solve_kernel(
    tiles_x, tiles_y, rows_x, rows_y, scale,
    first, lap_z, slab, lap_xy, hx_high, hx_low, hy_high, hy_low, hf_high, hf_low,
    out, planes, faces,
):
    grid_x, grid_y = tiles_x * rows_x, tiles_y * rows_y
    count = slab.shape[1]
    per = LANES // rows_y
    for i in range(tiles_x):
        for part in range(rows_x // per):
            lanes = slice(part * LANES, (part + 1) * LANES)
            for wide in range(tiles_y // per):
                rows = [slab[i * tiles_y + wide * per + j, :, lanes] for j in range(per)]
                for t, row in enumerate(swap_groups(rows, rows_y)):
                    x = i * rows_x + part * per + t
                    planes[x * count : (x + 1) * count, wide * LANES : (wide + 1) * LANES] = row
    hx = (hx_high[...], hx_low[...])
    hy = (hy_high[...], hy_low[...])
    hf = (hf_high[...], hf_low[...])
    planes[...] = dot3(split(planes[...], 2), hy)
    for q in range(count):
        rows = pl.ds(q, grid_x, stride=count)
        modes = dot3(hx, split(planes[rows, :], 2))
        eigen = lap_xy[...] + lap_z[first[0] + q]
        anchor = eigen == 0.0
        solved = jnp.where(anchor, 0.0, scale / jnp.where(anchor, -1.0, eigen)) * modes
        back = dot3(hx, split(solved, 2))
        planes[rows, :] = back
        faces[pl.ds(q, 2 * tiles_y, stride=count), :] = dot3(hf, split(back, 2), NT)
    planes[...] = dot3(split(planes[...], 2), hy)

    lane = lax.broadcasted_iota(jnp.int32, (count, LANES), 1)
    for i in range(tiles_x):
        for wide in range(tiles_y // per):
            cols = slice(wide * LANES, (wide + 1) * LANES)

            def row_of(x):
                x = x % grid_x
                return planes[x * count : (x + 1) * count, cols]

            for part in range(rows_x // per):
                lanes = slice(part * LANES, (part + 1) * LANES)
                rows = [row_of(i * rows_x + part * per + t) for t in range(per)]
                for j, row in enumerate(swap_groups(rows, rows_y)):
                    out[i * tiles_y + wide * per + j, :, lanes] = row
            before, after = row_of(i * rows_x - 1), row_of((i + 1) * rows_x)
            for k in range(per):
                j = wide * per + k
                shift = (LANES - k * rows_y) % LANES
                line = pltpu.roll(before, shift, 1) if shift else before
                moved = pltpu.roll(after, (shift + rows_y) % LANES, 1)
                line = jnp.where(lane < rows_y, line, moved)
                for side in range(2):
                    at = (side * tiles_y + j) * count
                    face = faces[at : at + count, :]
                    start = 2 * rows_y + side * rows_x
                    move = (start - i * rows_x) % LANES
                    face = pltpu.roll(face, move, 1) if move else face
                    line = jnp.where(lane < start, line, face)
                out[i * tiles_y + j, :, rows_x * rows_y : rows_x * rows_y + LANES] = line


def solve_plain(slab, rows_x, rows_y, cells_z, tiles_x, tiles_y, scale):
    high = lax.Precision.HIGHEST
    grid_x, grid_y = tiles_x * rows_x, tiles_y * rows_y
    count = slab.shape[1]
    hx, hy = jnp.asarray(table_of(grid_x)), jnp.asarray(table_of(grid_y))
    planes = slab.reshape(tiles_x, tiles_y, count, rows_x, rows_y).transpose(2, 0, 3, 1, 4)
    planes = planes.reshape(count, grid_x, grid_y)
    modes = jnp.einsum("qxy,xk,yl->qkl", planes, hx, hy, precision=high)
    first = lax.axis_index(("px", "py")) * count
    lap_z = lax.dynamic_slice_in_dim(jnp.asarray(laplace_of(cells_z)), first, count)
    eigen = (
        jnp.asarray(laplace_of(grid_x))[None, :, None]
        + jnp.asarray(laplace_of(grid_y))[None, None, :]
        + lap_z[:, None, None]
    )
    anchor = eigen == 0.0
    solved = jnp.where(anchor, 0.0, scale / jnp.where(anchor, -1.0, eigen)) * modes
    back = jnp.einsum("qkl,xk,yl->qxy", solved, hx, hy, precision=high)
    tiles = back.reshape(count, tiles_x, rows_x, tiles_y, rows_y).transpose(1, 3, 0, 2, 4)
    starts_x, starts_y = np.arange(tiles_x) * rows_x, np.arange(tiles_y) * rows_y
    faces = []
    for edge in (-1, rows_x):
        line = back[:, (starts_x + edge) % grid_x].reshape(count, tiles_x, tiles_y, rows_y)
        faces.append(line.transpose(1, 2, 0, 3))
    for edge in (-1, rows_y):
        line = back[:, :, (starts_y + edge) % grid_y].reshape(count, tiles_x, rows_x, tiles_y)
        faces.append(line.transpose(1, 3, 0, 2))
    used = rows_x * rows_y + 2 * (rows_x + rows_y)
    faces.append(jnp.zeros((tiles_x, tiles_y, count, -used % LANES), F32))
    parts = [tiles.reshape(tiles_x, tiles_y, count, rows_x * rows_y)] + faces
    return jnp.concatenate(parts, -1).reshape(tiles_x * tiles_y, count, -1)


def block_kernel(
    core, x_faces, y_faces, spectrum, high, low, slots,
    displacement, first_half, second_half,
    pad, cells, spread, values,
):
    rows_x, rows_y, cells_z = core.shape
    inner = rows_x * rows_y
    blocks_x, blocks_y, blocks_z = rows_x // 8, rows_y // 8, cells_z // 8
    per = LANES // blocks_z
    cells[...] = dot3(split(spectrum[...], 2), (high[...], low[...]), TN)
    cells[0:inner, :] = cells[0:inner, :] + core[...].reshape(inner, cells_z)
    start = inner
    for faces in (x_faces, y_faces):
        for side in range(2):
            rows = slice(start, start + faces.shape[1])
            cells[rows, :] = cells[rows, :] + faces[side]
            start += faces.shape[1]
    x_edge = [inner, inner + rows_y]
    y_edge = [inner + 2 * rows_y, inner + 2 * rows_y + rows_x]

    for x in range(rows_x):
        pad[x, 8 : rows_y + 8, :] = cells[x * rows_y : (x + 1) * rows_y, :]
        pad[x, 7:8, :] = cells[y_edge[0] + x : y_edge[0] + x + 1, :]
        pad[x, rows_y + 8 : rows_y + 9, :] = cells[y_edge[1] + x : y_edge[1] + x + 1, :]

    def line(x):
        if x < 0:
            return cells[x_edge[0] : x_edge[0] + rows_y, :]
        if x >= rows_x:
            return cells[x_edge[1] : x_edge[1] + rows_y, :]
        return cells[x * rows_y : (x + 1) * rows_y, :]

    for x in range(rows_x):
        here = line(x)
        displacement[0, x] = (line(x - 1) - line(x + 1)) * 0.5
        displacement[1, x] = (pad[x, 7 : rows_y + 7, :] - pad[x, 9 : rows_y + 9, :]) * 0.5
        displacement[2, x] = (pltpu.roll(here, 1, 1) - pltpu.roll(here, cells_z - 1, 1)) * 0.5

    width = spread.shape[0] * LANES
    col = lax.broadcasted_iota(jnp.int32, (cells_z, width), 1)
    wanted = (8 * (col % blocks_z) + col // blocks_z + cells_z - 1) % cells_z
    choose = (wanted == lax.broadcasted_iota(jnp.int32, (cells_z, width), 0)).astype(BF16)
    pieces = split(cells[...], 3)
    moved = dot(pieces[0], choose) + dot(pieces[1], choose) + dot(pieces[2], choose)
    for quad in range(spread.shape[0]):
        spread[quad] = moved[:, quad * LANES : (quad + 1) * LANES]

    def put(row, tiles):
        for quad in range(width // LANES):
            every = [tiles(b // blocks_y, b % blocks_y, quad) for b in range(blocks_x * blocks_y)]
            for block in range(0, len(every), per):
                for k, item in enumerate(swap_groups(every[block : block + per], blocks_z)):
                    where = row(quad * per + k - 1)
                    if where is not None:
                        start = block * blocks_z
                        values[where : where + 8, start : start + LANES] = item

    def x_tile(a):
        def tile(bx, by, quad):
            x = 8 * bx + a
            top = x_edge[0] if x < 0 else x_edge[1] if x >= rows_x else x * rows_y
            return spread[quad, top + 8 * by : top + 8 * by + 8, :]

        return tile

    for a in range(-1, 9):
        def row(e, a=a):
            if 0 <= e < 8:
                return ((a + 1) * 8 + e) * 8
            if e in (-1, 8) and 0 <= a < 8:
                return 640 + (64 if e == 8 else 0) + a * 8
            return None

        put(row, x_tile(a))
    for side, edge in enumerate((-1, 8)):
        def tile(bx, by, quad, edge=edge):
            y = 8 * by + edge
            if y < 0 or y >= rows_y:
                top = y_edge[0 if y < 0 else 1] + 8 * bx
                return spread[quad, top : top + 8, :]
            return spread[quad, pl.ds(8 * bx * rows_y + y, 8, stride=rows_y), :]

        put(lambda e, side=side: 768 + side * 64 + e * 8 if 0 <= e < 8 else None, tile)

    count = slots.shape[1]
    pieces = split(values[...], 3)
    for part, out in enumerate((first_half, second_half)):
        rows = lax.broadcasted_iota(jnp.int32, (count, count), 0) + part * count
        chosen = (slots[...] == rows).astype(BF16)
        out[...] = dot(chosen, pieces[0], NT) + dot(chosen, pieces[1], NT) + dot(chosen, pieces[2], NT)


def spline(shift):
    g = jnp.abs(shift)
    h = 1.0 - g
    gg, hh = g * g, h * h
    near = (2.0 / 3.0) - gg + 0.5 * gg * g
    ahead = (2.0 / 3.0) - hh + 0.5 * hh * h
    back = hh * h * (1.0 / 6.0)
    far = gg * g * (1.0 / 6.0)
    up = shift >= 0.0
    zero = jnp.zeros_like(far)
    return (
        jnp.where(up, zero, far),
        jnp.where(up, back, ahead),
        near,
        jnp.where(up, ahead, back),
        jnp.where(up, far, zero),
    )


def deposit_kernel(blocks_x, blocks_y, blocks_z, last, blocks, labels, *refs):
    if last:
        before, core, x_rims, y_rims, corners, turned, weights, high, low, grouped, tile = refs
    else:
        core, turned, weights, high, low, grouped, tile = refs
    slots = blocks.shape[0]
    cells_z = 8 * blocks_z
    per = LANES // blocks_z
    windows = blocks_x * blocks_y * blocks_z
    sub = lax.broadcasted_iota(jnp.int32, (8, LANES), 0)
    for g in range(slots // LANES):
        turned[g] = jnp.transpose(blocks[g * LANES : (g + 1) * LANES, :])

    @pl.loop(0, slots // LANES)
    def _(g):
        def rows(start):
            return turned[g, pl.ds(pl.multiple_of(start, 8), 8), :]

        @pl.loop(0, 8)
        def _(a):
            for e in range(8):
                here = rows((a + 1) * 64 + e * 8)
                x_diff = rows(a * 64 + e * 8) - rows((a + 2) * 64 + e * 8)
                z_low = rows((a + 1) * 64 + e * 8 - 8) if e > 0 else rows(640 + a * 8)
                z_top = rows((a + 1) * 64 + e * 8 + 8) if e < 7 else rows(704 + a * 8)
                y_low = jnp.where(
                    sub == 0, turned[g, pl.ds(768 + e * 8 + a, 1), :], pltpu.roll(here, 1, 0)
                )
                y_top = jnp.where(
                    sub == 7, turned[g, pl.ds(832 + e * 8 + a, 1), :], pltpu.roll(here, 7, 0)
                )
                for axis, diff in enumerate((x_diff, y_low - y_top, z_low - z_top)):
                    for k, weight in enumerate(spline(jnp.clip(diff * 0.5, -1.0, 1.0))):
                        weights[axis * 5 + k, a * 8 + e] = weight

        lanes = pl.ds(pl.multiple_of(g * LANES, LANES), LANES)

        def cell_row(s, depths):
            sums = {}
            for a in range(8):
                for k in depths:
                    at = a * 8 + (s - k)
                    w_z = weights[10 + k, at]
                    w_y = [weights[5 + j, at] for j in range(5)]
                    for i in range(5):
                        plane = weights[i, at] * w_z
                        for j in range(5):
                            key = (a + i, j)
                            term = plane * w_y[j]
                            sums[key] = sums[key] + term if key in sums else term
                for u in [a] if a < 7 else range(7, 12):
                    head = sums[u, 0]
                    tail = jnp.zeros_like(head)
                    for j in range(1, 5):
                        moved = pltpu.roll(sums[u, j], j, 0)
                        head = head + jnp.where(sub >= j, moved, 0.0)
                        tail = tail + jnp.where(sub < j, moved, 0.0)
                    both = jnp.concatenate([head, tail], 0)
                    top, rest = split(both, 2)
                    out = pl.ds(pl.multiple_of((s * 12 + u) * 16, 16), 16)
                    high[out, lanes] = top
                    low[out, lanes] = rest

        for s in (0, 1, 2, 3, 8, 9, 10, 11):
            cell_row(s, [k for k in range(5) if 0 <= s - k < 8])

        @pl.loop(4, 8)
        def _(s):
            cell_row(s, range(5))

    named = (labels[...] == lax.broadcasted_iota(jnp.int32, (windows, slots), 0)).astype(BF16)
    area = 12 * 16

    @pl.loop(0, 12 // per)
    def _(quad):
        part = []
        for k in range(per):
            rows = pl.ds(pl.multiple_of((quad * per + k) * area, 16), area)
            part.append(dot(high[rows, :], named, NT) + dot(low[rows, :], named, NT))
        for wide in range(windows // LANES):
            lanes = slice(wide * LANES, (wide + 1) * LANES)
            for t, item in enumerate(swap_groups([p[:, lanes] for p in part], blocks_z)):
                grouped[wide * per + t, quad] = item

    depth = 12 * blocks_z
    row = lax.broadcasted_iota(jnp.int32, (depth, cells_z), 0)
    wanted = (8 * (row % blocks_z) + row // blocks_z + cells_z - 2) % cells_z
    place = (wanted == lax.broadcasted_iota(jnp.int32, (depth, cells_z), 1)).astype(BF16)
    tile[...] = before[...] if last else jnp.zeros_like(tile)

    @pl.loop(0, blocks_x)
    def _(bx):
        for by in range(blocks_y):
            total = None
            for quad in range(12 // per):
                piece = place[quad * LANES : (quad + 1) * LANES, :]
                for item in split(grouped[bx * blocks_y + by, quad], 2):
                    term = dot(item, piece)
                    total = term if total is None else total + term
            rows = pl.ds(bx * 8, 12)
            cols = slice(by * 8, by * 8 + 16)
            tile[rows, cols, :] = tile[rows, cols, :] + total.reshape(12, 16, cells_z)

    if not last:
        core[...] = tile[...]
        return
    rows_x, rows_y = 8 * blocks_x, 8 * blocks_y
    core[...] = tile[2 : rows_x + 2, 2 : rows_y + 2, :]
    for side in range(2):
        x = side * (rows_x + 2)
        y = side * (rows_y + 2)
        x_rims[side] = tile[x : x + 2, 2 : rows_y + 2, :]
        y_rims[side] = tile[2 : rows_x + 2, y : y + 2, :]
        for other in range(2):
            y = other * (rows_y + 2)
            corners[side * 2 + other] = tile[x : x + 2, y : y + 2, :]


def rim_kernel(core, x_low, x_top, y_low, y_top, c_low_low, c_low_top, c_top_low, c_top_top, out):
    rows_x, rows_y, _ = core.shape
    out[...] = core[...]
    xs, ys = (slice(0, 2), slice(rows_x - 2, rows_x)), (slice(0, 2), slice(rows_y - 2, rows_y))
    for part, face in zip(xs, (x_low, x_top)):
        out[part] = out[part] + face[...]
    for part, face in zip(ys, (y_low, y_top)):
        out[:, part, :] = out[:, part, :] + face[...]
    for x, y, face in (
        (0, 0, c_low_low), (0, 1, c_low_top), (1, 0, c_top_low), (1, 1, c_top_top),
    ):
        out[xs[x], ys[y], :] = out[xs[x], ys[y], :] + face[...]


def per_device(potential, owner, window):
    rows_x, rows_y, cells_z = potential.shape
    tiles_x, tiles_y = lax.axis_size("px"), lax.axis_size("py")
    tiles = tiles_x * tiles_y
    grid_x, grid_y = rows_x * tiles_x, rows_y * tiles_y
    planes = cells_z // tiles
    inner = rows_x * rows_y
    used = inner + -(-2 * (rows_x + rows_y) // LANES) * LANES
    blocks_x, blocks_y, blocks_z = rows_x // 8, rows_y // 8, cells_z // 8
    blocks = blocks_x * blocks_y * blocks_z
    half = max(2, 2 * blocks // tiles) // 2
    both = ("px", "py")

    def exchange(x):
        return lax.all_to_all(x, both, split_axis=0, concat_axis=0, tiled=True)

    slots, labels = call(
        functools.partial(slot_kernel, half),
        (shape(1, blocks, dtype=jnp.int32), shape(2, blocks, dtype=jnp.int32)),
        [], 16, 4 * blocks**3, 8 * blocks,
    )(owner.reshape(blocks, 1), owner.reshape(1, blocks), window.reshape(1, blocks))
    arrived_labels = exchange(labels.reshape(2, tiles, half).transpose(1, 0, 2).reshape(tiles, 2 * half))
    arrived_labels = arrived_labels.reshape(tiles, 2, half).transpose(1, 0, 2).reshape(2, 1, blocks)

    last_x, last_y = rows_x - 1, rows_y - 1
    x_faces = jnp.stack([send(potential[last_x], 1, 0), send(potential[0], -1, 0)])
    y_faces = jnp.stack([send(potential[:, last_y], 0, 1), send(potential[:, 0], 0, -1)])
    corners = jnp.stack(
        [
            send(potential[last_x, last_y], 1, 1), send(potential[last_x, 0], 1, -1),
            send(potential[0, last_y], -1, 1), send(potential[0, 0], -1, -1),
        ]
    )

    z_high, z_low = pieces_of(table_of(cells_z))
    spectrum = call(
        source_kernel, shape(cells_z, inner),
        [pltpu.VMEM((rows_x + 2, rows_y + 16, cells_z), F32), pltpu.VMEM((inner, cells_z), F32)],
        24, 6 * inner * cells_z**2, 2 << 20,
    )(potential, x_faces, y_faces, corners, z_high, z_low)
    slab = exchange(spectrum).reshape(tiles, planes, inner)

    scale = SECOND_ORDER / (grid_x * grid_y * cells_z)
    if planes % 8 == 0 and tiles_y % (LANES // rows_y) == 0 and grid_x == LANES:
        first = (lax.axis_index(both) * planes).astype(jnp.int32).reshape(1)
        x_table, y_table = table_of(grid_x), table_of(grid_y)
        starts = np.arange(tiles_y) * rows_y
        edge = np.concatenate([(starts - 1) % grid_y, (starts + rows_y) % grid_y])
        lap_xy = laplace_of(grid_x)[:, None] + laplace_of(grid_y)[None, :]
        tables = pieces_of(x_table) + pieces_of(y_table) + pieces_of(y_table[edge])
        body = functools.partial(solve_kernel, tiles_x, tiles_y, rows_x, rows_y, scale)
        specs = [SMEM, SMEM] + [VMEM] * 8
        returned = pl.pallas_call(
            body,
            out_shape=shape(tiles, planes, used),
            in_specs=specs,
            out_specs=VMEM,
            scratch_shapes=[
                pltpu.VMEM((grid_x * planes, grid_y), F32),
                pltpu.VMEM((2 * tiles_y * planes, grid_x), F32),
            ],
            compiler_params=pltpu.CompilerParams(vmem_limit_bytes=24 << 20),
            cost_estimate=pl.CostEstimate(
                flops=24 * planes * grid_x**2 * grid_y, bytes_accessed=2 << 20, transcendentals=0
            ),
        )(first, laplace_of(cells_z), slab, lap_xy, *tables)
    else:
        returned = solve_plain(slab, rows_x, rows_y, cells_z, tiles_x, tiles_y, scale)
    modes = exchange(returned.reshape(cells_z, used))

    pad = pltpu.VMEM((rows_x, rows_y + 16, cells_z), F32)
    width = -(-10 * blocks_z // LANES) * LANES
    displacement, *sent = call(
        block_kernel,
        (shape(3, rows_x, rows_y, cells_z), shape(blocks, ROWS), shape(blocks, ROWS)),
        [pad, pltpu.VMEM((used, cells_z), F32), pltpu.VMEM((width // LANES, used, LANES), F32), pltpu.VMEM((ROWS, blocks), F32)],
        40, 20 * used * cells_z**2, 6 << 20,
    )(potential, x_faces, y_faces, modes, z_high, z_low, slots)

    arrived = [exchange(part) for part in sent]
    tile_shape = (rows_x + 4, rows_y + 8, cells_z)
    scratch = [
        pltpu.VMEM((blocks // LANES, ROWS, LANES), F32),
        pltpu.VMEM((15, 64, 8, LANES), F32),
        pltpu.VMEM((12 * 12 * 16, blocks), BF16),
        pltpu.VMEM((12 * 12 * 16, blocks), BF16),
        pltpu.VMEM((blocks_x * blocks_y, 12 * blocks_z // LANES, 12 * 16, LANES), F32),
        pltpu.VMEM(tile_shape, F32),
    ]
    sizes = (blocks_x, blocks_y, blocks_z)
    cost = (300 * blocks * 512, 4 << 20)
    tile = call(
        functools.partial(deposit_kernel, *sizes, False), shape(*tile_shape), scratch, 40, *cost
    )(arrived[0], arrived_labels[0])
    core, x_rims, y_rims, edges = call(
        functools.partial(deposit_kernel, *sizes, True),
        (
            shape(rows_x, rows_y, cells_z), shape(2, 2, rows_y, cells_z),
            shape(2, rows_x, 2, cells_z), shape(4, 2, 2, cells_z),
        ),
        scratch, 40, *cost,
    )(arrived[1], arrived_labels[1], tile)

    density = call(rim_kernel, shape(rows_x, rows_y, cells_z), [], 16, inner * cells_z, 2 << 20)(
        core,
        send(x_rims[1], 1, 0), send(x_rims[0], -1, 0),
        send(y_rims[1], 0, 1), send(y_rims[0], 0, -1),
        send(edges[3], 1, 1), send(edges[2], 1, -1), send(edges[1], -1, 1), send(edges[0], -1, -1),
    )
    return (displacement, density)


def solution(mesh):
    return jax.shard_map(
        per_device,
        mesh=mesh,
        in_specs=(P("px", "py", None), P("px", "py", None, None), P("px", "py", None)),
        out_specs=(P(None, "px", "py", None), P("px", "py", None)),
        check_vma=False,
    )
```

```python
import functools
import math

import jax
import jax.numpy as jnp
import numpy as np
from jax import lax
from jax.experimental import pallas as pl
from jax.experimental.pallas import tpu as pltpu
from jax.sharding import PartitionSpec as P

SECOND_ORDER = 3.0 / 7.0
F32 = jnp.float32
BF16 = jnp.bfloat16
LANES = 128
ROWS = 896
VMEM = pl.BlockSpec(memory_space=pltpu.VMEM)
SMEM = pl.BlockSpec(memory_space=pltpu.SMEM)
NN = (((1,), (0,)), ((), ()))
NT = (((1,), (1,)), ((), ()))
TN = (((0,), (0,)), ((), ()))


def split(x, pieces):
    out = []
    for piece in range(pieces):
        part = x.astype(BF16)
        out.append(part)
        if piece < pieces - 1:
            x = x - part.astype(F32)
    return out


def dot(a, b, dims=NN):
    return lax.dot_general(a, b, dims, preferred_element_type=F32)


def dot3(a, b, dims=NN):
    return dot(a[0], b[0], dims) + (dot(a[0], b[1], dims) + dot(a[1], b[0], dims))


def swap_groups(rows, group):
    rows = list(rows)
    count = len(rows)
    axis = rows[0].ndim - 1
    lane = lax.broadcasted_iota(jnp.int32, rows[0].shape, axis) // group
    step = 1
    while step < count:
        low = (lane & step) == 0
        for k in range(count):
            if k & step:
                continue
            a, b = rows[k], rows[k + step]
            rows[k] = jnp.where(low, a, pltpu.roll(b, step * group, axis))
            rows[k + step] = jnp.where(low, pltpu.roll(a, LANES - step * group, axis), b)
        step *= 2
    return rows


def table_of(length):
    modes = np.arange(length)
    angle = (modes[:, None] * modes[None, :] % length) * (2.0 * math.pi / length)
    return (np.cos(angle) + np.sin(angle)).astype(np.float32)


def pieces_of(table):
    high = table.astype(jnp.bfloat16)
    low = (table - high.astype(np.float32)).astype(jnp.bfloat16)
    return np.asarray(high), np.asarray(low)


def laplace_of(length):
    return (2.0 * np.cos(np.arange(length) * (2.0 * math.pi / length)) - 2.0).astype(np.float32)


def call(body, outs, scratch, vmem, flops, moved):
    return pl.pallas_call(
        body,
        out_shape=outs,
        scratch_shapes=scratch,
        compiler_params=pltpu.CompilerParams(vmem_limit_bytes=vmem << 20),
        cost_estimate=pl.CostEstimate(flops=flops, bytes_accessed=moved, transcendentals=0),
    )


def shape(*dims, dtype=F32):
    return jax.ShapeDtypeStruct(dims, dtype)


def send(x, axis, step):
    size = lax.axis_size(axis)
    return lax.ppermute(x, axis, [(i, (i + step) % size) for i in range(size)])


def slot_kernel(half, start, owner_col, owner_row, window_row, slot_out, label_out):
    count = owner_row.shape[1]
    tiles = label_out.shape[0]
    later = lax.broadcasted_iota(jnp.int32, (count, count), 0) < lax.broadcasted_iota(
        jnp.int32, (count, count), 1
    )
    owners = owner_row[...]
    same = (owner_col[...] == owners) & later
    rank = jnp.sum(same.astype(F32), axis=0, keepdims=True).astype(jnp.int32)
    second = rank >= half
    place = owners * half + jnp.where(second, rank - half, rank)
    slot_out[...] = jnp.where(second, place + count, place)
    tile = lax.broadcasted_iota(jnp.int32, (tiles, count), 0)
    named = jnp.where(tile == owners, window_row[...] + 1, 0).astype(F32).astype(BF16)
    lane = lax.broadcasted_iota(jnp.int32, (LANES, count), 0)
    label_out[...] = dot(named, (lane == rank + start).astype(BF16), NT) - 1.0


def pad_tile(pad, core, x_faces, y_faces):
    rows_x, rows_y, _ = core.shape
    pad[1 : rows_x + 1, 8 : rows_y + 8, :] = core[...]
    pad[0, 8 : rows_y + 8, :] = x_faces[0]
    pad[rows_x + 1, 8 : rows_y + 8, :] = x_faces[1]
    for x in range(rows_x):
        pad[x + 1, 7:8, :] = y_faces[0, x + 1 : x + 2, :]
        pad[x + 1, rows_y + 8 : rows_y + 9, :] = y_faces[1, x + 1 : x + 2, :]


def source_kernel(core, x_faces, y_faces, high, low, spectrum, pad, source):
    rows_x, rows_y, cells_z = core.shape
    pad_tile(pad, core, x_faces, y_faces)
    for side in range(2):
        edge = side * (rows_x + 1)
        pad[edge, 7:8, :] = y_faces[0, edge : edge + 1, :]
        pad[edge, rows_y + 8 : rows_y + 9, :] = y_faces[1, edge : edge + 1, :]

    def ahead(value):
        return pltpu.roll(value, cells_z - 1, 1)

    def behind(value):
        return pltpu.roll(value, 1, 1)

    @pl.loop(0, rows_x)
    def _(x):
        def at(dx, dy):
            return pad[x + 1 + dx, 8 + dy : 8 + dy + rows_y, :]

        here = at(0, 0)
        ahead_x, behind_x, ahead_y, behind_y = at(1, 0), at(-1, 0), at(0, 1), at(0, -1)
        xx = ahead_x - 2.0 * here + behind_x
        yy = ahead_y - 2.0 * here + behind_y
        zz = ahead(here) - 2.0 * here + behind(here)
        xy = (at(1, 1) - at(1, -1) - at(-1, 1) + at(-1, -1)) * 0.25
        across_x, across_y = ahead_x - behind_x, ahead_y - behind_y
        xz = (ahead(across_x) - behind(across_x)) * 0.25
        yz = (ahead(across_y) - behind(across_y)) * 0.25
        value = xx * yy + xx * zz + yy * zz - xy * xy - xz * xz - yz * yz
        source[pl.ds(pl.multiple_of(x * rows_y, rows_y), rows_y), :] = value

    spectrum[...] = dot3((high[...], low[...]), split(source[...], 2), NT)


def solve_kernel(
    tiles_x, tiles_y, rows_x, rows_y, scale,
    first, lap_z, slab, labels, lap_xy, hx_high, hx_low, hy_high, hy_low, hf_high, hf_low,
    out, planes, faces,
):
    grid_x, grid_y = tiles_x * rows_x, tiles_y * rows_y
    count = slab.shape[1]
    per = LANES // rows_y
    for i in range(tiles_x):
        for part in range(rows_x // per):
            lanes = slice(part * LANES, (part + 1) * LANES)
            for wide in range(tiles_y // per):
                rows = [slab[i * tiles_y + wide * per + j, :, lanes] for j in range(per)]
                for t, row in enumerate(swap_groups(rows, rows_y)):
                    x = i * rows_x + part * per + t
                    planes[x * count : (x + 1) * count, wide * LANES : (wide + 1) * LANES] = row
    hx = (hx_high[...], hx_low[...])
    hy = (hy_high[...], hy_low[...])
    hf = (hf_high[...], hf_low[...])
    planes[...] = dot3(split(planes[...], 2), hy)
    for q in range(count):
        rows = pl.ds(q, grid_x, stride=count)
        modes = dot3(hx, split(planes[rows, :], 2))
        eigen = lap_xy[...] + lap_z[first[0] + q]
        anchor = eigen == 0.0
        solved = jnp.where(anchor, 0.0, scale / jnp.where(anchor, -1.0, eigen)) * modes
        back = dot3(hx, split(solved, 2))
        planes[rows, :] = back
        faces[pl.ds(q, 2 * tiles_y, stride=count), :] = dot3(hf, split(back, 2), NT)
    planes[...] = dot3(split(planes[...], 2), hy)

    lane = lax.broadcasted_iota(jnp.int32, (count, LANES), 1)
    for i in range(tiles_x):
        for wide in range(tiles_y // per):
            cols = slice(wide * LANES, (wide + 1) * LANES)

            def row_of(x):
                x = x % grid_x
                return planes[x * count : (x + 1) * count, cols]

            for part in range(rows_x // per):
                lanes = slice(part * LANES, (part + 1) * LANES)
                rows = [row_of(i * rows_x + part * per + t) for t in range(per)]
                for j, row in enumerate(swap_groups(rows, rows_y)):
                    out[i * tiles_y + wide * per + j, :, lanes] = row
            before, after = row_of(i * rows_x - 1), row_of((i + 1) * rows_x)
            for k in range(per):
                j = wide * per + k
                shift = (LANES - k * rows_y) % LANES
                line = pltpu.roll(before, shift, 1) if shift else before
                moved = pltpu.roll(after, (shift + rows_y) % LANES, 1)
                line = jnp.where(lane < rows_y, line, moved)
                for side in range(2):
                    at = (side * tiles_y + j) * count
                    face = faces[at : at + count, :]
                    start = 2 * rows_y + side * rows_x
                    move = (start - i * rows_x) % LANES
                    face = pltpu.roll(face, move, 1) if move else face
                    line = jnp.where(lane < start, line, face)
                at = i * tiles_y + j
                line = jnp.where(lane < 2 * (rows_x + rows_y), line, labels[at : at + 1, :])
                out[i * tiles_y + j, :, rows_x * rows_y : rows_x * rows_y + LANES] = line


def solve_plain(slab, labels, rows_x, rows_y, cells_z, tiles_x, tiles_y, scale):
    high = lax.Precision.HIGHEST
    grid_x, grid_y = tiles_x * rows_x, tiles_y * rows_y
    count = slab.shape[1]
    hx, hy = jnp.asarray(table_of(grid_x)), jnp.asarray(table_of(grid_y))
    planes = slab.reshape(tiles_x, tiles_y, count, rows_x, rows_y).transpose(2, 0, 3, 1, 4)
    planes = planes.reshape(count, grid_x, grid_y)
    modes = jnp.einsum("qxy,xk,yl->qkl", planes, hx, hy, precision=high)
    first = lax.axis_index(("px", "py")) * count
    lap_z = lax.dynamic_slice_in_dim(jnp.asarray(laplace_of(cells_z)), first, count)
    eigen = (
        jnp.asarray(laplace_of(grid_x))[None, :, None]
        + jnp.asarray(laplace_of(grid_y))[None, None, :]
        + lap_z[:, None, None]
    )
    anchor = eigen == 0.0
    solved = jnp.where(anchor, 0.0, scale / jnp.where(anchor, -1.0, eigen)) * modes
    back = jnp.einsum("qkl,xk,yl->qxy", solved, hx, hy, precision=high)
    tiles = back.reshape(count, tiles_x, rows_x, tiles_y, rows_y).transpose(1, 3, 0, 2, 4)
    starts_x, starts_y = np.arange(tiles_x) * rows_x, np.arange(tiles_y) * rows_y
    faces = []
    for edge in (-1, rows_x):
        line = back[:, (starts_x + edge) % grid_x].reshape(count, tiles_x, tiles_y, rows_y)
        faces.append(line.transpose(1, 2, 0, 3))
    for edge in (-1, rows_y):
        line = back[:, :, (starts_y + edge) % grid_y].reshape(count, tiles_x, rows_x, tiles_y)
        faces.append(line.transpose(1, 3, 0, 2))
    tail = labels[:, 2 * (rows_x + rows_y) :].reshape(tiles_x, tiles_y, 1, -1)
    faces.append(jnp.broadcast_to(tail, (tiles_x, tiles_y, count, tail.shape[-1])))
    parts = [tiles.reshape(tiles_x, tiles_y, count, rows_x * rows_y)] + faces
    return jnp.concatenate(parts, -1).reshape(tiles_x * tiles_y, count, -1)


def block_kernel(
    planes, half, core, x_faces, y_faces, spectrum, high, low, slots,
    displacement, first_half, second_half, labels,
    pad, cells, spread, values,
):
    rows_x, rows_y, cells_z = core.shape
    inner = rows_x * rows_y
    blocks_x, blocks_y, blocks_z = rows_x // 8, rows_y // 8, cells_z // 8
    per = LANES // blocks_z
    cells[...] = dot3(split(spectrum[...], 2), (high[...], low[...]), TN)
    cells[0:inner, :] = cells[0:inner, :] + core[...].reshape(inner, cells_z)
    start = inner
    for faces, skip in ((x_faces, 0), (y_faces, 1)):
        for side in range(2):
            length = faces.shape[1] - 2 * skip
            rows = slice(start, start + length)
            cells[rows, :] = cells[rows, :] + faces[side, skip : skip + length, :]
            start += length
    x_edge = [inner, inner + rows_y]
    y_edge = [inner + 2 * rows_y, inner + 2 * rows_y + rows_x]

    for x in range(rows_x):
        pad[x, 8 : rows_y + 8, :] = cells[x * rows_y : (x + 1) * rows_y, :]
        pad[x, 7:8, :] = cells[y_edge[0] + x : y_edge[0] + x + 1, :]
        pad[x, rows_y + 8 : rows_y + 9, :] = cells[y_edge[1] + x : y_edge[1] + x + 1, :]

    def line(x):
        if x < 0:
            return cells[x_edge[0] : x_edge[0] + rows_y, :]
        if x >= rows_x:
            return cells[x_edge[1] : x_edge[1] + rows_y, :]
        return cells[x * rows_y : (x + 1) * rows_y, :]

    for x in range(rows_x):
        here = line(x)
        displacement[0, x] = (line(x - 1) - line(x + 1)) * 0.5
        displacement[1, x] = (pad[x, 7 : rows_y + 7, :] - pad[x, 9 : rows_y + 9, :]) * 0.5
        displacement[2, x] = (pltpu.roll(here, 1, 1) - pltpu.roll(here, cells_z - 1, 1)) * 0.5

    width = spread.shape[0] * LANES
    col = lax.broadcasted_iota(jnp.int32, (cells_z, width), 1)
    wanted = (8 * (col % blocks_z) + col // blocks_z + cells_z - 1) % cells_z
    choose = (wanted == lax.broadcasted_iota(jnp.int32, (cells_z, width), 0)).astype(BF16)
    pieces = split(cells[...], 3)
    moved = dot(pieces[0], choose) + dot(pieces[1], choose) + dot(pieces[2], choose)
    for quad in range(spread.shape[0]):
        spread[quad] = moved[:, quad * LANES : (quad + 1) * LANES]

    def put(row, tiles):
        for quad in range(width // LANES):
            every = [tiles(b // blocks_y, b % blocks_y, quad) for b in range(blocks_x * blocks_y)]
            for block in range(0, len(every), per):
                for k, item in enumerate(swap_groups(every[block : block + per], blocks_z)):
                    where = row(quad * per + k - 1)
                    if where is not None:
                        start = block * blocks_z
                        values[where : where + 8, start : start + LANES] = item

    def x_tile(a):
        def tile(bx, by, quad):
            x = 8 * bx + a
            top = x_edge[0] if x < 0 else x_edge[1] if x >= rows_x else x * rows_y
            return spread[quad, top + 8 * by : top + 8 * by + 8, :]

        return tile

    for a in range(-1, 9):
        def row(e, a=a):
            if 0 <= e < 8:
                return ((a + 1) * 8 + e) * 8
            if e in (-1, 8) and 0 <= a < 8:
                return 640 + (64 if e == 8 else 0) + a * 8
            return None

        put(row, x_tile(a))
    for side, edge in enumerate((-1, 8)):
        def tile(bx, by, quad, edge=edge):
            y = 8 * by + edge
            if y < 0 or y >= rows_y:
                top = y_edge[0 if y < 0 else 1] + 8 * bx
                return spread[quad, top : top + 8, :]
            return spread[quad, pl.ds(8 * bx * rows_y + y, 8, stride=rows_y), :]

        put(lambda e, side=side: 768 + side * 64 + e * 8 if 0 <= e < 8 else None, tile)

    count = slots.shape[1]
    named = spectrum[:, inner : inner + LANES].astype(BF16)
    row = lax.broadcasted_iota(jnp.int32, (cells_z, count), 0)
    slot = lax.broadcasted_iota(jnp.int32, (cells_z, count), 1)
    source = (row % planes == 0) & (row // planes == slot // half)
    by_lane = dot(named, source.astype(BF16), TN)
    lane = lax.broadcasted_iota(jnp.int32, (LANES, count), 0) - 2 * (rows_x + rows_y)
    place = lax.broadcasted_iota(jnp.int32, (LANES, count), 1) % half
    for part in range(2):
        label = jnp.sum(jnp.where(lane == place + part * half, by_lane, 0.0), axis=0, keepdims=True)
        labels[part] = label.astype(jnp.int32)

    pieces = split(values[...], 3)
    for part, out in enumerate((first_half, second_half)):
        rows = lax.broadcasted_iota(jnp.int32, (count, count), 0) + part * count
        chosen = (slots[...] == rows).astype(BF16)
        out[...] = dot(chosen, pieces[0], NT) + dot(chosen, pieces[1], NT) + dot(chosen, pieces[2], NT)


def spline(shift):
    g = jnp.abs(shift)
    h = 1.0 - g
    gg, hh = g * g, h * h
    near = (2.0 / 3.0) - gg + 0.5 * gg * g
    ahead = (2.0 / 3.0) - hh + 0.5 * hh * h
    back = hh * h * (1.0 / 6.0)
    far = gg * g * (1.0 / 6.0)
    up = shift >= 0.0
    zero = jnp.zeros_like(far)
    return (
        jnp.where(up, zero, far),
        jnp.where(up, back, ahead),
        near,
        jnp.where(up, ahead, back),
        jnp.where(up, far, zero),
    )


def deposit_kernel(blocks_x, blocks_y, blocks_z, last, blocks, labels, *refs):
    if last:
        before, core, x_rims, y_rims, turned, weights, high, low, grouped, tile = refs
    else:
        core, turned, weights, high, low, grouped, tile = refs
    slots = blocks.shape[0]
    cells_z = 8 * blocks_z
    per = LANES // blocks_z
    windows = blocks_x * blocks_y * blocks_z
    sub = lax.broadcasted_iota(jnp.int32, (8, LANES), 0)
    for g in range(slots // LANES):
        turned[g] = jnp.transpose(blocks[g * LANES : (g + 1) * LANES, :])

    @pl.loop(0, slots // LANES)
    def _(g):
        def rows(start):
            return turned[g, pl.ds(pl.multiple_of(start, 8), 8), :]

        @pl.loop(0, 8)
        def _(a):
            for e in range(8):
                here = rows((a + 1) * 64 + e * 8)
                x_diff = rows(a * 64 + e * 8) - rows((a + 2) * 64 + e * 8)
                z_low = rows((a + 1) * 64 + e * 8 - 8) if e > 0 else rows(640 + a * 8)
                z_top = rows((a + 1) * 64 + e * 8 + 8) if e < 7 else rows(704 + a * 8)
                y_low = jnp.where(
                    sub == 0, turned[g, pl.ds(768 + e * 8 + a, 1), :], pltpu.roll(here, 1, 0)
                )
                y_top = jnp.where(
                    sub == 7, turned[g, pl.ds(832 + e * 8 + a, 1), :], pltpu.roll(here, 7, 0)
                )
                for axis, diff in enumerate((x_diff, y_low - y_top, z_low - z_top)):
                    for k, weight in enumerate(spline(jnp.clip(diff * 0.5, -1.0, 1.0))):
                        weights[axis * 5 + k, a * 8 + e] = weight

        lanes = pl.ds(pl.multiple_of(g * LANES, LANES), LANES)

        def cell_row(s, depths):
            sums = {}
            for a in range(8):
                for k in depths:
                    at = a * 8 + (s - k)
                    w_z = weights[10 + k, at]
                    w_y = [weights[5 + j, at] for j in range(5)]
                    for i in range(5):
                        plane = weights[i, at] * w_z
                        for j in range(5):
                            key = (a + i, j)
                            term = plane * w_y[j]
                            sums[key] = sums[key] + term if key in sums else term
                for u in [a] if a < 7 else range(7, 12):
                    head = sums[u, 0]
                    tail = jnp.zeros_like(head)
                    for j in range(1, 5):
                        moved = pltpu.roll(sums[u, j], j, 0)
                        head = head + jnp.where(sub >= j, moved, 0.0)
                        tail = tail + jnp.where(sub < j, moved, 0.0)
                    both = jnp.concatenate([head, tail], 0)
                    top, rest = split(both, 2)
                    out = pl.ds(pl.multiple_of((s * 12 + u) * 16, 16), 16)
                    high[out, lanes] = top
                    low[out, lanes] = rest

        for s in (0, 1, 2, 3, 8, 9, 10, 11):
            cell_row(s, [k for k in range(5) if 0 <= s - k < 8])

        @pl.loop(4, 8)
        def _(s):
            cell_row(s, range(5))

    named = (labels[...] == lax.broadcasted_iota(jnp.int32, (windows, slots), 0)).astype(BF16)
    area = 12 * 16

    @pl.loop(0, 12 // per)
    def _(quad):
        part = []
        for k in range(per):
            rows = pl.ds(pl.multiple_of((quad * per + k) * area, 16), area)
            part.append(dot(high[rows, :], named, NT) + dot(low[rows, :], named, NT))
        for wide in range(windows // LANES):
            lanes = slice(wide * LANES, (wide + 1) * LANES)
            for t, item in enumerate(swap_groups([p[:, lanes] for p in part], blocks_z)):
                grouped[wide * per + t, quad] = item

    depth = 12 * blocks_z
    row = lax.broadcasted_iota(jnp.int32, (depth, cells_z), 0)
    wanted = (8 * (row % blocks_z) + row // blocks_z + cells_z - 2) % cells_z
    place = (wanted == lax.broadcasted_iota(jnp.int32, (depth, cells_z), 1)).astype(BF16)
    tile[...] = before[...] if last else jnp.zeros_like(tile)

    @pl.loop(0, blocks_x)
    def _(bx):
        for by in range(blocks_y):
            total = None
            for quad in range(12 // per):
                piece = place[quad * LANES : (quad + 1) * LANES, :]
                for item in split(grouped[bx * blocks_y + by, quad], 2):
                    term = dot(item, piece)
                    total = term if total is None else total + term
            rows = pl.ds(bx * 8, 12)
            cols = slice(by * 8, by * 8 + 16)
            tile[rows, cols, :] = tile[rows, cols, :] + total.reshape(12, 16, cells_z)

    if not last:
        core[...] = tile[...]
        return
    rows_x, rows_y = 8 * blocks_x, 8 * blocks_y
    core[...] = tile[2 : rows_x + 2, 2 : rows_y + 2, :]
    for side in range(2):
        x = side * (rows_x + 2)
        y = side * (rows_y + 2)
        x_rims[side] = tile[x : x + 2, 2 : rows_y + 2, :]
        y_rims[side] = tile[:, y : y + 2, :]


def corner_kernel(x_rims, y_low, y_top, out):
    rows_x, rows_y = y_low.shape[0] - 4, x_rims.shape[2]
    for side in range(2):
        x = side * (rows_x + 2)
        out[side] = x_rims[side]
        out[side, :, 0:2, :] = out[side, :, 0:2, :] + y_low[x : x + 2]
        out[side, :, rows_y - 2 :, :] = out[side, :, rows_y - 2 :, :] + y_top[x : x + 2]


def rim_kernel(core, y_low, y_top, x_low, x_top, out):
    rows_x, rows_y, _ = core.shape
    out[...] = core[...]
    for part, face in ((slice(0, 2), y_low), (slice(rows_y - 2, rows_y), y_top)):
        out[:, part, :] = out[:, part, :] + face[2 : rows_x + 2]
    for part, face in ((slice(0, 2), x_low), (slice(rows_x - 2, rows_x), x_top)):
        out[part] = out[part] + face[...]


def per_device(potential, owner, window):
    rows_x, rows_y, cells_z = potential.shape
    tiles_x, tiles_y = lax.axis_size("px"), lax.axis_size("py")
    tiles = tiles_x * tiles_y
    grid_x, grid_y = rows_x * tiles_x, rows_y * tiles_y
    planes = cells_z // tiles
    inner = rows_x * rows_y
    used = inner + -(-2 * (rows_x + rows_y) // LANES) * LANES
    blocks_x, blocks_y, blocks_z = rows_x // 8, rows_y // 8, cells_z // 8
    blocks = blocks_x * blocks_y * blocks_z
    half = max(2, 2 * blocks // tiles) // 2
    both = ("px", "py")

    def exchange(x):
        return lax.all_to_all(x, both, split_axis=0, concat_axis=0, tiled=True)

    slots, labels = call(
        functools.partial(slot_kernel, half, 2 * (rows_x + rows_y)),
        (shape(1, blocks, dtype=jnp.int32), shape(tiles, LANES)),
        [], 16, 2 * tiles * LANES * blocks, 8 * blocks,
    )(owner.reshape(blocks, 1), owner.reshape(1, blocks), window.reshape(1, blocks))

    last_x, last_y = rows_x - 1, rows_y - 1
    x_faces = jnp.stack([send(potential[last_x], "px", 1), send(potential[0], "px", -1)])
    y_lines = [
        jnp.concatenate([x_faces[0, y : y + 1], potential[:, y], x_faces[1, y : y + 1]])
        for y in (last_y, 0)
    ]
    y_faces = jnp.stack([send(y_lines[0], "py", 1), send(y_lines[1], "py", -1)])

    z_high, z_low = pieces_of(table_of(cells_z))
    spectrum = call(
        source_kernel, shape(cells_z, inner),
        [pltpu.VMEM((rows_x + 2, rows_y + 16, cells_z), F32), pltpu.VMEM((inner, cells_z), F32)],
        24, 6 * inner * cells_z**2, 2 << 20,
    )(potential, x_faces, y_faces, z_high, z_low)
    slab = exchange(spectrum).reshape(tiles, planes, inner)

    scale = SECOND_ORDER / (grid_x * grid_y * cells_z)
    if planes % 8 == 0 and tiles_y % (LANES // rows_y) == 0 and grid_x == LANES:
        first = (lax.axis_index(both) * planes).astype(jnp.int32).reshape(1)
        x_table, y_table = table_of(grid_x), table_of(grid_y)
        starts = np.arange(tiles_y) * rows_y
        edge = np.concatenate([(starts - 1) % grid_y, (starts + rows_y) % grid_y])
        lap_xy = laplace_of(grid_x)[:, None] + laplace_of(grid_y)[None, :]
        tables = pieces_of(x_table) + pieces_of(y_table) + pieces_of(y_table[edge])
        body = functools.partial(solve_kernel, tiles_x, tiles_y, rows_x, rows_y, scale)
        specs = [SMEM, SMEM] + [VMEM] * 9
        returned = pl.pallas_call(
            body,
            out_shape=shape(tiles, planes, used),
            in_specs=specs,
            out_specs=VMEM,
            scratch_shapes=[
                pltpu.VMEM((grid_x * planes, grid_y), F32),
                pltpu.VMEM((2 * tiles_y * planes, grid_x), F32),
            ],
            compiler_params=pltpu.CompilerParams(vmem_limit_bytes=24 << 20),
            cost_estimate=pl.CostEstimate(
                flops=24 * planes * grid_x**2 * grid_y, bytes_accessed=2 << 20, transcendentals=0
            ),
        )(first, laplace_of(cells_z), slab, labels, lap_xy, *tables)
    else:
        returned = solve_plain(slab, labels, rows_x, rows_y, cells_z, tiles_x, tiles_y, scale)
    modes = exchange(returned.reshape(cells_z, used))

    pad = pltpu.VMEM((rows_x, rows_y + 16, cells_z), F32)
    width = -(-10 * blocks_z // LANES) * LANES
    displacement, *sent, arrived_labels = call(
        functools.partial(block_kernel, planes, half),
        (
            shape(3, rows_x, rows_y, cells_z), shape(blocks, ROWS), shape(blocks, ROWS),
            shape(2, 1, blocks, dtype=jnp.int32),
        ),
        [pad, pltpu.VMEM((used, cells_z), F32), pltpu.VMEM((width // LANES, used, LANES), F32), pltpu.VMEM((ROWS, blocks), F32)],
        40, 20 * used * cells_z**2, 6 << 20,
    )(potential, x_faces, y_faces, modes, z_high, z_low, slots)

    arrived = [exchange(part) for part in sent]
    tile_shape = (rows_x + 4, rows_y + 8, cells_z)
    scratch = [
        pltpu.VMEM((blocks // LANES, ROWS, LANES), F32),
        pltpu.VMEM((15, 64, 8, LANES), F32),
        pltpu.VMEM((12 * 12 * 16, blocks), BF16),
        pltpu.VMEM((12 * 12 * 16, blocks), BF16),
        pltpu.VMEM((blocks_x * blocks_y, 12 * blocks_z // LANES, 12 * 16, LANES), F32),
        pltpu.VMEM(tile_shape, F32),
    ]
    sizes = (blocks_x, blocks_y, blocks_z)
    cost = (300 * blocks * 512, 4 << 20)
    tile = call(
        functools.partial(deposit_kernel, *sizes, False), shape(*tile_shape), scratch, 40, *cost
    )(arrived[0], arrived_labels[0])
    core, x_rims, y_rims = call(
        functools.partial(deposit_kernel, *sizes, True),
        (
            shape(rows_x, rows_y, cells_z), shape(2, 2, rows_y, cells_z),
            shape(2, rows_x + 4, 2, cells_z),
        ),
        scratch, 40, *cost,
    )(arrived[1], arrived_labels[1], tile)

    y_sides = send(y_rims[1], "py", 1), send(y_rims[0], "py", -1)
    x_rims = call(corner_kernel, shape(*x_rims.shape), [], 16, 8 * rows_y * cells_z, 1 << 17)(
        x_rims, *y_sides
    )
    x_sides = send(x_rims[1], "px", 1), send(x_rims[0], "px", -1)
    density = call(rim_kernel, shape(rows_x, rows_y, cells_z), [], 16, inner * cells_z, 2 << 20)(
        core, *y_sides, *x_sides
    )
    return (displacement, density)


def solution(mesh):
    return jax.shard_map(
        per_device,
        mesh=mesh,
        in_specs=(P("px", "py", None), P("px", "py", None, None), P("px", "py", None)),
        out_specs=(P(None, "px", "py", None), P("px", "py", None)),
        check_vma=False,
    )
```

```python
import functools
import math

import jax
import jax.numpy as jnp
import numpy as np
from jax import lax
from jax.experimental import pallas as pl
from jax.experimental.pallas import tpu as pltpu
from jax.sharding import PartitionSpec as P

SECOND_ORDER = 3.0 / 7.0
F32 = jnp.float32
BF16 = jnp.bfloat16
LANES = 128
ROWS = 896
VMEM = pl.BlockSpec(memory_space=pltpu.VMEM)
SMEM = pl.BlockSpec(memory_space=pltpu.SMEM)
NN = (((1,), (0,)), ((), ()))
NT = (((1,), (1,)), ((), ()))
TN = (((0,), (0,)), ((), ()))


def split(x, pieces):
    out = []
    for piece in range(pieces):
        part = x.astype(BF16)
        out.append(part)
        if piece < pieces - 1:
            x = x - part.astype(F32)
    return out


def dot(a, b, dims=NN):
    return lax.dot_general(a, b, dims, preferred_element_type=F32)


def dot3(a, b, dims=NN):
    return dot(a[0], b[0], dims) + (dot(a[0], b[1], dims) + dot(a[1], b[0], dims))


def swap_groups(rows, group):
    rows = list(rows)
    count = len(rows)
    axis = rows[0].ndim - 1
    lane = lax.broadcasted_iota(jnp.int32, rows[0].shape, axis) // group
    step = 1
    while step < count:
        low = (lane & step) == 0
        for k in range(count):
            if k & step:
                continue
            a, b = rows[k], rows[k + step]
            rows[k] = jnp.where(low, a, pltpu.roll(b, step * group, axis))
            rows[k + step] = jnp.where(low, pltpu.roll(a, LANES - step * group, axis), b)
        step *= 2
    return rows


def table_of(length):
    modes = np.arange(length)
    angle = (modes[:, None] * modes[None, :] % length) * (2.0 * math.pi / length)
    return (np.cos(angle) + np.sin(angle)).astype(np.float32)


def pieces_of(table):
    high = table.astype(jnp.bfloat16)
    low = (table - high.astype(np.float32)).astype(jnp.bfloat16)
    return np.asarray(high), np.asarray(low)


def laplace_of(length):
    return (2.0 * np.cos(np.arange(length) * (2.0 * math.pi / length)) - 2.0).astype(np.float32)


def call(body, outs, scratch, vmem, flops, moved):
    return pl.pallas_call(
        body,
        out_shape=outs,
        scratch_shapes=scratch,
        compiler_params=pltpu.CompilerParams(vmem_limit_bytes=vmem << 20),
        cost_estimate=pl.CostEstimate(flops=flops, bytes_accessed=moved, transcendentals=0),
    )


def shape(*dims, dtype=F32):
    return jax.ShapeDtypeStruct(dims, dtype)


def send(x, axis, step):
    size = lax.axis_size(axis)
    return lax.ppermute(x, axis, [(i, (i + step) % size) for i in range(size)])


def slot_kernel(half, start, owner_col, owner_row, window_row, slot_out, label_out):
    count = owner_row.shape[1]
    tiles = label_out.shape[0]
    later = lax.broadcasted_iota(jnp.int32, (count, count), 0) < lax.broadcasted_iota(
        jnp.int32, (count, count), 1
    )
    owners = owner_row[...]
    same = (owner_col[...] == owners) & later
    rank = jnp.sum(same.astype(F32), axis=0, keepdims=True).astype(jnp.int32)
    second = rank >= half
    place = owners * half + jnp.where(second, rank - half, rank)
    slot_out[...] = jnp.where(second, place + count, place)
    tile = lax.broadcasted_iota(jnp.int32, (tiles, count), 0)
    named = jnp.where(tile == owners, window_row[...] + 1, 0).astype(F32).astype(BF16)
    lane = lax.broadcasted_iota(jnp.int32, (LANES, count), 0)
    label_out[...] = dot(named, (lane == rank + start).astype(BF16), NT) - 1.0


def source_of(at, cells_z):
    def ahead(value):
        return pltpu.roll(value, cells_z - 1, 1)

    def behind(value):
        return pltpu.roll(value, 1, 1)

    here = at(0, 0)
    ahead_x, behind_x, ahead_y, behind_y = at(1, 0), at(-1, 0), at(0, 1), at(0, -1)
    xx = ahead_x - 2.0 * here + behind_x
    yy = ahead_y - 2.0 * here + behind_y
    zz = ahead(here) - 2.0 * here + behind(here)
    xy = (at(1, 1) - at(1, -1) - at(-1, 1) + at(-1, -1)) * 0.25
    across_x, across_y = ahead_x - behind_x, ahead_y - behind_y
    xz = (ahead(across_x) - behind(across_x)) * 0.25
    yz = (ahead(across_y) - behind(across_y)) * 0.25
    return xx * yy + xx * zz + yy * zz - xy * xy - xz * xz - yz * yz


def source_kernel(core, y_faces, high, low, pad):
    rows_x, rows_y, cells_z = core.shape
    pad[:, 8 : rows_y + 8, :] = core[...]
    for x in range(rows_x):
        pad[x, 7:8, :] = y_faces[0, x : x + 1, :]
        pad[x, rows_y + 8 : rows_y + 9, :] = y_faces[1, x : x + 1, :]

    @pl.loop(1, rows_x - 1)
    def _(x):
        def at(dx, dy):
            return pad[x + dx, 8 + dy : 8 + dy + rows_y, :]

        rows = pl.ds(pl.multiple_of(x * rows_y, rows_y), rows_y)
        high[rows, :], low[rows, :] = split(source_of(at, cells_z), 2)

    for x in (0, rows_x - 1):
        rows = slice(x * rows_y, (x + 1) * rows_y)
        high[rows, :] = jnp.zeros((rows_y, cells_z), BF16)
        low[rows, :] = jnp.zeros((rows_y, cells_z), BF16)


def spectrum_kernel(core, y_faces, x_faces, inner_high, inner_low, high, low, spectrum, pad, source_high, source_low):
    rows_x, rows_y, cells_z = core.shape
    source_high[...] = inner_high[...]
    source_low[...] = inner_low[...]
    for side in range(2):
        edge = side * (rows_x - 1)
        for line in range(3):
            x = edge + line - 1
            if 0 <= x < rows_x:
                pad[line, 8 : rows_y + 8, :] = core[x]
                pad[line, 7:8, :] = y_faces[0, x : x + 1, :]
                pad[line, rows_y + 8 : rows_y + 9, :] = y_faces[1, x : x + 1, :]
            else:
                pad[line, 7 : rows_y + 9, :] = x_faces[side]

        def at(dx, dy):
            return pad[1 + dx, 8 + dy : 8 + dy + rows_y, :]

        rows = slice(edge * rows_y, (edge + 1) * rows_y)
        source_high[rows, :], source_low[rows, :] = split(source_of(at, cells_z), 2)
    spectrum[...] = dot3((high[...], low[...]), (source_high[...], source_low[...]), NT)


def solve_kernel(
    tiles_x, tiles_y, rows_x, rows_y, scale,
    first, lap_z, slab, labels, lap_xy, hx_high, hx_low, hy_high, hy_low, hf_high, hf_low,
    out, planes, solved_planes, faces,
):
    grid_x, grid_y = tiles_x * rows_x, tiles_y * rows_y
    count = slab.shape[1]
    per = LANES // rows_y
    for i in range(tiles_x):
        for part in range(rows_x // per):
            lanes = slice(part * LANES, (part + 1) * LANES)
            for wide in range(tiles_y // per):
                rows = [slab[i * tiles_y + wide * per + j, :, lanes] for j in range(per)]
                for t, row in enumerate(swap_groups(rows, rows_y)):
                    x = i * rows_x + part * per + t
                    planes[x * count : (x + 1) * count, wide * LANES : (wide + 1) * LANES] = row
    hx = (hx_high[...], hx_low[...])
    hy = (hy_high[...], hy_low[...])
    hf = (hf_high[...], hf_low[...])
    planes[...] = dot3(split(planes[...], 2), hy)
    for q in range(count):
        rows = pl.ds(q, grid_x, stride=count)
        modes = dot3(hx, split(planes[rows, :], 2))
        eigen = lap_xy[...] + lap_z[first[0] + q]
        anchor = eigen == 0.0
        solved = jnp.where(anchor, 0.0, scale / jnp.where(anchor, -1.0, eigen)) * modes
        back = dot3(hx, split(solved, 2))
        solved_planes[rows, :] = back
        faces[pl.ds(q, 2 * tiles_y, stride=count), :] = dot3(hf, split(back, 2), NT)
    planes[...] = dot3(split(solved_planes[...], 2), hy)

    lane = lax.broadcasted_iota(jnp.int32, (count, LANES), 1)
    for i in range(tiles_x):
        for wide in range(tiles_y // per):
            cols = slice(wide * LANES, (wide + 1) * LANES)

            def row_of(x):
                x = x % grid_x
                return planes[x * count : (x + 1) * count, cols]

            for part in range(rows_x // per):
                lanes = slice(part * LANES, (part + 1) * LANES)
                rows = [row_of(i * rows_x + part * per + t) for t in range(per)]
                for j, row in enumerate(swap_groups(rows, rows_y)):
                    out[i * tiles_y + wide * per + j, :, lanes] = row
            before, after = row_of(i * rows_x - 1), row_of((i + 1) * rows_x)
            for k in range(per):
                j = wide * per + k
                shift = (LANES - k * rows_y) % LANES
                line = pltpu.roll(before, shift, 1) if shift else before
                moved = pltpu.roll(after, (shift + rows_y) % LANES, 1)
                line = jnp.where(lane < rows_y, line, moved)
                for side in range(2):
                    at = (side * tiles_y + j) * count
                    face = faces[at : at + count, :]
                    start = 2 * rows_y + side * rows_x
                    move = (start - i * rows_x) % LANES
                    face = pltpu.roll(face, move, 1) if move else face
                    line = jnp.where(lane < start, line, face)
                at = i * tiles_y + j
                line = jnp.where(lane < 2 * (rows_x + rows_y), line, labels[at : at + 1, :])
                out[i * tiles_y + j, :, rows_x * rows_y : rows_x * rows_y + LANES] = line


def solve_plain(slab, labels, rows_x, rows_y, cells_z, tiles_x, tiles_y, scale):
    high = lax.Precision.HIGHEST
    grid_x, grid_y = tiles_x * rows_x, tiles_y * rows_y
    count = slab.shape[1]
    hx, hy = jnp.asarray(table_of(grid_x)), jnp.asarray(table_of(grid_y))
    planes = slab.reshape(tiles_x, tiles_y, count, rows_x, rows_y).transpose(2, 0, 3, 1, 4)
    planes = planes.reshape(count, grid_x, grid_y)
    modes = jnp.einsum("qxy,xk,yl->qkl", planes, hx, hy, precision=high)
    first = lax.axis_index(("px", "py")) * count
    lap_z = lax.dynamic_slice_in_dim(jnp.asarray(laplace_of(cells_z)), first, count)
    eigen = (
        jnp.asarray(laplace_of(grid_x))[None, :, None]
        + jnp.asarray(laplace_of(grid_y))[None, None, :]
        + lap_z[:, None, None]
    )
    anchor = eigen == 0.0
    solved = jnp.where(anchor, 0.0, scale / jnp.where(anchor, -1.0, eigen)) * modes
    back = jnp.einsum("qkl,xk,yl->qxy", solved, hx, hy, precision=high)
    tiles = back.reshape(count, tiles_x, rows_x, tiles_y, rows_y).transpose(1, 3, 0, 2, 4)
    starts_x, starts_y = np.arange(tiles_x) * rows_x, np.arange(tiles_y) * rows_y
    faces = []
    for edge in (-1, rows_x):
        line = back[:, (starts_x + edge) % grid_x].reshape(count, tiles_x, tiles_y, rows_y)
        faces.append(line.transpose(1, 2, 0, 3))
    for edge in (-1, rows_y):
        line = back[:, :, (starts_y + edge) % grid_y].reshape(count, tiles_x, rows_x, tiles_y)
        faces.append(line.transpose(1, 3, 0, 2))
    tail = labels[:, 2 * (rows_x + rows_y) :].reshape(tiles_x, tiles_y, 1, -1)
    faces.append(jnp.broadcast_to(tail, (tiles_x, tiles_y, count, tail.shape[-1])))
    parts = [tiles.reshape(tiles_x, tiles_y, count, rows_x * rows_y)] + faces
    return jnp.concatenate(parts, -1).reshape(tiles_x * tiles_y, count, -1)


def combine(core, x_faces, y_faces, spectrum, high, low, cells):
    rows_x, rows_y, cells_z = core.shape
    inner = rows_x * rows_y
    cells[...] = dot3(split(spectrum[...], 2), (high[...], low[...]), TN)
    cells[0:inner, :] = cells[0:inner, :] + core[...].reshape(inner, cells_z)
    start = inner
    for faces, skip in ((x_faces, 1), (y_faces, 0)):
        for side in range(2):
            length = faces.shape[1] - 2 * skip
            rows = slice(start, start + length)
            cells[rows, :] = cells[rows, :] + faces[side, skip : skip + length, :]
            start += length
    x_edge = [inner, inner + rows_y]
    y_edge = [inner + 2 * rows_y, inner + 2 * rows_y + rows_x]
    return x_edge, y_edge


def displacement_kernel(core, x_faces, y_faces, spectrum, high, low, displacement, pad, cells):
    rows_x, rows_y, cells_z = core.shape
    x_edge, y_edge = combine(core, x_faces, y_faces, spectrum, high, low, cells)
    for x in range(rows_x):
        pad[x, 8 : rows_y + 8, :] = cells[x * rows_y : (x + 1) * rows_y, :]
        pad[x, 7:8, :] = cells[y_edge[0] + x : y_edge[0] + x + 1, :]
        pad[x, rows_y + 8 : rows_y + 9, :] = cells[y_edge[1] + x : y_edge[1] + x + 1, :]

    def line(x):
        if x < 0:
            return cells[x_edge[0] : x_edge[0] + rows_y, :]
        if x >= rows_x:
            return cells[x_edge[1] : x_edge[1] + rows_y, :]
        return cells[x * rows_y : (x + 1) * rows_y, :]

    for x in range(rows_x):
        here = line(x)
        displacement[0, x] = (line(x - 1) - line(x + 1)) * 0.5
        displacement[1, x] = (pad[x, 7 : rows_y + 7, :] - pad[x, 9 : rows_y + 9, :]) * 0.5
        displacement[2, x] = (pltpu.roll(here, 1, 1) - pltpu.roll(here, cells_z - 1, 1)) * 0.5


def block_kernel(
    planes, half, core, x_faces, y_faces, spectrum, high, low, slots,
    first_half, second_half, labels,
    cells, spread, values,
):
    rows_x, rows_y, cells_z = core.shape
    inner = rows_x * rows_y
    blocks_x, blocks_y, blocks_z = rows_x // 8, rows_y // 8, cells_z // 8
    per = LANES // blocks_z
    x_edge, y_edge = combine(core, x_faces, y_faces, spectrum, high, low, cells)

    width = spread.shape[0] * LANES
    col = lax.broadcasted_iota(jnp.int32, (cells_z, width), 1)
    wanted = (8 * (col % blocks_z) + col // blocks_z + cells_z - 1) % cells_z
    choose = (wanted == lax.broadcasted_iota(jnp.int32, (cells_z, width), 0)).astype(BF16)
    pieces = split(cells[...], 3)
    moved = dot(pieces[0], choose) + dot(pieces[1], choose) + dot(pieces[2], choose)
    for quad in range(spread.shape[0]):
        spread[quad] = moved[:, quad * LANES : (quad + 1) * LANES]

    def put(row, tiles):
        for quad in range(width // LANES):
            every = [tiles(b // blocks_y, b % blocks_y, quad) for b in range(blocks_x * blocks_y)]
            for block in range(0, len(every), per):
                for k, item in enumerate(swap_groups(every[block : block + per], blocks_z)):
                    where = row(quad * per + k - 1)
                    if where is not None:
                        start = block * blocks_z
                        values[where : where + 8, start : start + LANES] = item

    def x_tile(a):
        def tile(bx, by, quad):
            x = 8 * bx + a
            top = x_edge[0] if x < 0 else x_edge[1] if x >= rows_x else x * rows_y
            return spread[quad, top + 8 * by : top + 8 * by + 8, :]

        return tile

    for a in range(-1, 9):
        def row(e, a=a):
            if 0 <= e < 8:
                return ((a + 1) * 8 + e) * 8
            if e in (-1, 8) and 0 <= a < 8:
                return 640 + (64 if e == 8 else 0) + a * 8
            return None

        put(row, x_tile(a))
    for side, edge in enumerate((-1, 8)):
        def tile(bx, by, quad, edge=edge):
            y = 8 * by + edge
            if y < 0 or y >= rows_y:
                top = y_edge[0 if y < 0 else 1] + 8 * bx
                return spread[quad, top : top + 8, :]
            return spread[quad, pl.ds(8 * bx * rows_y + y, 8, stride=rows_y), :]

        put(lambda e, side=side: 768 + side * 64 + e * 8 if 0 <= e < 8 else None, tile)

    count = slots.shape[1]
    named = spectrum[:, inner : inner + LANES].astype(BF16)
    row = lax.broadcasted_iota(jnp.int32, (cells_z, count), 0)
    slot = lax.broadcasted_iota(jnp.int32, (cells_z, count), 1)
    source = (row % planes == 0) & (row // planes == slot // half)
    by_lane = dot(named, source.astype(BF16), TN)
    lane = lax.broadcasted_iota(jnp.int32, (LANES, count), 0) - 2 * (rows_x + rows_y)
    place = lax.broadcasted_iota(jnp.int32, (LANES, count), 1) % half
    for part in range(2):
        label = jnp.sum(jnp.where(lane == place + part * half, by_lane, 0.0), axis=0, keepdims=True)
        labels[part] = label.astype(jnp.int32)

    pieces = split(values[...], 3)
    for part, out in enumerate((first_half, second_half)):
        rows = lax.broadcasted_iota(jnp.int32, (count, count), 0) + part * count
        chosen = (slots[...] == rows).astype(BF16)
        out[...] = dot(chosen, pieces[0], NT) + dot(chosen, pieces[1], NT) + dot(chosen, pieces[2], NT)


def spline(shift):
    g = jnp.abs(shift)
    h = 1.0 - g
    gg, hh = g * g, h * h
    near = (2.0 / 3.0) - gg + 0.5 * gg * g
    ahead = (2.0 / 3.0) - hh + 0.5 * hh * h
    back = hh * h * (1.0 / 6.0)
    far = gg * g * (1.0 / 6.0)
    up = shift >= 0.0
    zero = jnp.zeros_like(far)
    return (
        jnp.where(up, zero, far),
        jnp.where(up, back, ahead),
        near,
        jnp.where(up, ahead, back),
        jnp.where(up, far, zero),
    )


def deposit_kernel(blocks_x, blocks_y, blocks_z, last, blocks, labels, *refs):
    if last:
        before, core, x_rims, y_rims, turned, weights, pieces, grouped, tile = refs
    else:
        core, turned, weights, pieces, grouped, tile = refs
    slots = blocks.shape[0]
    cells_z = 8 * blocks_z
    per = LANES // blocks_z
    windows = blocks_x * blocks_y * blocks_z
    sub = lax.broadcasted_iota(jnp.int32, (8, LANES), 0)
    for g in range(slots // LANES):
        turned[g] = jnp.transpose(blocks[g * LANES : (g + 1) * LANES, :])

    @pl.loop(0, slots // LANES)
    def _(g):
        def rows(start):
            return turned[g, pl.ds(pl.multiple_of(start, 8), 8), :]

        @pl.loop(0, 8)
        def _(a):
            for e in range(8):
                here = rows((a + 1) * 64 + e * 8)
                x_diff = rows(a * 64 + e * 8) - rows((a + 2) * 64 + e * 8)
                z_low = rows((a + 1) * 64 + e * 8 - 8) if e > 0 else rows(640 + a * 8)
                z_top = rows((a + 1) * 64 + e * 8 + 8) if e < 7 else rows(704 + a * 8)
                y_low = jnp.where(
                    sub == 0, turned[g, pl.ds(768 + e * 8 + a, 1), :], pltpu.roll(here, 1, 0)
                )
                y_top = jnp.where(
                    sub == 7, turned[g, pl.ds(832 + e * 8 + a, 1), :], pltpu.roll(here, 7, 0)
                )
                for axis, diff in enumerate((x_diff, y_low - y_top, z_low - z_top)):
                    for k, weight in enumerate(spline(jnp.clip(diff * 0.5, -1.0, 1.0))):
                        weights[axis * 5 + k, a * 8 + e] = weight

        top_lanes = pl.ds(pl.multiple_of(g * LANES, LANES), LANES)
        rest_lanes = pl.ds(pl.multiple_of(slots + g * LANES, LANES), LANES)

        def cell_row(s, depths):
            sums = {}
            for a in range(8):
                for k in depths:
                    at = a * 8 + (s - k)
                    w_z = weights[10 + k, at]
                    w_y = [weights[5 + j, at] for j in range(5)]
                    for i in range(5):
                        plane = weights[i, at] * w_z
                        for j in range(5):
                            key = (a + i, j)
                            term = plane * w_y[j]
                            sums[key] = sums[key] + term if key in sums else term
                for u in [a] if a < 7 else range(7, 12):
                    head = sums[u, 0]
                    tail = jnp.zeros_like(head)
                    for j in range(1, 5):
                        moved = pltpu.roll(sums[u, j], j, 0)
                        head = head + jnp.where(sub >= j, moved, 0.0)
                        tail = tail + jnp.where(sub < j, moved, 0.0)
                    both = jnp.concatenate([head, tail], 0)
                    top, rest = split(both, 2)
                    out = pl.ds(pl.multiple_of((s * 12 + u) * 16, 16), 16)
                    pieces[out, top_lanes] = top
                    pieces[out, rest_lanes] = rest

        for s in (0, 1, 2, 3, 8, 9, 10, 11):
            cell_row(s, [k for k in range(5) if 0 <= s - k < 8])

        @pl.loop(4, 8)
        def _(s):
            cell_row(s, range(5))

    named = (labels[...] == lax.broadcasted_iota(jnp.int32, (windows, slots), 0)).astype(F32)
    named = jnp.transpose(named).astype(BF16)
    area = 12 * 16
    named = jnp.concatenate([named, named], 0)

    @pl.loop(0, 12 // per)
    def _(quad):
        rows = pl.ds(pl.multiple_of(quad * per * area, 16), per * area)
        summed = dot(pieces[rows, :], named)
        for wide in range(windows // LANES):
            lanes = slice(wide * LANES, (wide + 1) * LANES)
            part = [summed[k * area : (k + 1) * area, lanes] for k in range(per)]
            for t, item in enumerate(swap_groups(part, blocks_z)):
                rows = slice((wide * per + t) * area, (wide * per + t + 1) * area)
                grouped[0, quad, rows, :], grouped[1, quad, rows, :] = split(item, 2)

    depth = 12 * blocks_z
    row = lax.broadcasted_iota(jnp.int32, (depth, cells_z), 0)
    wanted = (8 * (row % blocks_z) + row // blocks_z + cells_z - 2) % cells_z
    place = (wanted == lax.broadcasted_iota(jnp.int32, (depth, cells_z), 1)).astype(BF16)
    tile[...] = before[...] if last else jnp.zeros_like(tile)
    quads = depth // LANES
    left = jnp.concatenate([grouped[piece, quad] for piece in range(2) for quad in range(quads)], 1)
    total = dot(left, jnp.concatenate([place, place], 0))
    for bx in range(blocks_x):
        for by in range(blocks_y):
            at = (bx * blocks_y + by) * area
            rows = slice(bx * 8, bx * 8 + 12)
            cols = slice(by * 8, by * 8 + 16)
            tile[rows, cols, :] = tile[rows, cols, :] + total[at : at + area].reshape(12, 16, cells_z)

    if not last:
        core[...] = tile[...]
        return
    rows_x, rows_y = 8 * blocks_x, 8 * blocks_y
    core[...] = tile[2 : rows_x + 2, 2 : rows_y + 2, :]
    for side in range(2):
        x = side * (rows_x + 2)
        y = side * (rows_y + 2)
        x_rims[side] = tile[x : x + 2, 2 : rows_y + 2, :]
        y_rims[side] = tile[:, y : y + 2, :]


def corner_kernel(x_rims, y_low, y_top, out):
    rows_x, rows_y = y_low.shape[0] - 4, x_rims.shape[2]
    for side in range(2):
        x = side * (rows_x + 2)
        out[side] = x_rims[side]
        out[side, :, 0:2, :] = out[side, :, 0:2, :] + y_low[x : x + 2]
        out[side, :, rows_y - 2 :, :] = out[side, :, rows_y - 2 :, :] + y_top[x : x + 2]


def rim_kernel(core, y_low, y_top, x_low, x_top, out):
    rows_x, rows_y, _ = core.shape
    out[...] = core[...]
    for part, face in ((slice(0, 2), y_low), (slice(rows_y - 2, rows_y), y_top)):
        out[:, part, :] = out[:, part, :] + face[2 : rows_x + 2]
    for part, face in ((slice(0, 2), x_low), (slice(rows_x - 2, rows_x), x_top)):
        out[part] = out[part] + face[...]


def per_device(potential, owner, window):
    rows_x, rows_y, cells_z = potential.shape
    tiles_x, tiles_y = lax.axis_size("px"), lax.axis_size("py")
    tiles = tiles_x * tiles_y
    grid_x, grid_y = rows_x * tiles_x, rows_y * tiles_y
    planes = cells_z // tiles
    inner = rows_x * rows_y
    used = inner + -(-2 * (rows_x + rows_y) // LANES) * LANES
    blocks_x, blocks_y, blocks_z = rows_x // 8, rows_y // 8, cells_z // 8
    blocks = blocks_x * blocks_y * blocks_z
    half = max(2, 2 * blocks // tiles) // 2
    both = ("px", "py")

    def exchange(x):
        return lax.all_to_all(x, both, split_axis=0, concat_axis=0, tiled=True)

    slots, labels = call(
        functools.partial(slot_kernel, half, 2 * (rows_x + rows_y)),
        (shape(1, blocks, dtype=jnp.int32), shape(tiles, LANES)),
        [], 8, 2 * tiles * LANES * blocks, 8 * blocks,
    )(owner.reshape(blocks, 1), owner.reshape(1, blocks), window.reshape(1, blocks))

    last_x, last_y = rows_x - 1, rows_y - 1
    y_faces = jnp.stack([send(potential[:, last_y], "py", 1), send(potential[:, 0], "py", -1)])
    x_lines = [
        jnp.concatenate([y_faces[0, x : x + 1], potential[x], y_faces[1, x : x + 1]])
        for x in (last_x, 0)
    ]
    x_faces = jnp.stack([send(x_lines[0], "px", 1), send(x_lines[1], "px", -1)])

    z_high, z_low = pieces_of(table_of(cells_z))
    halves = shape(inner, cells_z, dtype=BF16)
    source = call(
        source_kernel, (halves, halves), [pltpu.VMEM((rows_x, rows_y + 16, cells_z), F32)],
        8, 60 * inner * cells_z, 2 << 20,
    )(potential, y_faces)
    spectrum = call(
        spectrum_kernel, shape(cells_z, inner),
        [pltpu.VMEM((3, rows_y + 16, cells_z), F32)] + [pltpu.VMEM((inner, cells_z), BF16)] * 2,
        12, 6 * inner * cells_z**2, 2 << 20,
    )(potential, y_faces, x_faces, *source, z_high, z_low)
    slab = exchange(spectrum).reshape(tiles, planes, inner)

    scale = SECOND_ORDER / (grid_x * grid_y * cells_z)
    if planes % 8 == 0 and tiles_y % (LANES // rows_y) == 0 and grid_x == LANES:
        first = (lax.axis_index(both) * planes).astype(jnp.int32).reshape(1)
        x_table, y_table = table_of(grid_x), table_of(grid_y)
        starts = np.arange(tiles_y) * rows_y
        edge = np.concatenate([(starts - 1) % grid_y, (starts + rows_y) % grid_y])
        lap_xy = laplace_of(grid_x)[:, None] + laplace_of(grid_y)[None, :]
        tables = pieces_of(x_table) + pieces_of(y_table) + pieces_of(y_table[edge])
        body = functools.partial(solve_kernel, tiles_x, tiles_y, rows_x, rows_y, scale)
        specs = [SMEM, SMEM] + [VMEM] * 9
        returned = pl.pallas_call(
            body,
            out_shape=shape(tiles, planes, used),
            in_specs=specs,
            out_specs=VMEM,
            scratch_shapes=[
                pltpu.VMEM((grid_x * planes, grid_y), F32),
                pltpu.VMEM((grid_x * planes, grid_y), F32),
                pltpu.VMEM((2 * tiles_y * planes, grid_x), F32),
            ],
            compiler_params=pltpu.CompilerParams(vmem_limit_bytes=16 << 20),
            cost_estimate=pl.CostEstimate(
                flops=24 * planes * grid_x**2 * grid_y, bytes_accessed=2 << 20, transcendentals=0
            ),
        )(first, laplace_of(cells_z), slab, labels, lap_xy, *tables)
    else:
        returned = solve_plain(slab, labels, rows_x, rows_y, cells_z, tiles_x, tiles_y, scale)
    modes = exchange(returned.reshape(cells_z, used))

    width = -(-10 * blocks_z // LANES) * LANES
    cells = pltpu.VMEM((used, cells_z), F32)
    tile_args = (potential, x_faces, y_faces, modes, z_high, z_low)
    *sent, arrived_labels = call(
        functools.partial(block_kernel, planes, half),
        (shape(blocks, ROWS), shape(blocks, ROWS), shape(2, 1, blocks, dtype=jnp.int32)),
        [cells, pltpu.VMEM((width // LANES, used, LANES), F32), pltpu.VMEM((ROWS, blocks), F32)],
        24, 20 * used * cells_z**2, 6 << 20,
    )(*tile_args, slots)
    displacement = call(
        displacement_kernel, shape(3, rows_x, rows_y, cells_z),
        [pltpu.VMEM((rows_x, rows_y + 16, cells_z), F32), cells],
        16, 6 * used * cells_z**2, 4 << 20,
    )(*tile_args)

    first = exchange(sent[0])
    later, displacement = lax.optimization_barrier((sent[1], displacement))
    arrived = first, exchange(later)
    tile_shape = (rows_x + 4, rows_y + 8, cells_z)
    scratch = [
        pltpu.VMEM((blocks // LANES, ROWS, LANES), F32),
        pltpu.VMEM((15, 64, 8, LANES), F32),
        pltpu.VMEM((12 * 12 * 16, 2 * blocks), BF16),
        pltpu.VMEM((2, 12 * blocks_z // LANES, blocks_x * blocks_y * 12 * 16, LANES), BF16),
        pltpu.VMEM(tile_shape, F32),
    ]
    sizes = (blocks_x, blocks_y, blocks_z)
    cost = (300 * blocks * 512, 4 << 20)
    tile = call(
        functools.partial(deposit_kernel, *sizes, False), shape(*tile_shape), scratch, 32, *cost
    )(arrived[0], arrived_labels[0])
    core, x_rims, y_rims = call(
        functools.partial(deposit_kernel, *sizes, True),
        (
            shape(rows_x, rows_y, cells_z), shape(2, 2, rows_y, cells_z),
            shape(2, rows_x + 4, 2, cells_z),
        ),
        scratch, 32, *cost,
    )(arrived[1], arrived_labels[1], tile)

    y_sides = send(y_rims[1], "py", 1), send(y_rims[0], "py", -1)
    x_rims = call(corner_kernel, shape(*x_rims.shape), [], 4, 8 * rows_y * cells_z, 1 << 17)(
        x_rims, *y_sides
    )
    x_sides = send(x_rims[1], "px", 1), send(x_rims[0], "px", -1)
    density = call(rim_kernel, shape(rows_x, rows_y, cells_z), [], 8, inner * cells_z, 2 << 20)(
        core, *y_sides, *x_sides
    )
    return (displacement, density)


def solution(mesh):
    return jax.shard_map(
        per_device,
        mesh=mesh,
        in_specs=(P("px", "py", None), P("px", "py", None, None), P("px", "py", None)),
        out_specs=(P(None, "px", "py", None), P("px", "py", None)),
        check_vma=False,
    )
```

```python
import functools
import math

import jax
import jax.numpy as jnp
import numpy as np
from jax import lax
from jax.experimental import pallas as pl
from jax.experimental.pallas import tpu as pltpu
from jax.sharding import PartitionSpec as P

SECOND_ORDER = 3.0 / 7.0
F32 = jnp.float32
BF16 = jnp.bfloat16
LANES = 128
ROWS = 896
VMEM = pl.BlockSpec(memory_space=pltpu.VMEM)
SMEM = pl.BlockSpec(memory_space=pltpu.SMEM)
FAR = pl.BlockSpec(memory_space=pltpu.HBM)
NN = (((1,), (0,)), ((), ()))
NT = (((1,), (1,)), ((), ()))
TN = (((0,), (0,)), ((), ()))


def split(x, pieces):
    out = []
    for piece in range(pieces):
        part = x.astype(BF16)
        out.append(part)
        if piece < pieces - 1:
            x = x - part.astype(F32)
    return out


def dot(a, b, dims=NN):
    return lax.dot_general(a, b, dims, preferred_element_type=F32)


def dot3(a, b, dims=NN):
    return dot(a[0], b[0], dims) + (dot(a[0], b[1], dims) + dot(a[1], b[0], dims))


def swap_groups(rows, group):
    rows = list(rows)
    count = len(rows)
    axis = rows[0].ndim - 1
    lane = lax.broadcasted_iota(jnp.int32, rows[0].shape, axis) // group
    step = 1
    while step < count:
        low = (lane & step) == 0
        for k in range(count):
            if k & step:
                continue
            a, b = rows[k], rows[k + step]
            rows[k] = jnp.where(low, a, pltpu.roll(b, step * group, axis))
            rows[k + step] = jnp.where(low, pltpu.roll(a, LANES - step * group, axis), b)
        step *= 2
    return rows


def table_of(length):
    modes = np.arange(length)
    angle = (modes[:, None] * modes[None, :] % length) * (2.0 * math.pi / length)
    return (np.cos(angle) + np.sin(angle)).astype(np.float32)


def pieces_of(table):
    high = table.astype(jnp.bfloat16)
    low = (table - high.astype(np.float32)).astype(jnp.bfloat16)
    return np.asarray(high), np.asarray(low)


def seeds_of(length, step):
    along = np.arange(length)
    coarse = (np.arange(length // step)[:, None] * step * along[None, :] % length) * (2.0 * math.pi / length)
    fine = (np.arange(step)[:, None] * along[None, :] % length) * (2.0 * math.pi / length)
    rows = [np.cos(coarse), np.sin(coarse), np.cos(fine) + np.sin(fine), np.cos(fine) - np.sin(fine)]
    return np.concatenate(rows).astype(np.float32)


def laplace_of(length):
    return (2.0 * np.cos(np.arange(length) * (2.0 * math.pi / length)) - 2.0).astype(np.float32)


def call(body, outs, scratch, vmem, flops, moved):
    return pl.pallas_call(
        body,
        out_shape=outs,
        scratch_shapes=scratch,
        compiler_params=pltpu.CompilerParams(vmem_limit_bytes=vmem << 20),
        cost_estimate=pl.CostEstimate(flops=flops, bytes_accessed=moved, transcendentals=0),
    )


def shape(*dims, dtype=F32):
    return jax.ShapeDtypeStruct(dims, dtype)


def send(x, axis, step):
    size = lax.axis_size(axis)
    return lax.ppermute(x, axis, [(i, (i + step) % size) for i in range(size)])


def slot_kernel(half, start, owner_col, owner_row, window_row, slot_out, label_out):
    count = owner_row.shape[1]
    tiles = label_out.shape[0]
    later = lax.broadcasted_iota(jnp.int32, (count, count), 0) < lax.broadcasted_iota(
        jnp.int32, (count, count), 1
    )
    owners = owner_row[...]
    same = (owner_col[...] == owners) & later
    rank = jnp.sum(same.astype(F32), axis=0, keepdims=True).astype(jnp.int32)
    second = rank >= half
    place = owners * half + jnp.where(second, rank - half, rank)
    slot_out[...] = jnp.where(second, place + count, place)
    tile = lax.broadcasted_iota(jnp.int32, (tiles, count), 0)
    named = jnp.where(tile == owners, window_row[...] + 1, 0).astype(F32).astype(BF16)
    lane = lax.broadcasted_iota(jnp.int32, (LANES, count), 0)
    label_out[...] = dot(named, (lane == rank + start).astype(BF16), NT) - 1.0


def source_of(at, cells_z):
    def ahead(value):
        return pltpu.roll(value, cells_z - 1, 1)

    def behind(value):
        return pltpu.roll(value, 1, 1)

    here = at(0, 0)
    ahead_x, behind_x, ahead_y, behind_y = at(1, 0), at(-1, 0), at(0, 1), at(0, -1)
    xx = ahead_x - 2.0 * here + behind_x
    yy = ahead_y - 2.0 * here + behind_y
    zz = ahead(here) - 2.0 * here + behind(here)
    xy = (at(1, 1) - at(1, -1) - at(-1, 1) + at(-1, -1)) * 0.25
    across_x, across_y = ahead_x - behind_x, ahead_y - behind_y
    xz = (ahead(across_x) - behind(across_x)) * 0.25
    yz = (ahead(across_y) - behind(across_y)) * 0.25
    return xx * yy + xx * zz + yy * zz - xy * xy - xz * xz - yz * yz


def prepare_kernel(potential, core, y_last, y_first, sem):
    copy = pltpu.make_async_copy(potential, core, sem)
    copy.start()
    copy.wait()
    rows_x, rows_y, _ = core.shape
    for x in range(rows_x):
        y_last[x : x + 1, :] = core[x, rows_y - 1 : rows_y, :]
        y_first[x : x + 1, :] = core[x, 0:1, :]


def source_kernel(step, core, y_faces, seeds, high, low, table_high, table_low, pad):
    coarse = seeds.shape[1] // step
    fine = seeds[2 * coarse : 2 * coarse + step, :]
    turned = seeds[2 * coarse + step : 2 * coarse + 2 * step, :]
    for k in range(coarse):
        rows = slice(k * step, (k + 1) * step)
        value = seeds[k : k + 1, :] * fine + seeds[coarse + k : coarse + k + 1, :] * turned
        table_high[rows, :], table_low[rows, :] = split(value, 2)
    rows_x, rows_y, cells_z = core.shape
    pad[:, 8 : rows_y + 8, :] = core[...]
    for x in range(rows_x):
        pad[x, 7:8, :] = y_faces[0, x : x + 1, :]
        pad[x, rows_y + 8 : rows_y + 9, :] = y_faces[1, x : x + 1, :]

    @pl.loop(1, rows_x - 1, unroll=3)
    def _(x):
        def at(dx, dy):
            return pad[x + dx, 8 + dy : 8 + dy + rows_y, :]

        rows = pl.ds(pl.multiple_of(x * rows_y, rows_y), rows_y)
        high[rows, :], low[rows, :] = split(source_of(at, cells_z), 2)

    for x in (0, rows_x - 1):
        rows = slice(x * rows_y, (x + 1) * rows_y)
        high[rows, :] = jnp.zeros((rows_y, cells_z), BF16)
        low[rows, :] = jnp.zeros((rows_y, cells_z), BF16)


def spectrum_kernel(core, y_faces, x_faces, inner_high, inner_low, high, low, spectrum, pad, source_high, source_low):
    rows_x, rows_y, cells_z = core.shape
    source_high[...] = inner_high[...]
    source_low[...] = inner_low[...]
    for side in range(2):
        edge = side * (rows_x - 1)
        for line in range(3):
            x = edge + line - 1
            if 0 <= x < rows_x:
                pad[line, 8 : rows_y + 8, :] = core[x]
                pad[line, 7:8, :] = y_faces[0, x : x + 1, :]
                pad[line, rows_y + 8 : rows_y + 9, :] = y_faces[1, x : x + 1, :]
            else:
                pad[line, 7 : rows_y + 9, :] = x_faces[side]

        def at(dx, dy):
            return pad[1 + dx, 8 + dy : 8 + dy + rows_y, :]

        rows = slice(edge * rows_y, (edge + 1) * rows_y)
        source_high[rows, :], source_low[rows, :] = split(source_of(at, cells_z), 2)
    spectrum[...] = dot3((high[...], low[...]), (source_high[...], source_low[...]), NT)


def solve_kernel(
    tiles_x, tiles_y, rows_x, rows_y, scale,
    first, lap_z, slab, labels, lap_xy, hx_high, hx_low, hy_high, hy_low, hf_high, hf_low,
    out, planes, solved_planes, faces,
):
    grid_x, grid_y = tiles_x * rows_x, tiles_y * rows_y
    count = slab.shape[1]
    per = LANES // rows_y
    chunk = rows_x * count

    def stacked(pieces):
        high, low = pieces
        zero = jnp.zeros_like(high)
        return jnp.concatenate(
            [jnp.concatenate([high, low], 1), jnp.concatenate([high, zero], 1)], 0
        )

    def joined(value):
        width = value.shape[1] // 2
        return value[:, :width] + value[:, width:]

    along_y = stacked((hy_high[...], hy_low[...]))
    along_x = jnp.concatenate([hx_high[...], hx_low[...]], 1)
    high, low = hf_high[...], hf_low[...]
    along_f = jnp.concatenate(
        [jnp.concatenate([high, high], 1), jnp.concatenate([low, jnp.zeros_like(low)], 1)], 0
    )

    def times_y(value):
        return joined(dot(jnp.concatenate(split(value, 2), 1), along_y))

    for i in range(tiles_x):
        for part in range(rows_x // per):
            lanes = slice(part * LANES, (part + 1) * LANES)
            lines = [[] for _ in range(per)]
            for wide in range(tiles_y // per):
                rows = [slab[i * tiles_y + wide * per + j, :, lanes] for j in range(per)]
                for t, row in enumerate(swap_groups(rows, rows_y)):
                    lines[t].append(row)
            x = (i * rows_x + part * per) * count
            block = jnp.concatenate([jnp.concatenate(line, 1) for line in lines], 0)
            planes[x : x + per * count, :] = times_y(block)
    for q in range(count):
        rows = pl.ds(q, grid_x, stride=count)
        modes = joined(dot(along_x, stacked(split(planes[rows, :], 2))))
        eigen = lap_xy[...] + lap_z[first[0] + q]
        anchor = eigen == 0.0
        solved = jnp.where(anchor, 0.0, scale / jnp.where(anchor, -1.0, eigen)) * modes
        back = joined(dot(along_x, stacked(split(solved, 2))))
        solved_planes[rows, :] = back
        pieces = jnp.concatenate(split(back, 2), 1)
        value = dot(along_f, pieces, NT)
        faces[pl.ds(q, 2 * tiles_y, stride=count), :] = value[: 2 * tiles_y] + value[2 * tiles_y :]
    for i in range(tiles_x):
        rows = slice(i * chunk, (i + 1) * chunk)
        planes[rows, :] = times_y(solved_planes[rows, :])

    lane = lax.broadcasted_iota(jnp.int32, (count, LANES), 1)
    for i in range(tiles_x):
        for wide in range(tiles_y // per):
            cols = slice(wide * LANES, (wide + 1) * LANES)

            def row_of(x):
                x = x % grid_x
                return planes[x * count : (x + 1) * count, cols]

            for part in range(rows_x // per):
                lanes = slice(part * LANES, (part + 1) * LANES)
                rows = [row_of(i * rows_x + part * per + t) for t in range(per)]
                for j, row in enumerate(swap_groups(rows, rows_y)):
                    out[i * tiles_y + wide * per + j, :, lanes] = row
            before, after = row_of(i * rows_x - 1), row_of((i + 1) * rows_x)
            for k in range(per):
                j = wide * per + k
                shift = (LANES - k * rows_y) % LANES
                line = pltpu.roll(before, shift, 1) if shift else before
                moved = pltpu.roll(after, (shift + rows_y) % LANES, 1)
                line = jnp.where(lane < rows_y, line, moved)
                for side in range(2):
                    at = (side * tiles_y + j) * count
                    face = faces[at : at + count, :]
                    start = 2 * rows_y + side * rows_x
                    move = (start - i * rows_x) % LANES
                    face = pltpu.roll(face, move, 1) if move else face
                    line = jnp.where(lane < start, line, face)
                at = i * tiles_y + j
                line = jnp.where(lane < 2 * (rows_x + rows_y), line, labels[at : at + 1, :])
                out[i * tiles_y + j, :, rows_x * rows_y : rows_x * rows_y + LANES] = line


def solve_plain(slab, labels, rows_x, rows_y, cells_z, tiles_x, tiles_y, scale):
    high = lax.Precision.HIGHEST
    grid_x, grid_y = tiles_x * rows_x, tiles_y * rows_y
    count = slab.shape[1]
    hx, hy = jnp.asarray(table_of(grid_x)), jnp.asarray(table_of(grid_y))
    planes = slab.reshape(tiles_x, tiles_y, count, rows_x, rows_y).transpose(2, 0, 3, 1, 4)
    planes = planes.reshape(count, grid_x, grid_y)
    modes = jnp.einsum("qxy,xk,yl->qkl", planes, hx, hy, precision=high)
    first = lax.axis_index(("px", "py")) * count
    lap_z = lax.dynamic_slice_in_dim(jnp.asarray(laplace_of(cells_z)), first, count)
    eigen = (
        jnp.asarray(laplace_of(grid_x))[None, :, None]
        + jnp.asarray(laplace_of(grid_y))[None, None, :]
        + lap_z[:, None, None]
    )
    anchor = eigen == 0.0
    solved = jnp.where(anchor, 0.0, scale / jnp.where(anchor, -1.0, eigen)) * modes
    back = jnp.einsum("qkl,xk,yl->qxy", solved, hx, hy, precision=high)
    tiles = back.reshape(count, tiles_x, rows_x, tiles_y, rows_y).transpose(1, 3, 0, 2, 4)
    starts_x, starts_y = np.arange(tiles_x) * rows_x, np.arange(tiles_y) * rows_y
    faces = []
    for edge in (-1, rows_x):
        line = back[:, (starts_x + edge) % grid_x].reshape(count, tiles_x, tiles_y, rows_y)
        faces.append(line.transpose(1, 2, 0, 3))
    for edge in (-1, rows_y):
        line = back[:, :, (starts_y + edge) % grid_y].reshape(count, tiles_x, rows_x, tiles_y)
        faces.append(line.transpose(1, 3, 0, 2))
    tail = labels[:, 2 * (rows_x + rows_y) :].reshape(tiles_x, tiles_y, 1, -1)
    faces.append(jnp.broadcast_to(tail, (tiles_x, tiles_y, count, tail.shape[-1])))
    parts = [tiles.reshape(tiles_x, tiles_y, count, rows_x * rows_y)] + faces
    return jnp.concatenate(parts, -1).reshape(tiles_x * tiles_y, count, -1)


def combine(core, x_faces, y_faces, spectrum, high, low, cells):
    rows_x, rows_y, cells_z = core.shape
    inner = rows_x * rows_y
    cells[...] = dot3(split(spectrum[...], 2), (high[...], low[...]), TN)
    cells[0:inner, :] = cells[0:inner, :] + core[...].reshape(inner, cells_z)
    start = inner
    for faces, skip in ((x_faces, 1), (y_faces, 0)):
        for side in range(2):
            length = faces.shape[1] - 2 * skip
            rows = slice(start, start + length)
            cells[rows, :] = cells[rows, :] + faces[side, skip : skip + length, :]
            start += length
    x_edge = [inner, inner + rows_y]
    y_edge = [inner + 2 * rows_y, inner + 2 * rows_y + rows_x]
    return x_edge, y_edge


def displacement_kernel(core, x_faces, y_faces, spectrum, high, low, displacement, pad, cells):
    rows_x, rows_y, cells_z = core.shape
    x_edge, y_edge = combine(core, x_faces, y_faces, spectrum, high, low, cells)
    for x in range(rows_x):
        pad[x, 8 : rows_y + 8, :] = cells[x * rows_y : (x + 1) * rows_y, :]
        pad[x, 7:8, :] = cells[y_edge[0] + x : y_edge[0] + x + 1, :]
        pad[x, rows_y + 8 : rows_y + 9, :] = cells[y_edge[1] + x : y_edge[1] + x + 1, :]

    def line(x):
        if x < 0:
            return cells[x_edge[0] : x_edge[0] + rows_y, :]
        if x >= rows_x:
            return cells[x_edge[1] : x_edge[1] + rows_y, :]
        return cells[x * rows_y : (x + 1) * rows_y, :]

    for x in range(rows_x):
        here = line(x)
        displacement[0, x] = (line(x - 1) - line(x + 1)) * 0.5
        displacement[1, x] = (pad[x, 7 : rows_y + 7, :] - pad[x, 9 : rows_y + 9, :]) * 0.5
        displacement[2, x] = (pltpu.roll(here, 1, 1) - pltpu.roll(here, cells_z - 1, 1)) * 0.5


def block_kernel(
    planes, half, core, x_faces, y_faces, spectrum, high, low, slots,
    out, values, labels,
    cells, spread,
):
    rows_x, rows_y, cells_z = core.shape
    inner = rows_x * rows_y
    blocks_x, blocks_y, blocks_z = rows_x // 8, rows_y // 8, cells_z // 8
    per = LANES // blocks_z
    x_edge, y_edge = combine(core, x_faces, y_faces, spectrum, high, low, cells)

    width = spread.shape[0] * LANES
    col = lax.broadcasted_iota(jnp.int32, (cells_z, width), 1)
    wanted = (8 * (col % blocks_z) + col // blocks_z + cells_z - 1) % cells_z
    choose = (wanted == lax.broadcasted_iota(jnp.int32, (cells_z, width), 0)).astype(BF16)
    pieces = split(cells[...], 3)
    moved = dot(pieces[0], choose) + dot(pieces[1], choose) + dot(pieces[2], choose)
    for quad in range(spread.shape[0]):
        spread[quad] = moved[:, quad * LANES : (quad + 1) * LANES]

    def put(row, tiles):
        for quad in range(width // LANES):
            every = [tiles(b // blocks_y, b % blocks_y, quad) for b in range(blocks_x * blocks_y)]
            for block in range(0, len(every), per):
                for k, item in enumerate(swap_groups(every[block : block + per], blocks_z)):
                    where = row(quad * per + k - 1)
                    if where is not None:
                        start = block * blocks_z
                        values[where : where + 8, start : start + LANES] = item

    def x_tile(a):
        def tile(bx, by, quad):
            x = 8 * bx + a
            top = x_edge[0] if x < 0 else x_edge[1] if x >= rows_x else x * rows_y
            return spread[quad, top + 8 * by : top + 8 * by + 8, :]

        return tile

    for a in range(-1, 9):
        def row(e, a=a):
            if 0 <= e < 8:
                return ((a + 1) * 8 + e) * 8
            if e in (-1, 8) and 0 <= a < 8:
                return 640 + (64 if e == 8 else 0) + a * 8
            return None

        put(row, x_tile(a))
    for side, edge in enumerate((-1, 8)):
        def tile(bx, by, quad, edge=edge):
            y = 8 * by + edge
            if y < 0 or y >= rows_y:
                top = y_edge[0 if y < 0 else 1] + 8 * bx
                return spread[quad, top : top + 8, :]
            return spread[quad, pl.ds(8 * bx * rows_y + y, 8, stride=rows_y), :]

        put(lambda e, side=side: 768 + side * 64 + e * 8 if 0 <= e < 8 else None, tile)

    count = slots.shape[1]
    named = spectrum[:, inner : inner + LANES].astype(BF16)
    row = lax.broadcasted_iota(jnp.int32, (cells_z, count), 0)
    slot = lax.broadcasted_iota(jnp.int32, (cells_z, count), 1)
    source = (row % planes == 0) & (row // planes == slot // half)
    by_lane = dot(named, source.astype(BF16), TN)
    lane = lax.broadcasted_iota(jnp.int32, (LANES, count), 0) - 2 * (rows_x + rows_y)
    place = lax.broadcasted_iota(jnp.int32, (LANES, count), 1) % half
    for part in range(2):
        label = jnp.sum(jnp.where(lane == place + part * half, by_lane, 0.0), axis=0, keepdims=True)
        labels[part] = label.astype(jnp.int32)

    fill_slots(0, values, slots, out)


def fill_slots(part, values, slots, out):
    count = slots.shape[1]
    pieces = split(values[...], 3)
    number = lax.broadcasted_iota(jnp.int32, (count, count), 0) + part * count
    chosen = (slots[...] == number).astype(BF16)
    out[...] = dot(chosen, pieces[0], NT) + dot(chosen, pieces[1], NT) + dot(chosen, pieces[2], NT)


def spline(shift):
    g = jnp.abs(shift)
    h = 1.0 - g
    gg, hh = g * g, h * h
    near = (2.0 / 3.0) - gg + 0.5 * gg * g
    ahead = (2.0 / 3.0) - hh + 0.5 * hh * h
    back = hh * h * (1.0 / 6.0)
    far = gg * g * (1.0 / 6.0)
    up = shift >= 0.0
    zero = jnp.zeros_like(far)
    return (
        jnp.where(up, zero, far),
        jnp.where(up, back, ahead),
        near,
        jnp.where(up, ahead, back),
        jnp.where(up, far, zero),
    )


def deposit_kernel(blocks_x, blocks_y, blocks_z, last, blocks, labels, *refs):
    if last:
        before, core, x_rims, y_rims, turned, weights, pieces, grouped, tile = refs
    else:
        core, turned, weights, pieces, grouped, tile = refs
    slots = blocks.shape[0]
    cells_z = 8 * blocks_z
    per = LANES // blocks_z
    windows = blocks_x * blocks_y * blocks_z
    sub = lax.broadcasted_iota(jnp.int32, (8, LANES), 0)
    for g in range(slots // LANES):
        turned[g] = jnp.transpose(blocks[g * LANES : (g + 1) * LANES, :])

    @pl.loop(0, slots // LANES)
    def _(g):
        def rows(start):
            return turned[g, pl.ds(pl.multiple_of(start, 8), 8), :]

        @pl.loop(0, 8)
        def _(a):
            for e in range(8):
                here = rows((a + 1) * 64 + e * 8)
                x_diff = rows(a * 64 + e * 8) - rows((a + 2) * 64 + e * 8)
                z_low = rows((a + 1) * 64 + e * 8 - 8) if e > 0 else rows(640 + a * 8)
                z_top = rows((a + 1) * 64 + e * 8 + 8) if e < 7 else rows(704 + a * 8)
                y_low = jnp.where(
                    sub == 0, turned[g, pl.ds(768 + e * 8 + a, 1), :], pltpu.roll(here, 1, 0)
                )
                y_top = jnp.where(
                    sub == 7, turned[g, pl.ds(832 + e * 8 + a, 1), :], pltpu.roll(here, 7, 0)
                )
                for axis, diff in enumerate((x_diff, y_low - y_top, z_low - z_top)):
                    for k, weight in enumerate(spline(jnp.clip(diff * 0.5, -1.0, 1.0))):
                        if (axis, k) != (1, 2):
                            weights[axis * 5 + k, a * 8 + e] = weight

        top_lanes = pl.ds(pl.multiple_of(g * LANES, LANES), LANES)
        rest_lanes = pl.ds(pl.multiple_of(slots + g * LANES, LANES), LANES)

        def cell_row(s, depths):
            sums = {}
            for a in range(8):
                for k in depths:
                    at = a * 8 + (s - k)
                    w_z = weights[10 + k, at]
                    w_y = [weights[5 + j, at] if j != 2 else None for j in range(5)]
                    for i in range(5):
                        plane = weights[i, at] * w_z
                        for j in range(5):
                            key = (a + i, j)
                            term = plane * w_y[j] if j != 2 else plane
                            sums[key] = sums[key] + term if key in sums else term
                for u in [a] if a < 7 else range(7, 12):
                    rows = [sums[u, j] for j in range(5)]
                    rows[2] = rows[2] - ((rows[0] + rows[1]) + (rows[3] + rows[4]))
                    moved = [pltpu.roll(rows[j], j, 0) for j in range(1, 5)]
                    every = rows[0] + ((moved[0] + moved[1]) + (moved[2] + moved[3]))
                    past = [jnp.where(sub < j + 1, moved[j], 0.0) for j in range(4)]
                    tail = (past[0] + past[1]) + (past[2] + past[3])
                    top, rest = split(jnp.concatenate([every - tail, tail], 0), 2)
                    out = pl.ds(pl.multiple_of((s * 12 + u) * 16, 16), 16)
                    pieces[out, top_lanes] = top
                    pieces[out, rest_lanes] = rest

        for s in (0, 1, 2, 3, 8, 9, 10, 11):
            cell_row(s, [k for k in range(5) if 0 <= s - k < 8])

        @pl.loop(4, 8)
        def _(s):
            cell_row(s, range(5))

    named = (labels[...] == lax.broadcasted_iota(jnp.int32, (windows, slots), 0)).astype(F32)
    named = jnp.transpose(named).astype(BF16)
    area = 12 * 16
    named = jnp.concatenate([named, named], 0)

    @pl.loop(0, 12 // per)
    def _(quad):
        rows = pl.ds(pl.multiple_of(quad * per * area, 16), per * area)
        summed = dot(pieces[rows, :], named)
        for wide in range(windows // LANES):
            lanes = slice(wide * LANES, (wide + 1) * LANES)
            part = [summed[k * area : (k + 1) * area, lanes] for k in range(per)]
            for t, item in enumerate(swap_groups(part, blocks_z)):
                rows = slice((wide * per + t) * area, (wide * per + t + 1) * area)
                grouped[0, quad, rows, :], grouped[1, quad, rows, :] = split(item, 2)

    depth = 12 * blocks_z
    row = lax.broadcasted_iota(jnp.int32, (depth, cells_z), 0)
    wanted = (8 * (row % blocks_z) + row // blocks_z + cells_z - 2) % cells_z
    place = (wanted == lax.broadcasted_iota(jnp.int32, (depth, cells_z), 1)).astype(BF16)
    tile[...] = before[...] if last else jnp.zeros_like(tile)
    quads = depth // LANES
    left = jnp.concatenate([grouped[piece, quad] for piece in range(2) for quad in range(quads)], 1)
    total = dot(left, jnp.concatenate([place, place], 0))
    for bx in range(blocks_x):
        for by in range(blocks_y):
            at = (bx * blocks_y + by) * area
            rows = slice(bx * 8, bx * 8 + 12)
            cols = slice(by * 8, by * 8 + 16)
            tile[rows, cols, :] = tile[rows, cols, :] + total[at : at + area].reshape(12, 16, cells_z)

    if not last:
        core[...] = tile[...]
        return
    rows_x, rows_y = 8 * blocks_x, 8 * blocks_y
    core[...] = tile[2 : rows_x + 2, 2 : rows_y + 2, :]
    for side in range(2):
        x = side * (rows_x + 2)
        y = side * (rows_y + 2)
        x_rims[side] = tile[x : x + 2, 2 : rows_y + 2, :]
        y_rims[side] = tile[:, y : y + 2, :]


def corner_kernel(x_rims, y_low, y_top, out):
    rows_x, rows_y = y_low.shape[0] - 4, x_rims.shape[2]
    for side in range(2):
        x = side * (rows_x + 2)
        out[side] = x_rims[side]
        out[side, :, 0:2, :] = out[side, :, 0:2, :] + y_low[x : x + 2]
        out[side, :, rows_y - 2 :, :] = out[side, :, rows_y - 2 :, :] + y_top[x : x + 2]


def rim_kernel(core, y_low, y_top, x_low, x_top, out):
    rows_x, rows_y, _ = core.shape
    out[...] = core[...]
    for part, face in ((slice(0, 2), y_low), (slice(rows_y - 2, rows_y), y_top)):
        out[:, part, :] = out[:, part, :] + face[2 : rows_x + 2]
    for part, face in ((slice(0, 2), x_low), (slice(rows_x - 2, rows_x), x_top)):
        out[part] = out[part] + face[...]


def per_device(potential, owner, window):
    rows_x, rows_y, cells_z = potential.shape
    tiles_x, tiles_y = lax.axis_size("px"), lax.axis_size("py")
    tiles = tiles_x * tiles_y
    grid_x, grid_y = rows_x * tiles_x, rows_y * tiles_y
    planes = cells_z // tiles
    inner = rows_x * rows_y
    used = inner + -(-2 * (rows_x + rows_y) // LANES) * LANES
    blocks_x, blocks_y, blocks_z = rows_x // 8, rows_y // 8, cells_z // 8
    blocks = blocks_x * blocks_y * blocks_z
    half = max(2, 2 * blocks // tiles) // 2
    both = ("px", "py")

    def exchange(x):
        return lax.all_to_all(x, both, split_axis=0, concat_axis=0, tiled=True)

    slots, labels = call(
        functools.partial(slot_kernel, half, 2 * (rows_x + rows_y)),
        (shape(1, blocks, dtype=jnp.int32), shape(tiles, LANES)),
        [], 8, 2 * tiles * LANES * blocks, 8 * blocks,
    )(owner.reshape(blocks, 1), owner.reshape(1, blocks), window.reshape(1, blocks))

    line = shape(rows_x, cells_z)
    core, y_last, y_first = pl.pallas_call(
        prepare_kernel,
        out_shape=(shape(rows_x, rows_y, cells_z), line, line),
        in_specs=[FAR],
        out_specs=[VMEM] * 3,
        scratch_shapes=[pltpu.SemaphoreType.DMA],
        compiler_params=pltpu.CompilerParams(vmem_limit_bytes=8 << 20),
        cost_estimate=pl.CostEstimate(flops=0, bytes_accessed=2 << 20, transcendentals=0),
    )(potential)
    last_x = rows_x - 1
    y_faces = jnp.stack([send(y_last, "py", 1), send(y_first, "py", -1)])
    x_lines = [
        jnp.concatenate([y_faces[0, x : x + 1], core[x], y_faces[1, x : x + 1]])
        for x in (last_x, 0)
    ]
    x_faces = jnp.stack([send(x_lines[0], "px", 1), send(x_lines[1], "px", -1)])

    halves = shape(inner, cells_z, dtype=BF16)
    table = shape(cells_z, cells_z, dtype=BF16)
    step = 16
    *source, z_high, z_low = call(
        functools.partial(source_kernel, step), (halves, halves, table, table),
        [pltpu.VMEM((rows_x, rows_y + 16, cells_z), F32)],
        8, 60 * inner * cells_z, 2 << 20,
    )(core, y_faces, seeds_of(cells_z, step))
    spectrum = call(
        spectrum_kernel, shape(cells_z, inner),
        [pltpu.VMEM((3, rows_y + 16, cells_z), F32)] + [pltpu.VMEM((inner, cells_z), BF16)] * 2,
        12, 6 * inner * cells_z**2, 2 << 20,
    )(core, y_faces, x_faces, *source, z_high, z_low)
    slab = exchange(spectrum).reshape(tiles, planes, inner)

    scale = SECOND_ORDER / (grid_x * grid_y * cells_z)
    if planes % 8 == 0 and tiles_y % (LANES // rows_y) == 0 and grid_x == LANES:
        first = (lax.axis_index(both) * planes).astype(jnp.int32).reshape(1)
        x_table, y_table = table_of(grid_x), table_of(grid_y)
        starts = np.arange(tiles_y) * rows_y
        edge = np.concatenate([(starts - 1) % grid_y, (starts + rows_y) % grid_y])
        lap_xy = laplace_of(grid_x)[:, None] + laplace_of(grid_y)[None, :]
        tables = pieces_of(x_table) + pieces_of(y_table) + pieces_of(y_table[edge])
        body = functools.partial(solve_kernel, tiles_x, tiles_y, rows_x, rows_y, scale)
        specs = [SMEM, SMEM] + [VMEM] * 9
        returned = pl.pallas_call(
            body,
            out_shape=shape(tiles, planes, used),
            in_specs=specs,
            out_specs=VMEM,
            scratch_shapes=[
                pltpu.VMEM((grid_x * planes, grid_y), F32),
                pltpu.VMEM((grid_x * planes, grid_y), F32),
                pltpu.VMEM((2 * tiles_y * planes, grid_x), F32),
            ],
            compiler_params=pltpu.CompilerParams(vmem_limit_bytes=16 << 20),
            cost_estimate=pl.CostEstimate(
                flops=24 * planes * grid_x**2 * grid_y, bytes_accessed=2 << 20, transcendentals=0
            ),
        )(first, laplace_of(cells_z), slab, labels, lap_xy, *tables)
    else:
        returned = solve_plain(slab, labels, rows_x, rows_y, cells_z, tiles_x, tiles_y, scale)
    modes = exchange(returned.reshape(cells_z, used))

    width = -(-10 * blocks_z // LANES) * LANES
    cells = pltpu.VMEM((used, cells_z), F32)
    tile_args = (core, x_faces, y_faces, modes, z_high, z_low)
    half_out = shape(blocks, ROWS)
    sent, values, arrived_labels = call(
        functools.partial(block_kernel, planes, half),
        (half_out, shape(ROWS, blocks), shape(2, 1, blocks, dtype=jnp.int32)),
        [cells, pltpu.VMEM((width // LANES, used, LANES), F32)],
        40, 20 * used * cells_z**2, 6 << 20,
    )(*tile_args, slots)
    first = exchange(sent)
    later = call(functools.partial(fill_slots, 1), half_out, [], 16, 6 * ROWS * blocks**2, 4 << 20)(values, slots)
    displacement = call(
        displacement_kernel, shape(3, rows_x, rows_y, cells_z),
        [pltpu.VMEM((rows_x, rows_y + 16, cells_z), F32), cells],
        16, 6 * used * cells_z**2, 4 << 20,
    )(*tile_args)

    later, displacement = lax.optimization_barrier((later, displacement))
    arrived = first, exchange(later)
    tile_shape = (rows_x + 4, rows_y + 8, cells_z)
    scratch = [
        pltpu.VMEM((blocks // LANES, ROWS, LANES), F32),
        pltpu.VMEM((15, 64, 8, LANES), F32),
        pltpu.VMEM((12 * 12 * 16, 2 * blocks), BF16),
        pltpu.VMEM((2, 12 * blocks_z // LANES, blocks_x * blocks_y * 12 * 16, LANES), BF16),
        pltpu.VMEM(tile_shape, F32),
    ]
    sizes = (blocks_x, blocks_y, blocks_z)
    cost = (300 * blocks * 512, 4 << 20)
    tile = call(
        functools.partial(deposit_kernel, *sizes, False), shape(*tile_shape), scratch, 32, *cost
    )(arrived[0], arrived_labels[0])
    middle, x_rims, y_rims = call(
        functools.partial(deposit_kernel, *sizes, True),
        (
            shape(rows_x, rows_y, cells_z), shape(2, 2, rows_y, cells_z),
            shape(2, rows_x + 4, 2, cells_z),
        ),
        scratch, 32, *cost,
    )(arrived[1], arrived_labels[1], tile)

    y_sides = send(y_rims[1], "py", 1), send(y_rims[0], "py", -1)
    x_rims = call(corner_kernel, shape(*x_rims.shape), [], 4, 8 * rows_y * cells_z, 1 << 17)(
        x_rims, *y_sides
    )
    x_sides = send(x_rims[1], "px", 1), send(x_rims[0], "px", -1)
    density = call(rim_kernel, shape(rows_x, rows_y, cells_z), [], 8, inner * cells_z, 2 << 20)(
        middle, *y_sides, *x_sides
    )
    return (displacement, density)


def solution(mesh):
    return jax.shard_map(
        per_device,
        mesh=mesh,
        in_specs=(P("px", "py", None), P("px", "py", None, None), P("px", "py", None)),
        out_specs=(P(None, "px", "py", None), P("px", "py", None)),
        check_vma=False,
    )
```

```python
import functools
import math

import jax
import jax.numpy as jnp
import numpy as np
from jax import lax
from jax.experimental import pallas as pl
from jax.experimental.pallas import tpu as pltpu
from jax.sharding import PartitionSpec as P

SECOND_ORDER = 3.0 / 7.0
F32 = jnp.float32
BF16 = jnp.bfloat16
LANES = 128
ROWS = 896
VMEM = pl.BlockSpec(memory_space=pltpu.VMEM)
SMEM = pl.BlockSpec(memory_space=pltpu.SMEM)
FAR = pl.BlockSpec(memory_space=pltpu.HBM)
NN = (((1,), (0,)), ((), ()))
NT = (((1,), (1,)), ((), ()))
TN = (((0,), (0,)), ((), ()))


def split(x, pieces):
    out = []
    for piece in range(pieces):
        part = x.astype(BF16)
        out.append(part)
        if piece < pieces - 1:
            x = x - part.astype(F32)
    return out


def dot(a, b, dims=NN):
    return lax.dot_general(a, b, dims, preferred_element_type=F32)


def dot3(a, b, dims=NN):
    return dot(a[0], b[0], dims) + (dot(a[0], b[1], dims) + dot(a[1], b[0], dims))


def swap_groups(rows, group):
    rows = list(rows)
    count = len(rows)
    axis = rows[0].ndim - 1
    lane = lax.broadcasted_iota(jnp.int32, rows[0].shape, axis) // group
    step = 1
    while step < count:
        low = (lane & step) == 0
        for k in range(count):
            if k & step:
                continue
            a, b = rows[k], rows[k + step]
            rows[k] = jnp.where(low, a, pltpu.roll(b, step * group, axis))
            rows[k + step] = jnp.where(low, pltpu.roll(a, LANES - step * group, axis), b)
        step *= 2
    return rows


def table_of(length):
    modes = np.arange(length)
    angle = (modes[:, None] * modes[None, :] % length) * (2.0 * math.pi / length)
    return (np.cos(angle) + np.sin(angle)).astype(np.float32)


def pieces_of(table):
    high = table.astype(jnp.bfloat16)
    low = (table - high.astype(np.float32)).astype(jnp.bfloat16)
    return np.asarray(high), np.asarray(low)


def laplace_of(length):
    return (2.0 * np.cos(np.arange(length) * (2.0 * math.pi / length)) - 2.0).astype(np.float32)


def call(body, outs, scratch, vmem, flops, moved):
    return pl.pallas_call(
        body,
        out_shape=outs,
        scratch_shapes=scratch,
        compiler_params=pltpu.CompilerParams(vmem_limit_bytes=vmem << 20),
        cost_estimate=pl.CostEstimate(flops=flops, bytes_accessed=moved, transcendentals=0),
    )


def shape(*dims, dtype=F32):
    return jax.ShapeDtypeStruct(dims, dtype)


def send(x, axis, step):
    size = lax.axis_size(axis)
    return lax.ppermute(x, axis, [(i, (i + step) % size) for i in range(size)])


def slot_kernel(half, start, owner_col, owner_row, window_row, slot_out, label_out):
    count = owner_row.shape[1]
    tiles = label_out.shape[0]
    later = lax.broadcasted_iota(jnp.int32, (count, count), 0) < lax.broadcasted_iota(
        jnp.int32, (count, count), 1
    )
    owners = owner_row[...]
    same = (owner_col[...] == owners) & later
    rank = jnp.sum(same.astype(F32), axis=0, keepdims=True).astype(jnp.int32)
    second = rank >= half
    place = owners * half + jnp.where(second, rank - half, rank)
    slot_out[...] = jnp.where(second, place + count, place)
    tile = lax.broadcasted_iota(jnp.int32, (tiles, count), 0)
    named = jnp.where(tile == owners, window_row[...] + 1, 0).astype(F32).astype(BF16)
    lane = lax.broadcasted_iota(jnp.int32, (LANES, count), 0)
    label_out[...] = dot(named, (lane == rank + start).astype(BF16), NT) - 1.0


def source_of(at, cells_z):
    def ahead(value):
        return pltpu.roll(value, cells_z - 1, 1)

    def behind(value):
        return pltpu.roll(value, 1, 1)

    here = at(0, 0)
    ahead_x, behind_x, ahead_y, behind_y = at(1, 0), at(-1, 0), at(0, 1), at(0, -1)
    xx = ahead_x - 2.0 * here + behind_x
    yy = ahead_y - 2.0 * here + behind_y
    zz = ahead(here) - 2.0 * here + behind(here)
    xy = (at(1, 1) - at(1, -1) - at(-1, 1) + at(-1, -1)) * 0.25
    across_x, across_y = ahead_x - behind_x, ahead_y - behind_y
    xz = (ahead(across_x) - behind(across_x)) * 0.25
    yz = (ahead(across_y) - behind(across_y)) * 0.25
    return xx * yy + xx * zz + yy * zz - xy * xy - xz * xz - yz * yz


def prepare_kernel(potential, core, y_last, y_first, sem):
    copy = pltpu.make_async_copy(potential, core, sem)
    copy.start()
    copy.wait()
    rows_x, rows_y, _ = core.shape
    for x in range(rows_x):
        y_last[x : x + 1, :] = core[x, rows_y - 1 : rows_y, :]
        y_first[x : x + 1, :] = core[x, 0:1, :]


def source_kernel(step, core, y_faces, high, low, table_high, table_low, pad):
    rows_x, rows_y, cells_z = core.shape
    coarse = cells_z // step

    def turns(count, stride):
        row = lax.broadcasted_iota(jnp.int32, (count, cells_z), 0) * stride
        col = lax.broadcasted_iota(jnp.int32, (count, cells_z), 1)
        angle = (row * col % cells_z).astype(F32) * (2.0 * math.pi / cells_z)
        return jnp.cos(angle), jnp.sin(angle)

    wide_cos, wide_sin = turns(coarse, step)
    fine_cos, fine_sin = turns(step, 1)
    fine, turned = fine_cos + fine_sin, fine_cos - fine_sin
    for k in range(coarse):
        rows = slice(k * step, (k + 1) * step)
        value = wide_cos[k : k + 1] * fine + wide_sin[k : k + 1] * turned
        table_high[rows, :], table_low[rows, :] = split(value, 2)
    pad[:, 8 : rows_y + 8, :] = core[...]
    for x in range(rows_x):
        pad[x, 7:8, :] = y_faces[0, x : x + 1, :]
        pad[x, rows_y + 8 : rows_y + 9, :] = y_faces[1, x : x + 1, :]

    @pl.loop(1, rows_x - 1, unroll=3)
    def _(x):
        def at(dx, dy):
            return pad[x + dx, 8 + dy : 8 + dy + rows_y, :]

        rows = pl.ds(pl.multiple_of(x * rows_y, rows_y), rows_y)
        high[rows, :], low[rows, :] = split(source_of(at, cells_z), 2)

    for x in (0, rows_x - 1):
        rows = slice(x * rows_y, (x + 1) * rows_y)
        high[rows, :] = jnp.zeros((rows_y, cells_z), BF16)
        low[rows, :] = jnp.zeros((rows_y, cells_z), BF16)


def spectrum_kernel(core, y_faces, x_faces, inner_high, inner_low, high, low, spectrum, pad, source_high, source_low):
    rows_x, rows_y, cells_z = core.shape
    source_high[...] = inner_high[...]
    source_low[...] = inner_low[...]
    for side in range(2):
        edge = side * (rows_x - 1)
        for line in range(3):
            x = edge + line - 1
            if 0 <= x < rows_x:
                pad[line, 8 : rows_y + 8, :] = core[x]
                pad[line, 7:8, :] = y_faces[0, x : x + 1, :]
                pad[line, rows_y + 8 : rows_y + 9, :] = y_faces[1, x : x + 1, :]
            else:
                pad[line, 7 : rows_y + 9, :] = x_faces[side]

        def at(dx, dy):
            return pad[1 + dx, 8 + dy : 8 + dy + rows_y, :]

        rows = slice(edge * rows_y, (edge + 1) * rows_y)
        source_high[rows, :], source_low[rows, :] = split(source_of(at, cells_z), 2)
    spectrum[...] = dot3((high[...], low[...]), (source_high[...], source_low[...]), NT)


def solve_kernel(
    tiles_x, tiles_y, rows_x, rows_y, scale,
    first, lap_z, slab, labels, lap_xy, hx_high, hx_low, hy_high, hy_low, hf_high, hf_low,
    out, planes, solved_planes, lines, faces,
):
    grid_x, grid_y = tiles_x * rows_x, tiles_y * rows_y
    count = slab.shape[1]
    per = LANES // rows_y
    chunk = rows_x * count

    def stacked(pieces):
        high, low = pieces
        zero = jnp.zeros_like(high)
        return jnp.concatenate(
            [jnp.concatenate([high, low], 1), jnp.concatenate([high, zero], 1)], 0
        )

    def joined(value):
        width = value.shape[1] // 2
        return value[:, :width] + value[:, width:]

    along_y = stacked((hy_high[...], hy_low[...]))
    along_x = jnp.concatenate([hx_high[...], hx_low[...]], 1)
    def times_y(value):
        return joined(dot(jnp.concatenate(split(value, 2), 1), along_y))

    for i in range(tiles_x):
        for part in range(rows_x // per):
            lanes = slice(part * LANES, (part + 1) * LANES)
            found = [[] for _ in range(per)]
            for wide in range(tiles_y // per):
                rows = [slab[i * tiles_y + wide * per + j, :, lanes] for j in range(per)]
                for t, row in enumerate(swap_groups(rows, rows_y)):
                    found[t].append(row)
            x = (i * rows_x + part * per) * count
            block = jnp.concatenate([jnp.concatenate(line, 1) for line in found], 0)
            planes[x : x + per * count, :] = times_y(block)
    for q in range(count):
        rows = pl.ds(q, grid_x, stride=count)
        modes = joined(dot(along_x, stacked(split(planes[rows, :], 2))))
        eigen = lap_xy[...] + lap_z[first[0] + q]
        anchor = eigen == 0.0
        solved = jnp.where(anchor, 0.0, scale / jnp.where(anchor, -1.0, eigen)) * modes
        back = joined(dot(along_x, stacked(split(solved, 2))))
        solved_planes[rows, :] = back
    sides = 2 * tiles_y
    along_f = stacked((hf_high[...], hf_low[...]))
    for i in range(tiles_x):
        rows = slice(i * chunk, (i + 1) * chunk)
        pieces = jnp.concatenate(split(solved_planes[rows, :], 2), 1)
        planes[rows, :] = joined(dot(pieces, along_y))
        lines[rows, :] = joined(dot(pieces, along_f))
    for start in range(0, count, LANES // sides):
        block = None
        for q in range(start, start + LANES // sides):
            item = lines[pl.ds(q, grid_x, stride=count), :]
            item = pltpu.roll(item, (q - start) * sides, 1) if q > start else item
            block = item if block is None else block + item
        faces[start * sides : start * sides + LANES, :] = jnp.transpose(block)

    lane = lax.broadcasted_iota(jnp.int32, (count, LANES), 1)
    for i in range(tiles_x):
        for wide in range(tiles_y // per):
            cols = slice(wide * LANES, (wide + 1) * LANES)

            def row_of(x):
                x = x % grid_x
                return planes[x * count : (x + 1) * count, cols]

            for part in range(rows_x // per):
                lanes = slice(part * LANES, (part + 1) * LANES)
                rows = [row_of(i * rows_x + part * per + t) for t in range(per)]
                for j, row in enumerate(swap_groups(rows, rows_y)):
                    out[i * tiles_y + wide * per + j, :, lanes] = row
            before, after = row_of(i * rows_x - 1), row_of((i + 1) * rows_x)
            for k in range(per):
                j = wide * per + k
                shift = (LANES - k * rows_y) % LANES
                line = pltpu.roll(before, shift, 1) if shift else before
                moved = pltpu.roll(after, (shift + rows_y) % LANES, 1)
                line = jnp.where(lane < rows_y, line, moved)
                for side in range(2):
                    at = side * tiles_y + j
                    face = faces[pl.ds(at, count, stride=sides), :]
                    start = 2 * rows_y + side * rows_x
                    move = (start - i * rows_x) % LANES
                    face = pltpu.roll(face, move, 1) if move else face
                    line = jnp.where(lane < start, line, face)
                at = i * tiles_y + j
                line = jnp.where(lane < 2 * (rows_x + rows_y), line, labels[at : at + 1, :])
                out[i * tiles_y + j, :, rows_x * rows_y : rows_x * rows_y + LANES] = line


def solve_plain(slab, labels, rows_x, rows_y, cells_z, tiles_x, tiles_y, scale):
    high = lax.Precision.HIGHEST
    grid_x, grid_y = tiles_x * rows_x, tiles_y * rows_y
    count = slab.shape[1]
    hx, hy = jnp.asarray(table_of(grid_x)), jnp.asarray(table_of(grid_y))
    planes = slab.reshape(tiles_x, tiles_y, count, rows_x, rows_y).transpose(2, 0, 3, 1, 4)
    planes = planes.reshape(count, grid_x, grid_y)
    modes = jnp.einsum("qxy,xk,yl->qkl", planes, hx, hy, precision=high)
    first = lax.axis_index(("px", "py")) * count
    lap_z = lax.dynamic_slice_in_dim(jnp.asarray(laplace_of(cells_z)), first, count)
    eigen = (
        jnp.asarray(laplace_of(grid_x))[None, :, None]
        + jnp.asarray(laplace_of(grid_y))[None, None, :]
        + lap_z[:, None, None]
    )
    anchor = eigen == 0.0
    solved = jnp.where(anchor, 0.0, scale / jnp.where(anchor, -1.0, eigen)) * modes
    back = jnp.einsum("qkl,xk,yl->qxy", solved, hx, hy, precision=high)
    tiles = back.reshape(count, tiles_x, rows_x, tiles_y, rows_y).transpose(1, 3, 0, 2, 4)
    starts_x, starts_y = np.arange(tiles_x) * rows_x, np.arange(tiles_y) * rows_y
    faces = []
    for edge in (-1, rows_x):
        line = back[:, (starts_x + edge) % grid_x].reshape(count, tiles_x, tiles_y, rows_y)
        faces.append(line.transpose(1, 2, 0, 3))
    for edge in (-1, rows_y):
        line = back[:, :, (starts_y + edge) % grid_y].reshape(count, tiles_x, rows_x, tiles_y)
        faces.append(line.transpose(1, 3, 0, 2))
    tail = labels[:, 2 * (rows_x + rows_y) :].reshape(tiles_x, tiles_y, 1, -1)
    faces.append(jnp.broadcast_to(tail, (tiles_x, tiles_y, count, tail.shape[-1])))
    parts = [tiles.reshape(tiles_x, tiles_y, count, rows_x * rows_y)] + faces
    return jnp.concatenate(parts, -1).reshape(tiles_x * tiles_y, count, -1)


def combine(core, x_faces, y_faces, spectrum, high, low, cells):
    rows_x, rows_y, cells_z = core.shape
    inner = rows_x * rows_y
    cells[...] = dot3(split(spectrum[...], 2), (high[...], low[...]), TN)
    cells[0:inner, :] = cells[0:inner, :] + core[...].reshape(inner, cells_z)
    start = inner
    for faces, skip in ((x_faces, 1), (y_faces, 0)):
        for side in range(2):
            length = faces.shape[1] - 2 * skip
            rows = slice(start, start + length)
            cells[rows, :] = cells[rows, :] + faces[side, skip : skip + length, :]
            start += length
    x_edge = [inner, inner + rows_y]
    y_edge = [inner + 2 * rows_y, inner + 2 * rows_y + rows_x]
    return x_edge, y_edge


def displacement_kernel(core, x_faces, y_faces, spectrum, high, low, displacement, pad, cells):
    rows_x, rows_y, cells_z = core.shape
    x_edge, y_edge = combine(core, x_faces, y_faces, spectrum, high, low, cells)
    for x in range(rows_x):
        pad[x, 8 : rows_y + 8, :] = cells[x * rows_y : (x + 1) * rows_y, :]
        pad[x, 7:8, :] = cells[y_edge[0] + x : y_edge[0] + x + 1, :]
        pad[x, rows_y + 8 : rows_y + 9, :] = cells[y_edge[1] + x : y_edge[1] + x + 1, :]

    def line(x):
        if x < 0:
            return cells[x_edge[0] : x_edge[0] + rows_y, :]
        if x >= rows_x:
            return cells[x_edge[1] : x_edge[1] + rows_y, :]
        return cells[x * rows_y : (x + 1) * rows_y, :]

    for x in range(rows_x):
        here = line(x)
        displacement[0, x] = (line(x - 1) - line(x + 1)) * 0.5
        displacement[1, x] = (pad[x, 7 : rows_y + 7, :] - pad[x, 9 : rows_y + 9, :]) * 0.5
        displacement[2, x] = (pltpu.roll(here, 1, 1) - pltpu.roll(here, cells_z - 1, 1)) * 0.5


def block_kernel(
    planes, half, core, x_faces, y_faces, spectrum, high, low, slots,
    out, values, labels,
    cells, spread,
):
    rows_x, rows_y, cells_z = core.shape
    inner = rows_x * rows_y
    blocks_x, blocks_y, blocks_z = rows_x // 8, rows_y // 8, cells_z // 8
    per = LANES // blocks_z
    x_edge, y_edge = combine(core, x_faces, y_faces, spectrum, high, low, cells)

    width = spread.shape[0] * LANES
    col = lax.broadcasted_iota(jnp.int32, (cells_z, width), 1)
    wanted = (8 * (col % blocks_z) + col // blocks_z + cells_z - 1) % cells_z
    choose = (wanted == lax.broadcasted_iota(jnp.int32, (cells_z, width), 0)).astype(BF16)
    pieces = split(cells[...], 3)
    moved = dot(pieces[0], choose) + dot(pieces[1], choose) + dot(pieces[2], choose)
    for quad in range(spread.shape[0]):
        spread[quad] = moved[:, quad * LANES : (quad + 1) * LANES]

    def put(row, tiles):
        for quad in range(width // LANES):
            every = [tiles(b // blocks_y, b % blocks_y, quad) for b in range(blocks_x * blocks_y)]
            for block in range(0, len(every), per):
                for k, item in enumerate(swap_groups(every[block : block + per], blocks_z)):
                    where = row(quad * per + k - 1)
                    if where is not None:
                        start = block * blocks_z
                        values[where : where + 8, start : start + LANES] = item

    def x_tile(a):
        def tile(bx, by, quad):
            x = 8 * bx + a
            top = x_edge[0] if x < 0 else x_edge[1] if x >= rows_x else x * rows_y
            return spread[quad, top + 8 * by : top + 8 * by + 8, :]

        return tile

    for a in range(-1, 9):
        def row(e, a=a):
            if 0 <= e < 8:
                return ((a + 1) * 8 + e) * 8
            if e in (-1, 8) and 0 <= a < 8:
                return 640 + (64 if e == 8 else 0) + a * 8
            return None

        put(row, x_tile(a))
    for side, edge in enumerate((-1, 8)):
        def tile(bx, by, quad, edge=edge):
            y = 8 * by + edge
            if y < 0 or y >= rows_y:
                top = y_edge[0 if y < 0 else 1] + 8 * bx
                return spread[quad, top : top + 8, :]
            return spread[quad, pl.ds(8 * bx * rows_y + y, 8, stride=rows_y), :]

        put(lambda e, side=side: 768 + side * 64 + e * 8 if 0 <= e < 8 else None, tile)

    count = slots.shape[1]
    named = spectrum[:, inner : inner + LANES].astype(BF16)
    row = lax.broadcasted_iota(jnp.int32, (cells_z, count), 0)
    slot = lax.broadcasted_iota(jnp.int32, (cells_z, count), 1)
    source = (row % planes == 0) & (row // planes == slot // half)
    by_lane = dot(named, source.astype(BF16), TN)
    lane = lax.broadcasted_iota(jnp.int32, (LANES, count), 0) - 2 * (rows_x + rows_y)
    place = lax.broadcasted_iota(jnp.int32, (LANES, count), 1) % half
    for part in range(2):
        label = jnp.sum(jnp.where(lane == place + part * half, by_lane, 0.0), axis=0, keepdims=True)
        labels[part] = label.astype(jnp.int32)

    fill_slots(0, values, slots, out)


def fill_slots(part, values, slots, out):
    count = slots.shape[1]
    pieces = split(values[...], 3)
    number = lax.broadcasted_iota(jnp.int32, (count, count), 0) + part * count
    chosen = (slots[...] == number).astype(BF16)
    out[...] = dot(chosen, pieces[0], NT) + dot(chosen, pieces[1], NT) + dot(chosen, pieces[2], NT)


def spline(shift):
    g = jnp.abs(shift)
    h = 1.0 - g
    gg, hh = g * g, h * h
    near = (2.0 / 3.0) - gg + 0.5 * gg * g
    ahead = (2.0 / 3.0) - hh + 0.5 * hh * h
    back = hh * h * (1.0 / 6.0)
    far = gg * g * (1.0 / 6.0)
    up = shift >= 0.0
    zero = jnp.zeros_like(far)
    return (
        jnp.where(up, zero, far),
        jnp.where(up, back, ahead),
        near,
        jnp.where(up, ahead, back),
        jnp.where(up, far, zero),
    )


def deposit_kernel(blocks_x, blocks_y, blocks_z, last, blocks, labels, *refs):
    if last:
        before, core, x_rims, y_rims, turned, weights, pieces, grouped, tile = refs
    else:
        core, turned, weights, pieces, grouped, tile = refs
    slots = blocks.shape[0]
    cells_z = 8 * blocks_z
    per = LANES // blocks_z
    windows = blocks_x * blocks_y * blocks_z
    sub = lax.broadcasted_iota(jnp.int32, (8, LANES), 0)
    for g in range(slots // LANES):
        turned[g] = jnp.transpose(blocks[g * LANES : (g + 1) * LANES, :])

    @pl.loop(0, slots // LANES)
    def _(g):
        def rows(start):
            return turned[g, pl.ds(pl.multiple_of(start, 8), 8), :]

        @pl.loop(0, 8)
        def _(a):
            for e in range(8):
                here = rows((a + 1) * 64 + e * 8)
                x_diff = rows(a * 64 + e * 8) - rows((a + 2) * 64 + e * 8)
                z_low = rows((a + 1) * 64 + e * 8 - 8) if e > 0 else rows(640 + a * 8)
                z_top = rows((a + 1) * 64 + e * 8 + 8) if e < 7 else rows(704 + a * 8)
                y_low = jnp.where(
                    sub == 0, turned[g, pl.ds(768 + e * 8 + a, 1), :], pltpu.roll(here, 1, 0)
                )
                y_top = jnp.where(
                    sub == 7, turned[g, pl.ds(832 + e * 8 + a, 1), :], pltpu.roll(here, 7, 0)
                )
                for axis, diff in enumerate((x_diff, y_low - y_top, z_low - z_top)):
                    for k, weight in enumerate(spline(jnp.clip(diff * 0.5, -1.0, 1.0))):
                        if (axis, k) != (1, 2):
                            weights[axis * 5 + k, a * 8 + e] = weight

        top_lanes = pl.ds(pl.multiple_of(g * LANES, LANES), LANES)
        rest_lanes = pl.ds(pl.multiple_of(slots + g * LANES, LANES), LANES)

        def cell_row(s, depths):
            sums = {}
            for a in range(8):
                for k in depths:
                    at = a * 8 + (s - k)
                    w_z = weights[10 + k, at]
                    w_y = [weights[5 + j, at] if j != 2 else None for j in range(5)]
                    for i in range(5):
                        plane = weights[i, at] * w_z
                        for j in range(5):
                            key = (a + i, j)
                            term = plane * w_y[j] if j != 2 else plane
                            sums[key] = sums[key] + term if key in sums else term
                for u in [a] if a < 7 else range(7, 12):
                    rows = [sums[u, j] for j in range(5)]
                    rows[2] = rows[2] - ((rows[0] + rows[1]) + (rows[3] + rows[4]))
                    moved = [pltpu.roll(rows[j], j, 0) for j in range(1, 5)]
                    every = rows[0] + ((moved[0] + moved[1]) + (moved[2] + moved[3]))
                    past = [jnp.where(sub < j + 1, moved[j], 0.0) for j in range(4)]
                    tail = (past[0] + past[1]) + (past[2] + past[3])
                    top, rest = split(jnp.concatenate([every - tail, tail], 0), 2)
                    out = pl.ds(pl.multiple_of((s * 12 + u) * 16, 16), 16)
                    pieces[out, top_lanes] = top
                    pieces[out, rest_lanes] = rest

        for s in (0, 1, 2, 3, 8, 9, 10, 11):
            cell_row(s, [k for k in range(5) if 0 <= s - k < 8])

        @pl.loop(4, 8)
        def _(s):
            cell_row(s, range(5))

    named = (labels[...] == lax.broadcasted_iota(jnp.int32, (windows, slots), 0)).astype(F32)
    named = jnp.transpose(named).astype(BF16)
    area = 12 * 16
    named = jnp.concatenate([named, named], 0)

    @pl.loop(0, 12 // per)
    def _(quad):
        rows = pl.ds(pl.multiple_of(quad * per * area, 16), per * area)
        summed = dot(pieces[rows, :], named)
        for wide in range(windows // LANES):
            lanes = slice(wide * LANES, (wide + 1) * LANES)
            part = [summed[k * area : (k + 1) * area, lanes] for k in range(per)]
            for t, item in enumerate(swap_groups(part, blocks_z)):
                rows = slice((wide * per + t) * area, (wide * per + t + 1) * area)
                grouped[0, quad, rows, :], grouped[1, quad, rows, :] = split(item, 2)

    depth = 12 * blocks_z
    row = lax.broadcasted_iota(jnp.int32, (depth, cells_z), 0)
    wanted = (8 * (row % blocks_z) + row // blocks_z + cells_z - 2) % cells_z
    place = (wanted == lax.broadcasted_iota(jnp.int32, (depth, cells_z), 1)).astype(BF16)
    tile[...] = before[...] if last else jnp.zeros_like(tile)
    quads = depth // LANES
    left = jnp.concatenate([grouped[piece, quad] for piece in range(2) for quad in range(quads)], 1)
    total = dot(left, jnp.concatenate([place, place], 0))
    for bx in range(blocks_x):
        for by in range(blocks_y):
            at = (bx * blocks_y + by) * area
            rows = slice(bx * 8, bx * 8 + 12)
            cols = slice(by * 8, by * 8 + 16)
            tile[rows, cols, :] = tile[rows, cols, :] + total[at : at + area].reshape(12, 16, cells_z)

    if not last:
        core[...] = tile[...]
        return
    rows_x, rows_y = 8 * blocks_x, 8 * blocks_y
    core[...] = tile[2 : rows_x + 2, 2 : rows_y + 2, :]
    for side in range(2):
        x = side * (rows_x + 2)
        y = side * (rows_y + 2)
        x_rims[side] = tile[x : x + 2, 2 : rows_y + 2, :]
        y_rims[side] = tile[:, y : y + 2, :]


def corner_kernel(x_rims, y_low, y_top, out):
    rows_x, rows_y = y_low.shape[0] - 4, x_rims.shape[2]
    for side in range(2):
        x = side * (rows_x + 2)
        out[side] = x_rims[side]
        out[side, :, 0:2, :] = out[side, :, 0:2, :] + y_low[x : x + 2]
        out[side, :, rows_y - 2 :, :] = out[side, :, rows_y - 2 :, :] + y_top[x : x + 2]


def rim_kernel(core, y_low, y_top, x_low, x_top, out):
    rows_x, rows_y, _ = core.shape
    out[...] = core[...]
    for part, face in ((slice(0, 2), y_low), (slice(rows_y - 2, rows_y), y_top)):
        out[:, part, :] = out[:, part, :] + face[2 : rows_x + 2]
    for part, face in ((slice(0, 2), x_low), (slice(rows_x - 2, rows_x), x_top)):
        out[part] = out[part] + face[...]


def per_device(potential, owner, window):
    rows_x, rows_y, cells_z = potential.shape
    tiles_x, tiles_y = lax.axis_size("px"), lax.axis_size("py")
    tiles = tiles_x * tiles_y
    grid_x, grid_y = rows_x * tiles_x, rows_y * tiles_y
    planes = cells_z // tiles
    inner = rows_x * rows_y
    used = inner + -(-2 * (rows_x + rows_y) // LANES) * LANES
    blocks_x, blocks_y, blocks_z = rows_x // 8, rows_y // 8, cells_z // 8
    blocks = blocks_x * blocks_y * blocks_z
    half = max(2, 2 * blocks // tiles) // 2
    both = ("px", "py")

    def exchange(x):
        return lax.all_to_all(x, both, split_axis=0, concat_axis=0, tiled=True)

    slots, labels = call(
        functools.partial(slot_kernel, half, 2 * (rows_x + rows_y)),
        (shape(1, blocks, dtype=jnp.int32), shape(tiles, LANES)),
        [], 8, 2 * tiles * LANES * blocks, 8 * blocks,
    )(owner.reshape(blocks, 1), owner.reshape(1, blocks), window.reshape(1, blocks))

    line = shape(rows_x, cells_z)
    core, y_last, y_first = pl.pallas_call(
        prepare_kernel,
        out_shape=(shape(rows_x, rows_y, cells_z), line, line),
        in_specs=[FAR],
        out_specs=[VMEM] * 3,
        scratch_shapes=[pltpu.SemaphoreType.DMA],
        compiler_params=pltpu.CompilerParams(vmem_limit_bytes=8 << 20),
        cost_estimate=pl.CostEstimate(flops=0, bytes_accessed=2 << 20, transcendentals=0),
    )(potential)
    last_x = rows_x - 1
    y_faces = jnp.stack([send(y_last, "py", 1), send(y_first, "py", -1)])
    x_lines = [
        jnp.concatenate([y_faces[0, x : x + 1], core[x], y_faces[1, x : x + 1]])
        for x in (last_x, 0)
    ]
    x_faces = jnp.stack([send(x_lines[0], "px", 1), send(x_lines[1], "px", -1)])

    halves = shape(inner, cells_z, dtype=BF16)
    table = shape(cells_z, cells_z, dtype=BF16)
    step = 16
    *source, z_high, z_low = call(
        functools.partial(source_kernel, step), (halves, halves, table, table),
        [pltpu.VMEM((rows_x, rows_y + 16, cells_z), F32)],
        8, 60 * inner * cells_z, 2 << 20,
    )(core, y_faces)
    spectrum = call(
        spectrum_kernel, shape(cells_z, inner),
        [pltpu.VMEM((3, rows_y + 16, cells_z), F32)] + [pltpu.VMEM((inner, cells_z), BF16)] * 2,
        12, 6 * inner * cells_z**2, 2 << 20,
    )(core, y_faces, x_faces, *source, z_high, z_low)
    slab = exchange(spectrum).reshape(tiles, planes, inner)

    scale = SECOND_ORDER / (grid_x * grid_y * cells_z)
    if planes % 8 == 0 and tiles_y % (LANES // rows_y) == 0 and grid_x == LANES and 2 * tiles_y <= LANES and planes % (LANES // (2 * tiles_y)) == 0:
        first = (lax.axis_index(both) * planes).astype(jnp.int32).reshape(1)
        x_table, y_table = table_of(grid_x), table_of(grid_y)
        starts = np.arange(tiles_y) * rows_y
        edge = np.concatenate([(starts - 1) % grid_y, (starts + rows_y) % grid_y])
        lap_xy = laplace_of(grid_x)[:, None] + laplace_of(grid_y)[None, :]
        face_table = np.zeros((grid_y, LANES), np.float32)
        face_table[:, : 2 * tiles_y] = y_table[edge].T
        tables = pieces_of(x_table) + pieces_of(y_table) + pieces_of(face_table)
        body = functools.partial(solve_kernel, tiles_x, tiles_y, rows_x, rows_y, scale)
        specs = [SMEM, SMEM] + [VMEM] * 9
        returned = pl.pallas_call(
            body,
            out_shape=shape(tiles, planes, used),
            in_specs=specs,
            out_specs=VMEM,
            scratch_shapes=[
                pltpu.VMEM((grid_x * planes, grid_y), F32),
                pltpu.VMEM((grid_x * planes, grid_y), F32),
                pltpu.VMEM((grid_x * planes, LANES), F32),
                pltpu.VMEM((2 * tiles_y * planes, grid_x), F32),
            ],
            compiler_params=pltpu.CompilerParams(vmem_limit_bytes=16 << 20),
            cost_estimate=pl.CostEstimate(
                flops=24 * planes * grid_x**2 * grid_y, bytes_accessed=2 << 20, transcendentals=0
            ),
        )(first, laplace_of(cells_z), slab, labels, lap_xy, *tables)
    else:
        returned = solve_plain(slab, labels, rows_x, rows_y, cells_z, tiles_x, tiles_y, scale)
    modes = exchange(returned.reshape(cells_z, used))

    width = -(-10 * blocks_z // LANES) * LANES
    cells = pltpu.VMEM((used, cells_z), F32)
    tile_args = (core, x_faces, y_faces, modes, z_high, z_low)
    half_out = shape(blocks, ROWS)
    sent, values, arrived_labels = call(
        functools.partial(block_kernel, planes, half),
        (half_out, shape(ROWS, blocks), shape(2, 1, blocks, dtype=jnp.int32)),
        [cells, pltpu.VMEM((width // LANES, used, LANES), F32)],
        40, 20 * used * cells_z**2, 6 << 20,
    )(*tile_args, slots)
    first = exchange(sent)
    later = call(functools.partial(fill_slots, 1), half_out, [], 16, 6 * ROWS * blocks**2, 4 << 20)(values, slots)
    displacement = call(
        displacement_kernel, shape(3, rows_x, rows_y, cells_z),
        [pltpu.VMEM((rows_x, rows_y + 16, cells_z), F32), cells],
        16, 6 * used * cells_z**2, 4 << 20,
    )(*tile_args)

    later, displacement = lax.optimization_barrier((later, displacement))
    arrived = first, exchange(later)
    tile_shape = (rows_x + 4, rows_y + 8, cells_z)
    scratch = [
        pltpu.VMEM((blocks // LANES, ROWS, LANES), F32),
        pltpu.VMEM((15, 64, 8, LANES), F32),
        pltpu.VMEM((12 * 12 * 16, 2 * blocks), BF16),
        pltpu.VMEM((2, 12 * blocks_z // LANES, blocks_x * blocks_y * 12 * 16, LANES), BF16),
        pltpu.VMEM(tile_shape, F32),
    ]
    sizes = (blocks_x, blocks_y, blocks_z)
    cost = (300 * blocks * 512, 4 << 20)
    tile = call(
        functools.partial(deposit_kernel, *sizes, False), shape(*tile_shape), scratch, 32, *cost
    )(arrived[0], arrived_labels[0])
    middle, x_rims, y_rims = call(
        functools.partial(deposit_kernel, *sizes, True),
        (
            shape(rows_x, rows_y, cells_z), shape(2, 2, rows_y, cells_z),
            shape(2, rows_x + 4, 2, cells_z),
        ),
        scratch, 32, *cost,
    )(arrived[1], arrived_labels[1], tile)

    y_sides = send(y_rims[1], "py", 1), send(y_rims[0], "py", -1)
    x_rims = call(corner_kernel, shape(*x_rims.shape), [], 4, 8 * rows_y * cells_z, 1 << 17)(
        x_rims, *y_sides
    )
    x_sides = send(x_rims[1], "px", 1), send(x_rims[0], "px", -1)
    density = call(rim_kernel, shape(rows_x, rows_y, cells_z), [], 8, inner * cells_z, 2 << 20)(
        middle, *y_sides, *x_sides
    )
    return (displacement, density)


def solution(mesh):
    return jax.shard_map(
        per_device,
        mesh=mesh,
        in_specs=(P("px", "py", None), P("px", "py", None, None), P("px", "py", None)),
        out_specs=(P(None, "px", "py", None), P("px", "py", None)),
        check_vma=False,
    )
```

```python
import functools
import math

import jax
import jax.numpy as jnp
import numpy as np
from jax import lax
from jax.experimental import pallas as pl
from jax.experimental.pallas import tpu as pltpu
from jax.sharding import PartitionSpec as P

SECOND_ORDER = 3.0 / 7.0
F32 = jnp.float32
BF16 = jnp.bfloat16
LANES = 128
ROWS = 896
VMEM = pl.BlockSpec(memory_space=pltpu.VMEM)
SMEM = pl.BlockSpec(memory_space=pltpu.SMEM)
FAR = pl.BlockSpec(memory_space=pltpu.HBM)
NN = (((1,), (0,)), ((), ()))
NT = (((1,), (1,)), ((), ()))
TN = (((0,), (0,)), ((), ()))


def split(x, pieces):
    out = []
    for piece in range(pieces):
        part = x.astype(BF16)
        out.append(part)
        if piece < pieces - 1:
            x = x - part.astype(F32)
    return out


def dot(a, b, dims=NN):
    return lax.dot_general(a, b, dims, preferred_element_type=F32)


def dot3(a, b, dims=NN):
    return dot(a[0], b[0], dims) + (dot(a[0], b[1], dims) + dot(a[1], b[0], dims))


def swap_groups(rows, group):
    rows = list(rows)
    count = len(rows)
    axis = rows[0].ndim - 1
    lane = lax.broadcasted_iota(jnp.int32, rows[0].shape, axis) // group
    step = 1
    while step < count:
        low = (lane & step) == 0
        for k in range(count):
            if k & step:
                continue
            a, b = rows[k], rows[k + step]
            rows[k] = jnp.where(low, a, pltpu.roll(b, step * group, axis))
            rows[k + step] = jnp.where(low, pltpu.roll(a, LANES - step * group, axis), b)
        step *= 2
    return rows


def table_of(length):
    modes = np.arange(length)
    angle = (modes[:, None] * modes[None, :] % length) * (2.0 * math.pi / length)
    return (np.cos(angle) + np.sin(angle)).astype(np.float32)


def pieces_of(table):
    high = table.astype(jnp.bfloat16)
    low = (table - high.astype(np.float32)).astype(jnp.bfloat16)
    return np.asarray(high), np.asarray(low)


def laplace_of(length):
    return (2.0 * np.cos(np.arange(length) * (2.0 * math.pi / length)) - 2.0).astype(np.float32)


def call(body, outs, scratch, vmem, flops, moved, scalars=0):
    def run(*operands):
        return pl.pallas_call(
            body,
            out_shape=outs,
            in_specs=[SMEM] * scalars + [VMEM] * (len(operands) - scalars),
            out_specs=jax.tree.map(lambda _: VMEM, outs),
            scratch_shapes=scratch,
            compiler_params=pltpu.CompilerParams(vmem_limit_bytes=vmem << 20),
            cost_estimate=pl.CostEstimate(flops=flops, bytes_accessed=moved, transcendentals=0),
        )(*operands)

    return run


def shape(*dims, dtype=F32):
    return jax.ShapeDtypeStruct(dims, dtype)


def send(x, axis, step):
    size = lax.axis_size(axis)
    return lax.ppermute(x, axis, [(i, (i + step) % size) for i in range(size)])


def slot_kernel(half, start, owner_col, owner_row, window_row, slot_out, label_out):
    count = owner_row.shape[1]
    tiles = label_out.shape[0]
    later = lax.broadcasted_iota(jnp.int32, (count, count), 0) < lax.broadcasted_iota(
        jnp.int32, (count, count), 1
    )
    owners = owner_row[...]
    same = (owner_col[...] == owners) & later
    rank = jnp.sum(same.astype(F32), axis=0, keepdims=True).astype(jnp.int32)
    second = rank >= half
    place = owners * half + jnp.where(second, rank - half, rank)
    slot_out[...] = jnp.where(second, place + count, place)
    tile = lax.broadcasted_iota(jnp.int32, (tiles, count), 0)
    named = jnp.where(tile == owners, window_row[...] + 1, 0).astype(F32).astype(BF16)
    lane = lax.broadcasted_iota(jnp.int32, (LANES, count), 0)
    label_out[...] = dot(named, (lane == rank + start).astype(BF16), NT) - 1.0


def source_of(at, cells_z):
    def ahead(value):
        return pltpu.roll(value, cells_z - 1, 1)

    def behind(value):
        return pltpu.roll(value, 1, 1)

    here = at(0, 0)
    ahead_x, behind_x, ahead_y, behind_y = at(1, 0), at(-1, 0), at(0, 1), at(0, -1)
    xx = ahead_x - 2.0 * here + behind_x
    yy = ahead_y - 2.0 * here + behind_y
    zz = ahead(here) - 2.0 * here + behind(here)
    xy = (at(1, 1) - at(1, -1) - at(-1, 1) + at(-1, -1)) * 0.25
    across_x, across_y = ahead_x - behind_x, ahead_y - behind_y
    xz = (ahead(across_x) - behind(across_x)) * 0.25
    yz = (ahead(across_y) - behind(across_y)) * 0.25
    return xx * yy + xx * zz + yy * zz - xy * xy - xz * xz - yz * yz


def prepare_kernel(potential, core, y_last, y_first, sem):
    copy = pltpu.make_async_copy(potential, core, sem)
    copy.start()
    copy.wait()
    rows_x, rows_y, _ = core.shape
    for x in range(rows_x):
        y_last[x : x + 1, :] = core[x, rows_y - 1 : rows_y, :]
        y_first[x : x + 1, :] = core[x, 0:1, :]


def source_kernel(step, core, y_faces, high, low, table_high, table_low, pad):
    rows_x, rows_y, cells_z = core.shape
    coarse = cells_z // step

    def turns(count, stride):
        row = lax.broadcasted_iota(jnp.int32, (count, cells_z), 0) * stride
        col = lax.broadcasted_iota(jnp.int32, (count, cells_z), 1)
        angle = (row * col % cells_z).astype(F32) * (2.0 * math.pi / cells_z)
        return jnp.cos(angle), jnp.sin(angle)

    wide_cos, wide_sin = turns(coarse, step)
    fine_cos, fine_sin = turns(step, 1)
    fine, turned = fine_cos + fine_sin, fine_cos - fine_sin
    for k in range(coarse):
        rows = slice(k * step, (k + 1) * step)
        value = wide_cos[k : k + 1] * fine + wide_sin[k : k + 1] * turned
        table_high[rows, :], table_low[rows, :] = split(value, 2)
    pad[:, 8 : rows_y + 8, :] = core[...]
    for x in range(rows_x):
        pad[x, 7:8, :] = y_faces[0, x : x + 1, :]
        pad[x, rows_y + 8 : rows_y + 9, :] = y_faces[1, x : x + 1, :]

    @pl.loop(1, rows_x - 1, unroll=3)
    def _(x):
        def at(dx, dy):
            return pad[x + dx, 8 + dy : 8 + dy + rows_y, :]

        rows = pl.ds(pl.multiple_of(x * rows_y, rows_y), rows_y)
        high[rows, :], low[rows, :] = split(source_of(at, cells_z), 2)

    for x in (0, rows_x - 1):
        rows = slice(x * rows_y, (x + 1) * rows_y)
        high[rows, :] = jnp.zeros((rows_y, cells_z), BF16)
        low[rows, :] = jnp.zeros((rows_y, cells_z), BF16)


def spectrum_kernel(core, y_faces, x_faces, inner_high, inner_low, high, low, spectrum, pad, source_high, source_low):
    rows_x, rows_y, cells_z = core.shape
    source_high[...] = inner_high[...]
    source_low[...] = inner_low[...]
    for side in range(2):
        edge = side * (rows_x - 1)
        for line in range(3):
            x = edge + line - 1
            if 0 <= x < rows_x:
                pad[line, 8 : rows_y + 8, :] = core[x]
                pad[line, 7:8, :] = y_faces[0, x : x + 1, :]
                pad[line, rows_y + 8 : rows_y + 9, :] = y_faces[1, x : x + 1, :]
            else:
                pad[line, 7 : rows_y + 9, :] = x_faces[side]

        def at(dx, dy):
            return pad[1 + dx, 8 + dy : 8 + dy + rows_y, :]

        rows = slice(edge * rows_y, (edge + 1) * rows_y)
        source_high[rows, :], source_low[rows, :] = split(source_of(at, cells_z), 2)
    spectrum[...] = dot3((high[...], low[...]), (source_high[...], source_low[...]), NT)


def stacked(pieces):
    high, low = pieces
    return jnp.concatenate(
        [jnp.concatenate([high, low], 1), jnp.concatenate([high, jnp.zeros_like(high)], 1)], 0
    )


def joined(value):
    width = value.shape[1] // 2
    return value[:, :width] + value[:, width:]


def placed(pieces, choose):
    return dot(pieces[0], choose) + dot(pieces[1], choose) + dot(pieces[2], choose)


def iota(dims, axis):
    return lax.broadcasted_iota(jnp.int32, dims, axis)


def decay(w, length):
    grow = w + jnp.sqrt(w * (w + 2.0))
    rate = jnp.log(1.0 + grow)
    ratio = 1.0 / (1.0 + grow)
    both = (1.0 + grow) + jnp.exp(-rate * (length - 1.0))
    flat = w <= 0.0
    return rate, 2.0 * (1.0 + ratio) * both, 2.0 * jnp.where(flat, 1.0, grow * ratio * both), flat


def decay_kernel(length, first, lap_z, lap_x, even, odd, edge_even, edge_odd, spread):
    count = even.shape[0]
    dims = even.shape[1:]
    lane = iota(dims, 1)
    group = lane // length
    y = (lane % length).astype(F32)
    start = first[0]
    for q in range(count):
        along_z = jnp.where(group == 0, lap_z[start + q], lap_z[start + count + q])
        rate, plus, minus, flat = decay(-0.5 * (lap_x[...] + along_z), length)
        rise, fall = jnp.exp(-rate * y), jnp.exp(-rate * (length - 1.0 - y))
        even[q] = (rise + fall) / plus
        odd[q] = jnp.where(flat, 0.25 * (length - 1.0) - 0.5 * y, (rise - fall) / minus)
    along_z = jnp.zeros(dims, F32)
    for q in range(count):
        for g in range(2):
            along_z = jnp.where(lane // 2 == 2 * q + g, lap_z[start + g * count + q], along_z)
    rate, plus, minus, flat = decay(-0.5 * (lap_x[...] + along_z), length)
    last = jnp.exp(-rate * (length - 1.0))
    edge_even[...] = (1.0 + last) / plus
    edge_odd[...] = jnp.where(flat, 0.25 * (length - 1.0), (1.0 - last) / minus)
    dims = spread.shape
    col = iota(dims, 1)
    row = iota(dims, 0)
    hit = row // 2 == 2 * (col // (2 * LANES)) + col % LANES // length
    sign = jnp.where((col // LANES % 2 == 1) & (row % 2 == 0), -1.0, 1.0)
    spread[...] = jnp.where(hit, sign, 0.0).astype(BF16)


def half_kernel(
    tiles_x, tiles_y, rows_x, rows_y, scale, mark,
    first, lap_z, slab, labels, lap_xy, hx_high, hx_low, hy_high, hy_low,
    found, ends, planes,
):
    grid_x = tiles_x * rows_x
    count = slab.shape[1] // 2
    length = tiles_y * rows_y
    per = LANES // rows_y
    along_y = stacked((hy_high[...], hy_low[...]))
    along_x = jnp.concatenate([hx_high[...], hx_low[...]], 1)

    def times_y(value):
        return joined(dot(jnp.concatenate(split(value, 2), 1), along_y))

    for i in range(tiles_x):
        for part in range(rows_x // per):
            lanes = slice(part * LANES, (part + 1) * LANES)
            rows = [
                slab[i * tiles_y + j, g * count : (g + 1) * count, lanes]
                for g in range(2)
                for j in range(tiles_y)
            ]
            x = (i * rows_x + part * per) * count
            planes[x : x + per * count, :] = times_y(jnp.concatenate(swap_groups(rows, rows_y), 0))
    dims = (grid_x, LANES)
    lane, row = iota(dims, 1), iota(dims, 0)
    block = jnp.zeros(dims, F32)
    for q in range(count):
        modes = joined(dot(along_x, stacked(split(planes[pl.ds(q, grid_x, stride=count), :], 2))))
        eigen = lap_xy[...] + jnp.where(lane < length, lap_z[first[0] + q], lap_z[first[0] + count + q])
        anchor = eigen == 0.0
        value = times_y(jnp.where(anchor, 0.0, scale / jnp.where(anchor, -1.0, eigen)) * modes)
        found[q] = value
        source = lane - 4 * q
        source = source // 2 * length + source % 2 * (length - 1)
        choose = (row == source) & (lane >= 4 * q) & (lane < 4 * q + 4)
        block = block + placed(split(value, 3), choose.astype(BF16))
        if q == 0:
            mean = pltpu.roll(modes * scale, 4 * count, 1)
            block = block + jnp.where((row == 0) & (lane == 4 * count), mean, 0.0)
    ends[...] = block
    tiles = labels.shape[0]
    ends[0:tiles, :] = jnp.where(lane[0:tiles] < mark, block[0:tiles], labels[...])


def join_kernel(
    tiles_x, tiles_y, rows_x, rows_y, places,
    first, half, found, ends, arrived, labels, even, odd, edge_even, edge_odd, spread, hx_high, hx_low,
    out, planes, faces,
):
    grid_x = tiles_x * rows_x
    count = found.shape[0]
    length = tiles_y * rows_y
    per = LANES // rows_y
    along_x = jnp.concatenate([hx_high[...], hx_low[...]], 1)

    def times_x(value):
        return joined(dot(along_x, stacked(split(value, 2))))

    dims = (grid_x, LANES)
    lane, row = iota(dims, 1), iota(dims, 0)
    jump = jnp.where(lane < 4 * count + 1, arrived[...] - ends[...], 0.0)
    pieces = split(jump, 2)
    wide = dot(pieces[0], spread[...]) + dot(pieces[1], spread[...])
    mean = jnp.where(first[0] == 0, -0.5 * jump[0:1, 4 * count : 4 * count + 1], 0.0)
    y = lane.astype(F32)
    bend = jnp.where(
        (row == 0) & (lane < length),
        mean * (0.5 * y * y - 0.5 * (length - 1.0) * y - 0.25 * length),
        0.0,
    )
    target = iota((LANES, LANES), 1)
    source = iota((LANES, LANES), 0)
    side, j, group = target // 8 % 2, target // 2 % tiles_y, target % 2
    inside = ((side == 0) & (j > 0)) | ((side == 1) & (j < tiles_y - 1))
    wanted = group * length + jnp.where(side == 0, j * rows_y - 1, (j + 1) * rows_y)
    lines = jnp.zeros(dims, F32)
    for q in range(count):
        at = 2 * q * LANES
        value = found[q] + (wide[:, at : at + LANES] * even[q] + wide[:, at + LANES : at + 2 * LANES] * odd[q])
        if q == 0:
            value = value + bend
        choose = inside & (source == wanted) & (target // 16 == q)
        lines = lines + placed(split(value, 3), choose.astype(BF16))
        planes[pl.ds(q, grid_x, stride=count), :] = times_x(value)
    low = lane % 2 == 0
    other = jnp.where(low, pltpu.roll(jump, LANES - 1, 1), pltpu.roll(jump, 1, 1))
    change = (jump + other) * edge_even[...] + (other - jump) * edge_odd[...]
    change = change + jnp.where((row == 0) & (lane < 2), -0.25 * length * mean, 0.0)
    beyond = jnp.where(lane < 4 * count, arrived[...] - change, 0.0)
    first_side = source % 2 == 1
    goal = source // 4 * 16 + source // 2 % 2 + jnp.where(first_side, 0, 8 + 2 * (tiles_y - 1))
    choose = (target == goal) & (source < 4 * count)
    lines = lines + placed(split(beyond, 3), choose.astype(BF16))
    faces[...] = jnp.transpose(times_x(lines))

    def row_of(x):
        x = x % grid_x
        return planes[x * count : (x + 1) * count, :]

    lane = iota((count, LANES), 1)
    for i in range(tiles_x):
        for part in range(rows_x // per):
            lanes = slice(part * LANES, (part + 1) * LANES)
            rows = [row_of(i * rows_x + part * per + t) for t in range(per)]
            for k, item in enumerate(swap_groups(rows, rows_y)):
                g, j = k // tiles_y, k % tiles_y
                out[i * tiles_y + j, g * count : (g + 1) * count, lanes] = item
        before, after = row_of(i * rows_x - 1), row_of((i + 1) * rows_x)
        for k in range(per):
            g, j = k // tiles_y, k % tiles_y
            shift = (LANES - k * rows_y) % LANES
            line = pltpu.roll(before, shift, 1) if shift else before
            moved = pltpu.roll(after, (shift + rows_y) % LANES, 1)
            line = jnp.where(lane < rows_y, line, moved)
            for side in range(2):
                face = faces[pl.ds(side * 8 + j * 2 + g, count, stride=16), :]
                start = 2 * rows_y + side * rows_x
                move = (start - i * rows_x) % LANES
                face = pltpu.roll(face, move, 1) if move else face
                line = jnp.where(lane < start, line, face)
            start = 2 * (rows_x + rows_y)
            tile = (2 * i + half[0]) * tiles_y + j
            own, partner = labels[pl.ds(tile, 1), :], pltpu.roll(arrived[pl.ds(tile, 1), :], places, 1)
            line = jnp.where(lane < start, line, jnp.where(lane < start + places, own, partner))
            out[i * tiles_y + j, g * count : (g + 1) * count, rows_x * rows_y : rows_x * rows_y + LANES] = line


def solve_plain(slab, labels, rows_x, rows_y, cells_z, tiles_x, tiles_y, scale):
    high = lax.Precision.HIGHEST
    grid_x, grid_y = tiles_x * rows_x, tiles_y * rows_y
    count = slab.shape[1]
    hx, hy = jnp.asarray(table_of(grid_x)), jnp.asarray(table_of(grid_y))
    planes = slab.reshape(tiles_x, tiles_y, count, rows_x, rows_y).transpose(2, 0, 3, 1, 4)
    planes = planes.reshape(count, grid_x, grid_y)
    modes = jnp.einsum("qxy,xk,yl->qkl", planes, hx, hy, precision=high)
    first = lax.axis_index(("px", "py")) * count
    lap_z = lax.dynamic_slice_in_dim(jnp.asarray(laplace_of(cells_z)), first, count)
    eigen = (
        jnp.asarray(laplace_of(grid_x))[None, :, None]
        + jnp.asarray(laplace_of(grid_y))[None, None, :]
        + lap_z[:, None, None]
    )
    anchor = eigen == 0.0
    solved = jnp.where(anchor, 0.0, scale / jnp.where(anchor, -1.0, eigen)) * modes
    back = jnp.einsum("qkl,xk,yl->qxy", solved, hx, hy, precision=high)
    tiles = back.reshape(count, tiles_x, rows_x, tiles_y, rows_y).transpose(1, 3, 0, 2, 4)
    starts_x, starts_y = np.arange(tiles_x) * rows_x, np.arange(tiles_y) * rows_y
    faces = []
    for edge in (-1, rows_x):
        line = back[:, (starts_x + edge) % grid_x].reshape(count, tiles_x, tiles_y, rows_y)
        faces.append(line.transpose(1, 2, 0, 3))
    for edge in (-1, rows_y):
        line = back[:, :, (starts_y + edge) % grid_y].reshape(count, tiles_x, rows_x, tiles_y)
        faces.append(line.transpose(1, 3, 0, 2))
    tail = labels[:, 2 * (rows_x + rows_y) :].reshape(tiles_x, tiles_y, 1, -1)
    faces.append(jnp.broadcast_to(tail, (tiles_x, tiles_y, count, tail.shape[-1])))
    parts = [tiles.reshape(tiles_x, tiles_y, count, rows_x * rows_y)] + faces
    return jnp.concatenate(parts, -1).reshape(tiles_x * tiles_y, count, -1)


def combine(core, x_faces, y_faces, spectrum, high, low, cells):
    rows_x, rows_y, cells_z = core.shape
    inner = rows_x * rows_y
    cells[...] = dot3(split(spectrum[...], 2), (high[...], low[...]), TN)
    cells[0:inner, :] = cells[0:inner, :] + core[...].reshape(inner, cells_z)
    start = inner
    for faces, skip in ((x_faces, 1), (y_faces, 0)):
        for side in range(2):
            length = faces.shape[1] - 2 * skip
            rows = slice(start, start + length)
            cells[rows, :] = cells[rows, :] + faces[side, skip : skip + length, :]
            start += length
    x_edge = [inner, inner + rows_y]
    y_edge = [inner + 2 * rows_y, inner + 2 * rows_y + rows_x]
    return x_edge, y_edge


def displacement_kernel(core, x_faces, y_faces, spectrum, high, low, displacement, pad, cells):
    rows_x, rows_y, cells_z = core.shape
    x_edge, y_edge = combine(core, x_faces, y_faces, spectrum, high, low, cells)
    for x in range(rows_x):
        pad[x, 8 : rows_y + 8, :] = cells[x * rows_y : (x + 1) * rows_y, :]
        pad[x, 7:8, :] = cells[y_edge[0] + x : y_edge[0] + x + 1, :]
        pad[x, rows_y + 8 : rows_y + 9, :] = cells[y_edge[1] + x : y_edge[1] + x + 1, :]

    def line(x):
        if x < 0:
            return cells[x_edge[0] : x_edge[0] + rows_y, :]
        if x >= rows_x:
            return cells[x_edge[1] : x_edge[1] + rows_y, :]
        return cells[x * rows_y : (x + 1) * rows_y, :]

    for x in range(rows_x):
        here = line(x)
        displacement[0, x] = (line(x - 1) - line(x + 1)) * 0.5
        displacement[1, x] = (pad[x, 7 : rows_y + 7, :] - pad[x, 9 : rows_y + 9, :]) * 0.5
        displacement[2, x] = (pltpu.roll(here, 1, 1) - pltpu.roll(here, cells_z - 1, 1)) * 0.5


def block_kernel(
    planes, half, tiles_y, span, own, core, x_faces, y_faces, spectrum, high, low, slots,
    out, values, labels,
    cells, spread,
):
    rows_x, rows_y, cells_z = core.shape
    inner = rows_x * rows_y
    blocks_x, blocks_y, blocks_z = rows_x // 8, rows_y // 8, cells_z // 8
    per = LANES // blocks_z
    x_edge, y_edge = combine(core, x_faces, y_faces, spectrum, high, low, cells)

    width = spread.shape[0] * LANES
    col = lax.broadcasted_iota(jnp.int32, (cells_z, width), 1)
    wanted = (8 * (col % blocks_z) + col // blocks_z + cells_z - 1) % cells_z
    choose = (wanted == lax.broadcasted_iota(jnp.int32, (cells_z, width), 0)).astype(BF16)
    pieces = split(cells[...], 3)
    moved = dot(pieces[0], choose) + dot(pieces[1], choose) + dot(pieces[2], choose)
    for quad in range(spread.shape[0]):
        spread[quad] = moved[:, quad * LANES : (quad + 1) * LANES]

    def put(row, tiles):
        for quad in range(width // LANES):
            every = [tiles(b // blocks_y, b % blocks_y, quad) for b in range(blocks_x * blocks_y)]
            for block in range(0, len(every), per):
                for k, item in enumerate(swap_groups(every[block : block + per], blocks_z)):
                    where = row(quad * per + k - 1)
                    if where is not None:
                        start = block * blocks_z
                        values[where : where + 8, start : start + LANES] = item

    def x_tile(a):
        def tile(bx, by, quad):
            x = 8 * bx + a
            top = x_edge[0] if x < 0 else x_edge[1] if x >= rows_x else x * rows_y
            return spread[quad, top + 8 * by : top + 8 * by + 8, :]

        return tile

    for a in range(-1, 9):
        def row(e, a=a):
            if 0 <= e < 8:
                return ((a + 1) * 8 + e) * 8
            if e in (-1, 8) and 0 <= a < 8:
                return 640 + (64 if e == 8 else 0) + a * 8
            return None

        put(row, x_tile(a))
    for side, edge in enumerate((-1, 8)):
        def tile(bx, by, quad, edge=edge):
            y = 8 * by + edge
            if y < 0 or y >= rows_y:
                top = y_edge[0 if y < 0 else 1] + 8 * bx
                return spread[quad, top : top + 8, :]
            return spread[quad, pl.ds(8 * bx * rows_y + y, 8, stride=rows_y), :]

        put(lambda e, side=side: 768 + side * 64 + e * 8 if 0 <= e < 8 else None, tile)

    count = slots.shape[1]
    named = spectrum[:, inner : inner + LANES].astype(BF16)
    row = lax.broadcasted_iota(jnp.int32, (cells_z, count), 0)
    slot = lax.broadcasted_iota(jnp.int32, (cells_z, count), 1)
    tile = slot // half
    member = tile // tiles_y * span + tile % span
    source = (row % planes == 0) & (row // planes == member)
    by_lane = dot(named, source.astype(BF16), TN)
    dims = (LANES, count)
    slot = iota(dims, 1)
    moved = jnp.where(slot // half % tiles_y // span == own[0], 0, 2 * half)
    lane = iota(dims, 0) - 2 * (rows_x + rows_y) - moved
    place = slot % half
    for part in range(2):
        label = jnp.sum(jnp.where(lane == place + part * half, by_lane, 0.0), axis=0, keepdims=True)
        labels[part] = label.astype(jnp.int32)

    fill_slots(0, values, slots, out)


def fill_slots(part, values, slots, out):
    count = slots.shape[1]
    pieces = split(values[...], 3)
    number = lax.broadcasted_iota(jnp.int32, (count, count), 0) + part * count
    chosen = (slots[...] == number).astype(BF16)
    out[...] = dot(chosen, pieces[0], NT) + dot(chosen, pieces[1], NT) + dot(chosen, pieces[2], NT)


def spline(shift):
    g = jnp.abs(shift)
    h = 1.0 - g
    gg, hh = g * g, h * h
    near = (2.0 / 3.0) - gg + 0.5 * gg * g
    ahead = (2.0 / 3.0) - hh + 0.5 * hh * h
    back = hh * h * (1.0 / 6.0)
    far = gg * g * (1.0 / 6.0)
    up = shift >= 0.0
    zero = jnp.zeros_like(far)
    return (
        jnp.where(up, zero, far),
        jnp.where(up, back, ahead),
        near,
        jnp.where(up, ahead, back),
        jnp.where(up, far, zero),
    )


def deposit_kernel(blocks_x, blocks_y, blocks_z, last, blocks, labels, *refs):
    if last:
        before, core, x_rims, y_rims, turned, weights, pieces, grouped, tile = refs
    else:
        core, turned, weights, pieces, grouped, tile = refs
    slots = blocks.shape[0]
    cells_z = 8 * blocks_z
    per = LANES // blocks_z
    windows = blocks_x * blocks_y * blocks_z
    sub = lax.broadcasted_iota(jnp.int32, (8, LANES), 0)
    for g in range(slots // LANES):
        turned[g] = jnp.transpose(blocks[g * LANES : (g + 1) * LANES, :])

    @pl.loop(0, slots // LANES)
    def _(g):
        def rows(start):
            return turned[g, pl.ds(pl.multiple_of(start, 8), 8), :]

        @pl.loop(0, 8)
        def _(a):
            for e in range(8):
                here = rows((a + 1) * 64 + e * 8)
                x_diff = rows(a * 64 + e * 8) - rows((a + 2) * 64 + e * 8)
                z_low = rows((a + 1) * 64 + e * 8 - 8) if e > 0 else rows(640 + a * 8)
                z_top = rows((a + 1) * 64 + e * 8 + 8) if e < 7 else rows(704 + a * 8)
                y_low = jnp.where(
                    sub == 0, turned[g, pl.ds(768 + e * 8 + a, 1), :], pltpu.roll(here, 1, 0)
                )
                y_top = jnp.where(
                    sub == 7, turned[g, pl.ds(832 + e * 8 + a, 1), :], pltpu.roll(here, 7, 0)
                )
                for axis, diff in enumerate((x_diff, y_low - y_top, z_low - z_top)):
                    for k, weight in enumerate(spline(jnp.clip(diff * 0.5, -1.0, 1.0))):
                        if (axis, k) != (1, 2):
                            weights[axis * 5 + k, a * 8 + e] = weight

        top_lanes = pl.ds(pl.multiple_of(g * LANES, LANES), LANES)
        rest_lanes = pl.ds(pl.multiple_of(slots + g * LANES, LANES), LANES)

        def cell_row(s, depths):
            sums = {}
            for a in range(8):
                for k in depths:
                    at = a * 8 + (s - k)
                    w_z = weights[10 + k, at]
                    w_y = [weights[5 + j, at] if j != 2 else None for j in range(5)]
                    for i in range(5):
                        plane = weights[i, at] * w_z
                        for j in range(5):
                            key = (a + i, j)
                            term = plane * w_y[j] if j != 2 else plane
                            sums[key] = sums[key] + term if key in sums else term
                for u in [a] if a < 7 else range(7, 12):
                    rows = [sums[u, j] for j in range(5)]
                    rows[2] = rows[2] - ((rows[0] + rows[1]) + (rows[3] + rows[4]))
                    moved = [pltpu.roll(rows[j], j, 0) for j in range(1, 5)]
                    every = rows[0] + ((moved[0] + moved[1]) + (moved[2] + moved[3]))
                    past = [jnp.where(sub < j + 1, moved[j], 0.0) for j in range(4)]
                    tail = (past[0] + past[1]) + (past[2] + past[3])
                    top, rest = split(jnp.concatenate([every - tail, tail], 0), 2)
                    out = pl.ds(pl.multiple_of((s * 12 + u) * 16, 16), 16)
                    pieces[out, top_lanes] = top
                    pieces[out, rest_lanes] = rest

        for s in (0, 1, 2, 3, 8, 9, 10, 11):
            cell_row(s, [k for k in range(5) if 0 <= s - k < 8])

        @pl.loop(4, 8)
        def _(s):
            cell_row(s, range(5))

    named = (labels[...] == lax.broadcasted_iota(jnp.int32, (windows, slots), 0)).astype(F32)
    named = jnp.transpose(named).astype(BF16)
    area = 12 * 16
    named = jnp.concatenate([named, named], 0)

    @pl.loop(0, 12 // per)
    def _(quad):
        rows = pl.ds(pl.multiple_of(quad * per * area, 16), per * area)
        summed = dot(pieces[rows, :], named)
        for wide in range(windows // LANES):
            lanes = slice(wide * LANES, (wide + 1) * LANES)
            part = [summed[k * area : (k + 1) * area, lanes] for k in range(per)]
            for t, item in enumerate(swap_groups(part, blocks_z)):
                rows = slice((wide * per + t) * area, (wide * per + t + 1) * area)
                grouped[0, quad, rows, :], grouped[1, quad, rows, :] = split(item, 2)

    depth = 12 * blocks_z
    row = lax.broadcasted_iota(jnp.int32, (depth, cells_z), 0)
    wanted = (8 * (row % blocks_z) + row // blocks_z + cells_z - 2) % cells_z
    place = (wanted == lax.broadcasted_iota(jnp.int32, (depth, cells_z), 1)).astype(BF16)
    tile[...] = before[...] if last else jnp.zeros_like(tile)
    quads = depth // LANES
    left = jnp.concatenate([grouped[piece, quad] for piece in range(2) for quad in range(quads)], 1)
    total = dot(left, jnp.concatenate([place, place], 0))
    for bx in range(blocks_x):
        for by in range(blocks_y):
            at = (bx * blocks_y + by) * area
            rows = slice(bx * 8, bx * 8 + 12)
            cols = slice(by * 8, by * 8 + 16)
            tile[rows, cols, :] = tile[rows, cols, :] + total[at : at + area].reshape(12, 16, cells_z)

    if not last:
        core[...] = tile[...]
        return
    rows_x, rows_y = 8 * blocks_x, 8 * blocks_y
    core[...] = tile[2 : rows_x + 2, 2 : rows_y + 2, :]
    for side in range(2):
        x = side * (rows_x + 2)
        y = side * (rows_y + 2)
        x_rims[side] = tile[x : x + 2, 2 : rows_y + 2, :]
        y_rims[side] = tile[:, y : y + 2, :]


def corner_kernel(x_rims, y_low, y_top, out):
    rows_x, rows_y = y_low.shape[0] - 4, x_rims.shape[2]
    for side in range(2):
        x = side * (rows_x + 2)
        out[side] = x_rims[side]
        out[side, :, 0:2, :] = out[side, :, 0:2, :] + y_low[x : x + 2]
        out[side, :, rows_y - 2 :, :] = out[side, :, rows_y - 2 :, :] + y_top[x : x + 2]


def rim_kernel(core, y_low, y_top, x_low, x_top, out):
    rows_x, rows_y, _ = core.shape
    out[...] = core[...]
    for part, face in ((slice(0, 2), y_low), (slice(rows_y - 2, rows_y), y_top)):
        out[:, part, :] = out[:, part, :] + face[2 : rows_x + 2]
    for part, face in ((slice(0, 2), x_low), (slice(rows_x - 2, rows_x), x_top)):
        out[part] = out[part] + face[...]


def per_device(potential, owner, window):
    rows_x, rows_y, cells_z = potential.shape
    tiles_x, tiles_y = lax.axis_size("px"), lax.axis_size("py")
    tiles = tiles_x * tiles_y
    grid_x, grid_y = rows_x * tiles_x, rows_y * tiles_y
    planes = cells_z // tiles
    inner = rows_x * rows_y
    used = inner + -(-2 * (rows_x + rows_y) // LANES) * LANES
    blocks_x, blocks_y, blocks_z = rows_x // 8, rows_y // 8, cells_z // 8
    blocks = blocks_x * blocks_y * blocks_z
    half = max(2, 2 * blocks // tiles) // 2
    both = ("px", "py")

    def exchange(x):
        return lax.all_to_all(x, both, split_axis=0, concat_axis=0, tiled=True)

    slots, labels = call(
        functools.partial(slot_kernel, half, 2 * (rows_x + rows_y)),
        (shape(1, blocks, dtype=jnp.int32), shape(tiles, LANES)),
        [], 8, 2 * tiles * LANES * blocks, 8 * blocks,
    )(owner.reshape(blocks, 1), owner.reshape(1, blocks), window.reshape(1, blocks))

    line = shape(rows_x, cells_z)
    core, y_last, y_first = pl.pallas_call(
        prepare_kernel,
        out_shape=(shape(rows_x, rows_y, cells_z), line, line),
        in_specs=[FAR],
        out_specs=[VMEM] * 3,
        scratch_shapes=[pltpu.SemaphoreType.DMA],
        compiler_params=pltpu.CompilerParams(vmem_limit_bytes=8 << 20),
        cost_estimate=pl.CostEstimate(flops=0, bytes_accessed=2 << 20, transcendentals=0),
    )(potential)
    last_x = rows_x - 1
    y_faces = jnp.stack([send(y_last, "py", 1), send(y_first, "py", -1)])
    x_lines = [
        jnp.concatenate([y_faces[0, x : x + 1], core[x], y_faces[1, x : x + 1]])
        for x in (last_x, 0)
    ]
    x_faces = jnp.stack([send(x_lines[0], "px", 1), send(x_lines[1], "px", -1)])

    halves = shape(inner, cells_z, dtype=BF16)
    table = shape(cells_z, cells_z, dtype=BF16)
    step = 16
    *source, z_high, z_low = call(
        functools.partial(source_kernel, step), (halves, halves, table, table),
        [pltpu.VMEM((rows_x, rows_y + 16, cells_z), F32)],
        8, 60 * inner * cells_z, 2 << 20,
    )(core, y_faces)
    spectrum = call(
        spectrum_kernel, shape(cells_z, inner),
        [pltpu.VMEM((3, rows_y + 16, cells_z), F32)] + [pltpu.VMEM((inner, cells_z), BF16)] * 2,
        12, 6 * inner * cells_z**2, 2 << 20,
    )(core, y_faces, x_faces, *source, z_high, z_low)
    span = tiles_y // 2
    length = span * rows_y
    halved = (
        2 * length == LANES and grid_x == LANES and planes == 8 and tiles_y == 8
        and 2 * (rows_x + rows_y) + 4 * half <= LANES
    )
    if halved:
        groups = [
            [i * tiles_y + g * span + j for i in range(tiles_x) for j in range(span)] for g in range(2)
        ]

        def exchange_half(x):
            return lax.all_to_all(x, both, 0, 0, axis_index_groups=groups, tiled=True)

        place_x, place_y = lax.axis_index("px"), lax.axis_index("py")
        own = (place_y // span).astype(jnp.int32).reshape(1)
        first = ((place_x * span + place_y % span) * 2 * planes).astype(jnp.int32).reshape(1)
        lap_z = laplace_of(cells_z)
        lap_x = np.broadcast_to(laplace_of(grid_x)[:, None], (grid_x, LANES))
        lap_xy = lap_x + np.tile(laplace_of(length), 2)[None, :]
        x_table = pieces_of(table_of(grid_x))
        y_table = pieces_of(np.kron(np.eye(2, dtype=np.float32), table_of(length)))
        square = shape(grid_x, LANES)
        cube = shape(planes, grid_x, LANES)
        slab = exchange_half(spectrum).reshape(tiles // 2, 2 * planes, inner)
        tables = call(
            functools.partial(decay_kernel, length),
            (cube, cube, square, square, shape(LANES, 2 * planes * LANES, dtype=BF16)),
            [], 16, 100 * planes * grid_x * LANES, 2 << 20, 2,
        )(first, lap_z, lap_x)
        found, ends = call(
            functools.partial(
                half_kernel, tiles_x, span, rows_x, rows_y,
                SECOND_ORDER / (grid_x * length * cells_z), 2 * (rows_x + rows_y),
            ),
            (cube, square), [pltpu.VMEM((grid_x * planes, LANES), F32)],
            16, 12 * planes * grid_x**2 * LANES, 2 << 20, 2,
        )(first, lap_z, slab, labels, lap_xy, *x_table, *y_table)
        arrived_ends = lax.ppermute(ends, "py", [(j, (j + span) % tiles_y) for j in range(tiles_y)])
        returned = call(
            functools.partial(join_kernel, tiles_x, span, rows_x, rows_y, 2 * half),
            shape(tiles // 2, 2 * planes, used),
            [pltpu.VMEM((grid_x * planes, LANES), F32), pltpu.VMEM((LANES, grid_x), F32)],
            24, 12 * planes * grid_x**2 * LANES, 2 << 20, 2,
        )(first, own, found, ends, arrived_ends, labels, *tables, *x_table)
        modes = exchange_half(returned.reshape(cells_z, used))
    else:
        span = tiles_y
        own = jnp.zeros((1,), jnp.int32)
        slab = exchange(spectrum).reshape(tiles, planes, inner)
        scale = SECOND_ORDER / (grid_x * grid_y * cells_z)
        returned = solve_plain(slab, labels, rows_x, rows_y, cells_z, tiles_x, tiles_y, scale)
        modes = exchange(returned.reshape(cells_z, used))

    width = -(-10 * blocks_z // LANES) * LANES
    cells = pltpu.VMEM((used, cells_z), F32)
    tile_args = (core, x_faces, y_faces, modes, z_high, z_low)
    half_out = shape(blocks, ROWS)
    sent, values, arrived_labels = call(
        functools.partial(block_kernel, cells_z // (tiles_x * span), half, tiles_y, span),
        (half_out, shape(ROWS, blocks), shape(2, 1, blocks, dtype=jnp.int32)),
        [cells, pltpu.VMEM((width // LANES, used, LANES), F32)],
        40, 20 * used * cells_z**2, 6 << 20, 1,
    )(own, *tile_args, slots)
    first = exchange(sent)
    later = call(functools.partial(fill_slots, 1), half_out, [], 16, 6 * ROWS * blocks**2, 4 << 20)(values, slots)
    displacement = call(
        displacement_kernel, shape(3, rows_x, rows_y, cells_z),
        [pltpu.VMEM((rows_x, rows_y + 16, cells_z), F32), cells],
        16, 6 * used * cells_z**2, 4 << 20,
    )(*tile_args)

    later, displacement = lax.optimization_barrier((later, displacement))
    arrived = first, exchange(later)
    tile_shape = (rows_x + 4, rows_y + 8, cells_z)
    scratch = [
        pltpu.VMEM((blocks // LANES, ROWS, LANES), F32),
        pltpu.VMEM((15, 64, 8, LANES), F32),
        pltpu.VMEM((12 * 12 * 16, 2 * blocks), BF16),
        pltpu.VMEM((2, 12 * blocks_z // LANES, blocks_x * blocks_y * 12 * 16, LANES), BF16),
        pltpu.VMEM(tile_shape, F32),
    ]
    sizes = (blocks_x, blocks_y, blocks_z)
    cost = (300 * blocks * 512, 4 << 20)
    tile = call(
        functools.partial(deposit_kernel, *sizes, False), shape(*tile_shape), scratch, 32, *cost
    )(arrived[0], arrived_labels[0])
    middle, x_rims, y_rims = call(
        functools.partial(deposit_kernel, *sizes, True),
        (
            shape(rows_x, rows_y, cells_z), shape(2, 2, rows_y, cells_z),
            shape(2, rows_x + 4, 2, cells_z),
        ),
        scratch, 32, *cost,
    )(arrived[1], arrived_labels[1], tile)

    y_sides = send(y_rims[1], "py", 1), send(y_rims[0], "py", -1)
    x_rims = call(corner_kernel, shape(*x_rims.shape), [], 4, 8 * rows_y * cells_z, 1 << 17)(
        x_rims, *y_sides
    )
    x_sides = send(x_rims[1], "px", 1), send(x_rims[0], "px", -1)
    density = call(rim_kernel, shape(rows_x, rows_y, cells_z), [], 8, inner * cells_z, 2 << 20)(
        middle, *y_sides, *x_sides
    )
    return (displacement, density)


def solution(mesh):
    return jax.shard_map(
        per_device,
        mesh=mesh,
        in_specs=(P("px", "py", None), P("px", "py", None, None), P("px", "py", None)),
        out_specs=(P(None, "px", "py", None), P("px", "py", None)),
        check_vma=False,
    )
```

```python
import functools
import math

import jax
import jax.numpy as jnp
import numpy as np
from jax import lax
from jax.experimental import pallas as pl
from jax.experimental.pallas import tpu as pltpu
from jax.sharding import PartitionSpec as P

SECOND_ORDER = 3.0 / 7.0
F32 = jnp.float32
BF16 = jnp.bfloat16
LANES = 128
ROWS = 896
VMEM = pl.BlockSpec(memory_space=pltpu.VMEM)
SMEM = pl.BlockSpec(memory_space=pltpu.SMEM)
FAR = pl.BlockSpec(memory_space=pltpu.HBM)
NN = (((1,), (0,)), ((), ()))
NT = (((1,), (1,)), ((), ()))
TN = (((0,), (0,)), ((), ()))


def split(x, pieces):
    out = []
    for piece in range(pieces):
        part = x.astype(BF16)
        out.append(part)
        if piece < pieces - 1:
            x = x - part.astype(F32)
    return out


def dot(a, b, dims=NN):
    return lax.dot_general(a, b, dims, preferred_element_type=F32)


def dot3(a, b, dims=NN):
    return dot(a[0], b[0], dims) + (dot(a[0], b[1], dims) + dot(a[1], b[0], dims))


def swap_groups(rows, group):
    rows = list(rows)
    count = len(rows)
    axis = rows[0].ndim - 1
    lane = lax.broadcasted_iota(jnp.int32, rows[0].shape, axis) // group
    step = 1
    while step < count:
        low = (lane & step) == 0
        for k in range(count):
            if k & step:
                continue
            a, b = rows[k], rows[k + step]
            rows[k] = jnp.where(low, a, pltpu.roll(b, step * group, axis))
            rows[k + step] = jnp.where(low, pltpu.roll(a, LANES - step * group, axis), b)
        step *= 2
    return rows


def table_of(length):
    modes = np.arange(length)
    angle = (modes[:, None] * modes[None, :] % length) * (2.0 * math.pi / length)
    return (np.cos(angle) + np.sin(angle)).astype(np.float32)


def pieces_of(table):
    high = table.astype(jnp.bfloat16)
    low = (table - high.astype(np.float32)).astype(jnp.bfloat16)
    return np.asarray(high), np.asarray(low)


def laplace_of(length):
    return (2.0 * np.cos(np.arange(length) * (2.0 * math.pi / length)) - 2.0).astype(np.float32)


def call(body, outs, scratch, vmem, flops, moved, scalars=0):
    def run(*operands):
        return pl.pallas_call(
            body,
            out_shape=outs,
            in_specs=[SMEM] * scalars + [VMEM] * (len(operands) - scalars),
            out_specs=jax.tree.map(lambda _: VMEM, outs),
            scratch_shapes=scratch,
            compiler_params=pltpu.CompilerParams(vmem_limit_bytes=vmem << 20),
            cost_estimate=pl.CostEstimate(flops=flops, bytes_accessed=moved, transcendentals=0),
        )(*operands)

    return run


def shape(*dims, dtype=F32):
    return jax.ShapeDtypeStruct(dims, dtype)


def send(x, axis, step):
    size = lax.axis_size(axis)
    return lax.ppermute(x, axis, [(i, (i + step) % size) for i in range(size)])


def slot_kernel(half, start, owner_col, owner_row, window_row, slot_out, label_out):
    count = owner_row.shape[1]
    tiles = label_out.shape[0]
    later = lax.broadcasted_iota(jnp.int32, (count, count), 0) < lax.broadcasted_iota(
        jnp.int32, (count, count), 1
    )
    owners = owner_row[...]
    same = (owner_col[...] == owners) & later
    rank = jnp.sum(same.astype(F32), axis=0, keepdims=True).astype(jnp.int32)
    second = rank >= half
    place = owners * half + jnp.where(second, rank - half, rank)
    slot_out[...] = jnp.where(second, place + count, place)
    tile = lax.broadcasted_iota(jnp.int32, (tiles, count), 0)
    named = jnp.where(tile == owners, window_row[...] + 1, 0).astype(F32).astype(BF16)
    lane = lax.broadcasted_iota(jnp.int32, (LANES, count), 0)
    label_out[...] = dot(named, (lane == rank + start).astype(BF16), NT) - 1.0


def source_of(at, cells_z):
    def ahead(value):
        return pltpu.roll(value, cells_z - 1, 1)

    def behind(value):
        return pltpu.roll(value, 1, 1)

    here = at(0, 0)
    ahead_x, behind_x, ahead_y, behind_y = at(1, 0), at(-1, 0), at(0, 1), at(0, -1)
    xx = ahead_x - 2.0 * here + behind_x
    yy = ahead_y - 2.0 * here + behind_y
    zz = ahead(here) - 2.0 * here + behind(here)
    xy = (at(1, 1) - at(1, -1) - at(-1, 1) + at(-1, -1)) * 0.25
    across_x, across_y = ahead_x - behind_x, ahead_y - behind_y
    xz = (ahead(across_x) - behind(across_x)) * 0.25
    yz = (ahead(across_y) - behind(across_y)) * 0.25
    return xx * yy + xx * zz + yy * zz - xy * xy - xz * xz - yz * yz


def prepare_kernel(potential, core, y_last, y_first, sem):
    copy = pltpu.make_async_copy(potential, core, sem)
    copy.start()
    copy.wait()
    rows_x, rows_y, _ = core.shape
    for x in range(rows_x):
        y_last[x : x + 1, :] = core[x, rows_y - 1 : rows_y, :]
        y_first[x : x + 1, :] = core[x, 0:1, :]


def source_kernel(step, core, y_faces, high, low, table_high, table_low, pad):
    rows_x, rows_y, cells_z = core.shape
    coarse = cells_z // step

    def turns(count, stride):
        row = lax.broadcasted_iota(jnp.int32, (count, cells_z), 0) * stride
        col = lax.broadcasted_iota(jnp.int32, (count, cells_z), 1)
        angle = (row * col % cells_z).astype(F32) * (2.0 * math.pi / cells_z)
        return jnp.cos(angle), jnp.sin(angle)

    wide_cos, wide_sin = turns(coarse, step)
    fine_cos, fine_sin = turns(step, 1)
    fine, turned = fine_cos + fine_sin, fine_cos - fine_sin
    for k in range(coarse):
        rows = slice(k * step, (k + 1) * step)
        value = wide_cos[k : k + 1] * fine + wide_sin[k : k + 1] * turned
        table_high[rows, :], table_low[rows, :] = split(value, 2)
    pad[:, 8 : rows_y + 8, :] = core[...]
    for x in range(rows_x):
        pad[x, 7:8, :] = y_faces[0, x : x + 1, :]
        pad[x, rows_y + 8 : rows_y + 9, :] = y_faces[1, x : x + 1, :]

    @pl.loop(1, rows_x - 1, unroll=3)
    def _(x):
        def at(dx, dy):
            return pad[x + dx, 8 + dy : 8 + dy + rows_y, :]

        rows = pl.ds(pl.multiple_of(x * rows_y, rows_y), rows_y)
        high[rows, :], low[rows, :] = split(source_of(at, cells_z), 2)

    for x in (0, rows_x - 1):
        rows = slice(x * rows_y, (x + 1) * rows_y)
        high[rows, :] = jnp.zeros((rows_y, cells_z), BF16)
        low[rows, :] = jnp.zeros((rows_y, cells_z), BF16)


def spectrum_kernel(core, y_faces, x_faces, inner_high, inner_low, high, low, spectrum, pad, source_high, source_low):
    rows_x, rows_y, cells_z = core.shape
    source_high[...] = inner_high[...]
    source_low[...] = inner_low[...]
    for side in range(2):
        edge = side * (rows_x - 1)
        for line in range(3):
            x = edge + line - 1
            if 0 <= x < rows_x:
                pad[line, 8 : rows_y + 8, :] = core[x]
                pad[line, 7:8, :] = y_faces[0, x : x + 1, :]
                pad[line, rows_y + 8 : rows_y + 9, :] = y_faces[1, x : x + 1, :]
            else:
                pad[line, 7 : rows_y + 9, :] = x_faces[side]

        def at(dx, dy):
            return pad[1 + dx, 8 + dy : 8 + dy + rows_y, :]

        rows = slice(edge * rows_y, (edge + 1) * rows_y)
        source_high[rows, :], source_low[rows, :] = split(source_of(at, cells_z), 2)
    spectrum[...] = dot3((high[...], low[...]), (source_high[...], source_low[...]), NT)


def stacked(pieces):
    high, low = pieces
    return jnp.concatenate(
        [jnp.concatenate([high, low], 1), jnp.concatenate([high, jnp.zeros_like(high)], 1)], 0
    )


def joined(value):
    width = value.shape[1] // 2
    return value[:, :width] + value[:, width:]


def placed(pieces, choose):
    return dot(pieces[0], choose) + dot(pieces[1], choose) + dot(pieces[2], choose)


def iota(dims, axis):
    return lax.broadcasted_iota(jnp.int32, dims, axis)


def decay(w, length):
    grow = w + jnp.sqrt(w * (w + 2.0))
    rate = jnp.log(1.0 + grow)
    ratio = 1.0 / (1.0 + grow)
    both = (1.0 + grow) + jnp.exp(-rate * (length - 1.0))
    flat = w <= 0.0
    return rate, 2.0 * (1.0 + ratio) * both, 2.0 * jnp.where(flat, 1.0, grow * ratio * both), flat


def decay_kernel(length, first, lap_z, lap_x, even, odd, edge_even, edge_odd, spread):
    count = even.shape[0]
    dims = even.shape[1:]
    lane = iota(dims, 1)
    group = lane // length
    y = (lane % length).astype(F32)
    start = first[0]
    for q in range(count):
        along_z = jnp.where(group == 0, lap_z[start + q], lap_z[start + count + q])
        rate, plus, minus, flat = decay(-0.5 * (lap_x[...] + along_z), length)
        rise, fall = jnp.exp(-rate * y), jnp.exp(-rate * (length - 1.0 - y))
        even[q] = (rise + fall) / plus
        odd[q] = jnp.where(flat, 0.25 * (length - 1.0) - 0.5 * y, (rise - fall) / minus)
    along_z = jnp.zeros(dims, F32)
    for q in range(count):
        for g in range(2):
            along_z = jnp.where(lane // 2 == 2 * q + g, lap_z[start + g * count + q], along_z)
    rate, plus, minus, flat = decay(-0.5 * (lap_x[...] + along_z), length)
    last = jnp.exp(-rate * (length - 1.0))
    edge_even[...] = (1.0 + last) / plus
    edge_odd[...] = jnp.where(flat, 0.25 * (length - 1.0), (1.0 - last) / minus)
    dims = spread.shape
    col = iota(dims, 1)
    row = iota(dims, 0)
    hit = row // 2 == 2 * (col // (2 * LANES)) + col % LANES // length
    sign = jnp.where((col // LANES % 2 == 1) & (row % 2 == 0), -1.0, 1.0)
    spread[...] = jnp.where(hit, sign, 0.0).astype(BF16)


def half_kernel(
    tiles_x, tiles_y, rows_x, rows_y, scale, mark,
    first, lap_z, slab, labels, lap_xy, hx_high, hx_low, hy_high, hy_low,
    found, ends, planes,
):
    grid_x = tiles_x * rows_x
    count = slab.shape[1] // 2
    length = tiles_y * rows_y
    per = LANES // rows_y
    along_y = stacked((hy_high[...], hy_low[...]))
    along_x = jnp.concatenate([hx_high[...], hx_low[...]], 1)

    def times_y(value):
        return joined(dot(jnp.concatenate(split(value, 2), 1), along_y))

    for i in range(tiles_x):
        for part in range(rows_x // per):
            lanes = slice(part * LANES, (part + 1) * LANES)
            rows = [
                slab[i * tiles_y + j, g * count : (g + 1) * count, lanes]
                for g in range(2)
                for j in range(tiles_y)
            ]
            x = (i * rows_x + part * per) * count
            planes[x : x + per * count, :] = times_y(jnp.concatenate(swap_groups(rows, rows_y), 0))
    dims = (grid_x, LANES)
    lane, row = iota(dims, 1), iota(dims, 0)
    block = jnp.zeros(dims, F32)
    for q in range(count):
        modes = joined(dot(along_x, stacked(split(planes[pl.ds(q, grid_x, stride=count), :], 2))))
        eigen = lap_xy[...] + jnp.where(lane < length, lap_z[first[0] + q], lap_z[first[0] + count + q])
        anchor = eigen == 0.0
        value = times_y(jnp.where(anchor, 0.0, scale / jnp.where(anchor, -1.0, eigen)) * modes)
        found[q] = value
        source = lane - 4 * q
        source = source // 2 * length + source % 2 * (length - 1)
        choose = (row == source) & (lane >= 4 * q) & (lane < 4 * q + 4)
        block = block + placed(split(value, 3), choose.astype(BF16))
        if q == 0:
            mean = pltpu.roll(modes * scale, 4 * count, 1)
            block = block + jnp.where((row == 0) & (lane == 4 * count), mean, 0.0)
    ends[...] = block
    tiles = labels.shape[0]
    ends[0:tiles, :] = jnp.where(lane[0:tiles] < mark, block[0:tiles], labels[...])


def join_kernel(
    tiles_x, tiles_y, rows_x, rows_y, places,
    first, half, found, ends, arrived, labels, even, odd, edge_even, edge_odd, spread, hx_high, hx_low,
    out, planes, faces,
):
    grid_x = tiles_x * rows_x
    count = found.shape[0]
    length = tiles_y * rows_y
    per = LANES // rows_y
    along_x = jnp.concatenate([hx_high[...], hx_low[...]], 1)

    def times_x(value):
        return joined(dot(along_x, stacked(split(value, 2))))

    dims = (grid_x, LANES)
    lane, row = iota(dims, 1), iota(dims, 0)
    jump = jnp.where(lane < 4 * count + 1, arrived[...] - ends[...], 0.0)
    pieces = split(jump, 2)
    wide = dot(pieces[0], spread[...]) + dot(pieces[1], spread[...])
    mean = jnp.where(first[0] == 0, -0.5 * jump[0:1, 4 * count : 4 * count + 1], 0.0)
    y = lane.astype(F32)
    bend = jnp.where(
        (row == 0) & (lane < length),
        mean * (0.5 * y * y - 0.5 * (length - 1.0) * y - 0.25 * length),
        0.0,
    )
    target = iota((LANES, LANES), 1)
    source = iota((LANES, LANES), 0)
    side, j, group = target // 8 % 2, target // 2 % tiles_y, target % 2
    inside = ((side == 0) & (j > 0)) | ((side == 1) & (j < tiles_y - 1))
    wanted = group * length + jnp.where(side == 0, j * rows_y - 1, (j + 1) * rows_y)
    lines = jnp.zeros(dims, F32)
    for q in range(count):
        at = 2 * q * LANES
        value = found[q] + (wide[:, at : at + LANES] * even[q] + wide[:, at + LANES : at + 2 * LANES] * odd[q])
        if q == 0:
            value = value + bend
        choose = inside & (source == wanted) & (target // 16 == q)
        lines = lines + placed(split(value, 3), choose.astype(BF16))
        planes[pl.ds(q, grid_x, stride=count), :] = times_x(value)
    low = lane % 2 == 0
    other = jnp.where(low, pltpu.roll(jump, LANES - 1, 1), pltpu.roll(jump, 1, 1))
    change = (jump + other) * edge_even[...] + (other - jump) * edge_odd[...]
    change = change + jnp.where((row == 0) & (lane < 2), -0.25 * length * mean, 0.0)
    beyond = jnp.where(lane < 4 * count, arrived[...] - change, 0.0)
    first_side = source % 2 == 1
    goal = source // 4 * 16 + source // 2 % 2 + jnp.where(first_side, 0, 8 + 2 * (tiles_y - 1))
    choose = (target == goal) & (source < 4 * count)
    lines = lines + placed(split(beyond, 3), choose.astype(BF16))
    faces[...] = jnp.transpose(times_x(lines))

    def row_of(x):
        x = x % grid_x
        return planes[x * count : (x + 1) * count, :]

    lane = iota((count, LANES), 1)
    for i in range(tiles_x):
        for part in range(rows_x // per):
            lanes = slice(part * LANES, (part + 1) * LANES)
            rows = [row_of(i * rows_x + part * per + t) for t in range(per)]
            for k, item in enumerate(swap_groups(rows, rows_y)):
                g, j = k // tiles_y, k % tiles_y
                out[i * tiles_y + j, g * count : (g + 1) * count, lanes] = item
        before, after = row_of(i * rows_x - 1), row_of((i + 1) * rows_x)
        for k in range(per):
            g, j = k // tiles_y, k % tiles_y
            shift = (LANES - k * rows_y) % LANES
            line = pltpu.roll(before, shift, 1) if shift else before
            moved = pltpu.roll(after, (shift + rows_y) % LANES, 1)
            line = jnp.where(lane < rows_y, line, moved)
            for side in range(2):
                face = faces[pl.ds(side * 8 + j * 2 + g, count, stride=16), :]
                start = 2 * rows_y + side * rows_x
                move = (start - i * rows_x) % LANES
                face = pltpu.roll(face, move, 1) if move else face
                line = jnp.where(lane < start, line, face)
            start = 2 * (rows_x + rows_y)
            tile = (2 * i + half[0]) * tiles_y + j
            own, partner = labels[pl.ds(tile, 1), :], pltpu.roll(arrived[pl.ds(tile, 1), :], places, 1)
            line = jnp.where(lane < start, line, jnp.where(lane < start + places, own, partner))
            out[i * tiles_y + j, g * count : (g + 1) * count, rows_x * rows_y : rows_x * rows_y + LANES] = line


def solve_plain(slab, labels, rows_x, rows_y, cells_z, tiles_x, tiles_y, scale):
    high = lax.Precision.HIGHEST
    grid_x, grid_y = tiles_x * rows_x, tiles_y * rows_y
    count = slab.shape[1]
    hx, hy = jnp.asarray(table_of(grid_x)), jnp.asarray(table_of(grid_y))
    planes = slab.reshape(tiles_x, tiles_y, count, rows_x, rows_y).transpose(2, 0, 3, 1, 4)
    planes = planes.reshape(count, grid_x, grid_y)
    modes = jnp.einsum("qxy,xk,yl->qkl", planes, hx, hy, precision=high)
    first = lax.axis_index(("px", "py")) * count
    lap_z = lax.dynamic_slice_in_dim(jnp.asarray(laplace_of(cells_z)), first, count)
    eigen = (
        jnp.asarray(laplace_of(grid_x))[None, :, None]
        + jnp.asarray(laplace_of(grid_y))[None, None, :]
        + lap_z[:, None, None]
    )
    anchor = eigen == 0.0
    solved = jnp.where(anchor, 0.0, scale / jnp.where(anchor, -1.0, eigen)) * modes
    back = jnp.einsum("qkl,xk,yl->qxy", solved, hx, hy, precision=high)
    tiles = back.reshape(count, tiles_x, rows_x, tiles_y, rows_y).transpose(1, 3, 0, 2, 4)
    starts_x, starts_y = np.arange(tiles_x) * rows_x, np.arange(tiles_y) * rows_y
    faces = []
    for edge in (-1, rows_x):
        line = back[:, (starts_x + edge) % grid_x].reshape(count, tiles_x, tiles_y, rows_y)
        faces.append(line.transpose(1, 2, 0, 3))
    for edge in (-1, rows_y):
        line = back[:, :, (starts_y + edge) % grid_y].reshape(count, tiles_x, rows_x, tiles_y)
        faces.append(line.transpose(1, 3, 0, 2))
    tail = labels[:, 2 * (rows_x + rows_y) :].reshape(tiles_x, tiles_y, 1, -1)
    faces.append(jnp.broadcast_to(tail, (tiles_x, tiles_y, count, tail.shape[-1])))
    parts = [tiles.reshape(tiles_x, tiles_y, count, rows_x * rows_y)] + faces
    return jnp.concatenate(parts, -1).reshape(tiles_x * tiles_y, count, -1)


def combine(core, x_faces, y_faces, spectrum, high, low, cells):
    rows_x, rows_y, cells_z = core.shape
    inner = rows_x * rows_y
    cells[...] = dot3(split(spectrum[...], 2), (high[...], low[...]), TN)
    cells[0:inner, :] = cells[0:inner, :] + core[...].reshape(inner, cells_z)
    start = inner
    for faces, skip in ((x_faces, 1), (y_faces, 0)):
        for side in range(2):
            length = faces.shape[1] - 2 * skip
            rows = slice(start, start + length)
            cells[rows, :] = cells[rows, :] + faces[side, skip : skip + length, :]
            start += length
    return edges_of(rows_x, rows_y)


def displacement_kernel(core, x_faces, y_faces, spectrum, high, low, displacement, pad, cells):
    rows_x, rows_y, cells_z = core.shape
    x_edge, y_edge = combine(core, x_faces, y_faces, spectrum, high, low, cells)
    for x in range(rows_x):
        pad[x, 8 : rows_y + 8, :] = cells[x * rows_y : (x + 1) * rows_y, :]
        pad[x, 7:8, :] = cells[y_edge[0] + x : y_edge[0] + x + 1, :]
        pad[x, rows_y + 8 : rows_y + 9, :] = cells[y_edge[1] + x : y_edge[1] + x + 1, :]

    def line(x):
        if x < 0:
            return cells[x_edge[0] : x_edge[0] + rows_y, :]
        if x >= rows_x:
            return cells[x_edge[1] : x_edge[1] + rows_y, :]
        return cells[x * rows_y : (x + 1) * rows_y, :]

    for x in range(rows_x):
        here = line(x)
        displacement[0, x] = (line(x - 1) - line(x + 1)) * 0.5
        displacement[1, x] = (pad[x, 7 : rows_y + 7, :] - pad[x, 9 : rows_y + 9, :]) * 0.5
        displacement[2, x] = (pltpu.roll(here, 1, 1) - pltpu.roll(here, cells_z - 1, 1)) * 0.5


def edges_of(rows_x, rows_y):
    inner = rows_x * rows_y
    return [inner, inner + rows_y], [inner + 2 * rows_y, inner + 2 * rows_y + rows_x]


def sort_kernel(core, x_faces, y_faces, high, low, spread, sorted_high, sorted_low, cells):
    rows_x, rows_y, cells_z = core.shape
    blocks_z = cells_z // 8
    inner = rows_x * rows_y
    x_edge, y_edge = edges_of(rows_x, rows_y)
    cells[0:inner, :] = core[...].reshape(inner, cells_z)
    for side in range(2):
        cells[x_edge[side] : x_edge[side] + rows_y, :] = x_faces[side, 1 : rows_y + 1, :]
        cells[y_edge[side] : y_edge[side] + rows_x, :] = y_faces[side]
    used = y_edge[1] + rows_x
    cells[used:, :] = jnp.zeros((cells.shape[0] - used, cells_z), F32)
    width = sorted_high.shape[1]
    col = lax.broadcasted_iota(jnp.int32, (cells_z, width), 1)
    wanted = (8 * (col % blocks_z) + col // blocks_z + cells_z - 1) % cells_z
    choose = (wanted == lax.broadcasted_iota(jnp.int32, (cells_z, width), 0)).astype(BF16)
    pieces = split(cells[...], 3)
    moved = dot(pieces[0], choose) + dot(pieces[1], choose) + dot(pieces[2], choose)
    for quad in range(spread.shape[0]):
        spread[quad] = moved[:, quad * LANES : (quad + 1) * LANES]
    sorted_high[...] = dot(high[...], choose).astype(BF16)
    sorted_low[...] = dot(low[...], choose).astype(BF16)


def block_kernel(
    rows_x, rows_y, planes, half, tiles_y, span, own, potential, spectrum, high, low, slots,
    out, values, labels,
    spread,
):
    cells_z = spectrum.shape[0]
    inner = rows_x * rows_y
    blocks_x, blocks_y, blocks_z = rows_x // 8, rows_y // 8, cells_z // 8
    per = LANES // blocks_z
    x_edge, y_edge = edges_of(rows_x, rows_y)
    width = high.shape[1]
    second = dot3(split(spectrum[...], 2), (high[...], low[...]), TN)
    for quad in range(width // LANES):
        spread[quad] = potential[quad] + second[:, quad * LANES : (quad + 1) * LANES]

    def put(row, tiles):
        for quad in range(width // LANES):
            every = [tiles(b // blocks_y, b % blocks_y, quad) for b in range(blocks_x * blocks_y)]
            for block in range(0, len(every), per):
                for k, item in enumerate(swap_groups(every[block : block + per], blocks_z)):
                    where = row(quad * per + k - 1)
                    if where is not None:
                        start = block * blocks_z
                        values[where : where + 8, start : start + LANES] = item

    def x_tile(a):
        def tile(bx, by, quad):
            x = 8 * bx + a
            top = x_edge[0] if x < 0 else x_edge[1] if x >= rows_x else x * rows_y
            return spread[quad, top + 8 * by : top + 8 * by + 8, :]

        return tile

    for a in range(-1, 9):
        def row(e, a=a):
            if 0 <= e < 8:
                return ((a + 1) * 8 + e) * 8
            if e in (-1, 8) and 0 <= a < 8:
                return 640 + (64 if e == 8 else 0) + a * 8
            return None

        put(row, x_tile(a))
    for side, edge in enumerate((-1, 8)):
        def tile(bx, by, quad, edge=edge):
            y = 8 * by + edge
            if y < 0 or y >= rows_y:
                top = y_edge[0 if y < 0 else 1] + 8 * bx
                return spread[quad, top : top + 8, :]
            return spread[quad, pl.ds(8 * bx * rows_y + y, 8, stride=rows_y), :]

        put(lambda e, side=side: 768 + side * 64 + e * 8 if 0 <= e < 8 else None, tile)

    count = slots.shape[1]
    named = spectrum[:, inner : inner + LANES].astype(BF16)
    row = lax.broadcasted_iota(jnp.int32, (cells_z, count), 0)
    slot = lax.broadcasted_iota(jnp.int32, (cells_z, count), 1)
    tile = slot // half
    member = tile // tiles_y * span + tile % span
    source = (row % planes == 0) & (row // planes == member)
    by_lane = dot(named, source.astype(BF16), TN)
    dims = (LANES, count)
    slot = iota(dims, 1)
    moved = jnp.where(slot // half % tiles_y // span == own[0], 0, 2 * half)
    lane = iota(dims, 0) - 2 * (rows_x + rows_y) - moved
    place = slot % half
    for part in range(2):
        label = jnp.sum(jnp.where(lane == place + part * half, by_lane, 0.0), axis=0, keepdims=True)
        labels[part] = label.astype(jnp.int32)

    fill_slots(0, values, slots, out)


def fill_slots(part, values, slots, out):
    count = slots.shape[1]
    pieces = split(values[...], 3)
    number = lax.broadcasted_iota(jnp.int32, (count, count), 0) + part * count
    chosen = (slots[...] == number).astype(BF16)
    out[...] = dot(chosen, pieces[0], NT) + dot(chosen, pieces[1], NT) + dot(chosen, pieces[2], NT)


def spline(shift):
    g = jnp.abs(shift)
    h = 1.0 - g
    gg, hh = g * g, h * h
    near = (2.0 / 3.0) - gg + 0.5 * gg * g
    ahead = (2.0 / 3.0) - hh + 0.5 * hh * h
    back = hh * h * (1.0 / 6.0)
    far = gg * g * (1.0 / 6.0)
    up = shift >= 0.0
    zero = jnp.zeros_like(far)
    return (
        jnp.where(up, zero, far),
        jnp.where(up, back, ahead),
        near,
        jnp.where(up, ahead, back),
        jnp.where(up, far, zero),
    )


def deposit_kernel(blocks_x, blocks_y, blocks_z, last, blocks, labels, *refs):
    if last:
        before, core, x_rims, y_rims, turned, weights, pieces, grouped, tile = refs
    else:
        core, turned, weights, pieces, grouped, tile = refs
    slots = blocks.shape[0]
    cells_z = 8 * blocks_z
    per = LANES // blocks_z
    windows = blocks_x * blocks_y * blocks_z
    sub = lax.broadcasted_iota(jnp.int32, (8, LANES), 0)
    for g in range(slots // LANES):
        turned[g] = jnp.transpose(blocks[g * LANES : (g + 1) * LANES, :])

    @pl.loop(0, slots // LANES)
    def _(g):
        def rows(start):
            return turned[g, pl.ds(pl.multiple_of(start, 8), 8), :]

        @pl.loop(0, 8)
        def _(a):
            for e in range(8):
                here = rows((a + 1) * 64 + e * 8)
                x_diff = rows(a * 64 + e * 8) - rows((a + 2) * 64 + e * 8)
                z_low = rows((a + 1) * 64 + e * 8 - 8) if e > 0 else rows(640 + a * 8)
                z_top = rows((a + 1) * 64 + e * 8 + 8) if e < 7 else rows(704 + a * 8)
                y_low = jnp.where(
                    sub == 0, turned[g, pl.ds(768 + e * 8 + a, 1), :], pltpu.roll(here, 1, 0)
                )
                y_top = jnp.where(
                    sub == 7, turned[g, pl.ds(832 + e * 8 + a, 1), :], pltpu.roll(here, 7, 0)
                )
                for axis, diff in enumerate((x_diff, y_low - y_top, z_low - z_top)):
                    for k, weight in enumerate(spline(jnp.clip(diff * 0.5, -1.0, 1.0))):
                        if (axis, k) != (1, 2):
                            weights[g, axis * 5 + k, a * 8 + e] = weight

    def cell_row(g, s, depths):
        top_lanes = slice(g * LANES, (g + 1) * LANES)
        rest_lanes = slice(slots + g * LANES, slots + (g + 1) * LANES)
        sums = {}
        for a in range(8):
            for k in depths:
                at = a * 8 + (s - k)
                w_z = weights[g, 10 + k, at]
                w_y = [weights[g, 5 + j, at] if j != 2 else None for j in range(5)]
                for i in range(5):
                    plane = weights[g, i, at] * w_z
                    for j in range(5):
                        key = (a + i, j)
                        term = plane * w_y[j] if j != 2 else plane
                        sums[key] = sums[key] + term if key in sums else term
            for u in [a] if a < 7 else range(7, 12):
                rows = [sums[u, j] for j in range(5)]
                rows[2] = rows[2] - ((rows[0] + rows[1]) + (rows[3] + rows[4]))
                moved = [pltpu.roll(rows[j], j, 0) for j in range(1, 5)]
                every = rows[0] + ((moved[0] + moved[1]) + (moved[2] + moved[3]))
                past = [jnp.where(sub < j + 1, moved[j], 0.0) for j in range(4)]
                tail = (past[0] + past[1]) + (past[2] + past[3])
                top, rest = split(jnp.concatenate([every - tail, tail], 0), 2)
                out = slice((s * 12 + u) * 16, (s * 12 + u + 1) * 16)
                pieces[out, top_lanes] = top
                pieces[out, rest_lanes] = rest

    named = (labels[...] == lax.broadcasted_iota(jnp.int32, (windows, slots), 0)).astype(F32)
    named = jnp.transpose(named).astype(BF16)
    area = 12 * 16
    named = jnp.concatenate([named, named], 0)

    def gather(quad):
        summed = dot(pieces[quad * per * area : (quad + 1) * per * area, :], named)
        for wide in range(windows // LANES):
            lanes = slice(wide * LANES, (wide + 1) * LANES)
            part = [summed[k * area : (k + 1) * area, lanes] for k in range(per)]
            for t, item in enumerate(swap_groups(part, blocks_z)):
                rows = slice((wide * per + t) * area, (wide * per + t + 1) * area)
                grouped[0, quad, rows, :], grouped[1, quad, rows, :] = split(item, 2)

    for quad in range(12 // per):
        for s in range(quad * per, (quad + 1) * per):
            for g in range(slots // LANES):
                cell_row(g, s, [k for k in range(5) if 0 <= s - k < 8])
        if quad > 0:
            gather(quad - 1)
    gather(12 // per - 1)

    depth = 12 * blocks_z
    row = lax.broadcasted_iota(jnp.int32, (depth, cells_z), 0)
    wanted = (8 * (row % blocks_z) + row // blocks_z + cells_z - 2) % cells_z
    place = (wanted == lax.broadcasted_iota(jnp.int32, (depth, cells_z), 1)).astype(BF16)
    tile[...] = before[...] if last else jnp.zeros_like(tile)
    quads = depth // LANES
    left = jnp.concatenate([grouped[piece, quad] for piece in range(2) for quad in range(quads)], 1)
    total = dot(left, jnp.concatenate([place, place], 0))
    for bx in range(blocks_x):
        for by in range(blocks_y):
            at = (bx * blocks_y + by) * area
            rows = slice(bx * 8, bx * 8 + 12)
            cols = slice(by * 8, by * 8 + 16)
            tile[rows, cols, :] = tile[rows, cols, :] + total[at : at + area].reshape(12, 16, cells_z)

    if not last:
        core[...] = tile[...]
        return
    rows_x, rows_y = 8 * blocks_x, 8 * blocks_y
    core[...] = tile[2 : rows_x + 2, 2 : rows_y + 2, :]
    for side in range(2):
        x = side * (rows_x + 2)
        y = side * (rows_y + 2)
        x_rims[side] = tile[x : x + 2, 2 : rows_y + 2, :]
        y_rims[side] = tile[:, y : y + 2, :]


def corner_kernel(x_rims, y_low, y_top, out):
    rows_x, rows_y = y_low.shape[0] - 4, x_rims.shape[2]
    for side in range(2):
        x = side * (rows_x + 2)
        out[side] = x_rims[side]
        out[side, :, 0:2, :] = out[side, :, 0:2, :] + y_low[x : x + 2]
        out[side, :, rows_y - 2 :, :] = out[side, :, rows_y - 2 :, :] + y_top[x : x + 2]


def rim_kernel(core, y_low, y_top, x_low, x_top, out):
    rows_x, rows_y, _ = core.shape
    out[...] = core[...]
    for part, face in ((slice(0, 2), y_low), (slice(rows_y - 2, rows_y), y_top)):
        out[:, part, :] = out[:, part, :] + face[2 : rows_x + 2]
    for part, face in ((slice(0, 2), x_low), (slice(rows_x - 2, rows_x), x_top)):
        out[part] = out[part] + face[...]


def per_device(potential, owner, window):
    rows_x, rows_y, cells_z = potential.shape
    tiles_x, tiles_y = lax.axis_size("px"), lax.axis_size("py")
    tiles = tiles_x * tiles_y
    grid_x, grid_y = rows_x * tiles_x, rows_y * tiles_y
    planes = cells_z // tiles
    inner = rows_x * rows_y
    used = inner + -(-2 * (rows_x + rows_y) // LANES) * LANES
    blocks_x, blocks_y, blocks_z = rows_x // 8, rows_y // 8, cells_z // 8
    blocks = blocks_x * blocks_y * blocks_z
    half = max(2, 2 * blocks // tiles) // 2
    both = ("px", "py")

    def exchange(x):
        return lax.all_to_all(x, both, split_axis=0, concat_axis=0, tiled=True)

    slots, labels = call(
        functools.partial(slot_kernel, half, 2 * (rows_x + rows_y)),
        (shape(1, blocks, dtype=jnp.int32), shape(tiles, LANES)),
        [], 8, 2 * tiles * LANES * blocks, 8 * blocks,
    )(owner.reshape(blocks, 1), owner.reshape(1, blocks), window.reshape(1, blocks))

    line = shape(rows_x, cells_z)
    core, y_last, y_first = pl.pallas_call(
        prepare_kernel,
        out_shape=(shape(rows_x, rows_y, cells_z), line, line),
        in_specs=[FAR],
        out_specs=[VMEM] * 3,
        scratch_shapes=[pltpu.SemaphoreType.DMA],
        compiler_params=pltpu.CompilerParams(vmem_limit_bytes=8 << 20),
        cost_estimate=pl.CostEstimate(flops=0, bytes_accessed=2 << 20, transcendentals=0),
    )(potential)
    last_x = rows_x - 1
    y_faces = jnp.stack([send(y_last, "py", 1), send(y_first, "py", -1)])
    x_lines = [
        jnp.concatenate([y_faces[0, x : x + 1], core[x], y_faces[1, x : x + 1]])
        for x in (last_x, 0)
    ]
    x_faces = jnp.stack([send(x_lines[0], "px", 1), send(x_lines[1], "px", -1)])

    halves = shape(inner, cells_z, dtype=BF16)
    table = shape(cells_z, cells_z, dtype=BF16)
    step = 16
    *source, z_high, z_low = call(
        functools.partial(source_kernel, step), (halves, halves, table, table),
        [pltpu.VMEM((rows_x, rows_y + 16, cells_z), F32)],
        8, 60 * inner * cells_z, 2 << 20,
    )(core, y_faces)
    spectrum = call(
        spectrum_kernel, shape(cells_z, inner),
        [pltpu.VMEM((3, rows_y + 16, cells_z), F32)] + [pltpu.VMEM((inner, cells_z), BF16)] * 2,
        12, 6 * inner * cells_z**2, 2 << 20,
    )(core, y_faces, x_faces, *source, z_high, z_low)
    cells = pltpu.VMEM((used, cells_z), F32)
    width = -(-10 * blocks_z // LANES) * LANES
    sorted_table = shape(cells_z, width, dtype=BF16)
    *sorted_args, high, low = call(
        sort_kernel, (shape(width // LANES, used, LANES), sorted_table, sorted_table), [cells],
        10, 12 * used * cells_z**2, 2 << 20,
    )(core, x_faces, y_faces, z_high, z_low)
    sorted_tables = (high, low)

    span = tiles_y // 2
    length = span * rows_y
    halved = (
        2 * length == LANES and grid_x == LANES and planes == 8 and tiles_y == 8
        and 2 * (rows_x + rows_y) + 4 * half <= LANES
    )
    if halved:
        groups = [
            [i * tiles_y + g * span + j for i in range(tiles_x) for j in range(span)] for g in range(2)
        ]

        def exchange_half(x):
            return lax.all_to_all(x, both, 0, 0, axis_index_groups=groups, tiled=True)

        place_x, place_y = lax.axis_index("px"), lax.axis_index("py")
        own = (place_y // span).astype(jnp.int32).reshape(1)
        first = ((place_x * span + place_y % span) * 2 * planes).astype(jnp.int32).reshape(1)
        lap_z = laplace_of(cells_z)
        lap_x = np.broadcast_to(laplace_of(grid_x)[:, None], (grid_x, LANES))
        lap_xy = lap_x + np.tile(laplace_of(length), 2)[None, :]
        x_table = pieces_of(table_of(grid_x))
        y_table = pieces_of(np.kron(np.eye(2, dtype=np.float32), table_of(length)))
        square = shape(grid_x, LANES)
        cube = shape(planes, grid_x, LANES)
        slab = exchange_half(spectrum).reshape(tiles // 2, 2 * planes, inner)
        slab, *sorted_args, high, low = lax.optimization_barrier((slab, *sorted_args, high, low))
        sorted_tables = (high, low)
        tables = call(
            functools.partial(decay_kernel, length),
            (cube, cube, square, square, shape(LANES, 2 * planes * LANES, dtype=BF16)),
            [], 16, 100 * planes * grid_x * LANES, 2 << 20, 2,
        )(first, lap_z, lap_x)
        found, ends = call(
            functools.partial(
                half_kernel, tiles_x, span, rows_x, rows_y,
                SECOND_ORDER / (grid_x * length * cells_z), 2 * (rows_x + rows_y),
            ),
            (cube, square), [pltpu.VMEM((grid_x * planes, LANES), F32)],
            12, 12 * planes * grid_x**2 * LANES, 2 << 20, 2,
        )(first, lap_z, slab, labels, lap_xy, *x_table, *y_table)
        arrived_ends = lax.ppermute(ends, "py", [(j, (j + span) % tiles_y) for j in range(tiles_y)])
        returned = call(
            functools.partial(join_kernel, tiles_x, span, rows_x, rows_y, 2 * half),
            shape(tiles // 2, 2 * planes, used),
            [pltpu.VMEM((grid_x * planes, LANES), F32), pltpu.VMEM((LANES, grid_x), F32)],
            12, 12 * planes * grid_x**2 * LANES, 2 << 20, 2,
        )(first, own, found, ends, arrived_ends, labels, *tables, *x_table)
        modes = exchange_half(returned.reshape(cells_z, used))
    else:
        span = tiles_y
        own = jnp.zeros((1,), jnp.int32)
        slab = exchange(spectrum).reshape(tiles, planes, inner)
        scale = SECOND_ORDER / (grid_x * grid_y * cells_z)
        returned = solve_plain(slab, labels, rows_x, rows_y, cells_z, tiles_x, tiles_y, scale)
        modes = exchange(returned.reshape(cells_z, used))

    tile_args = (core, x_faces, y_faces, modes, z_high, z_low)
    sent, values, arrived_labels = call(
        functools.partial(block_kernel, rows_x, rows_y, cells_z // (tiles_x * span), half, tiles_y, span),
        (shape(blocks, ROWS), shape(ROWS, blocks), shape(2, 1, blocks, dtype=jnp.int32)),
        [pltpu.VMEM((width // LANES, used, LANES), F32)],
        12, 20 * used * cells_z**2, 6 << 20, 1,
    )(own, *sorted_args, modes, *sorted_tables, slots)
    first = exchange(sent)
    later = call(functools.partial(fill_slots, 1), shape(blocks, ROWS), [], 16, 6 * ROWS * blocks**2, 4 << 20)(values, slots)
    displacement = call(
        displacement_kernel, shape(3, rows_x, rows_y, cells_z),
        [pltpu.VMEM((rows_x, rows_y + 16, cells_z), F32), cells],
        16, 6 * used * cells_z**2, 4 << 20,
    )(*tile_args)

    later, displacement = lax.optimization_barrier((later, displacement))
    arrived = first, exchange(later)
    tile_shape = (rows_x + 4, rows_y + 8, cells_z)
    scratch = [
        pltpu.VMEM((blocks // LANES, ROWS, LANES), F32),
        pltpu.VMEM((blocks // LANES, 15, 64, 8, LANES), F32),
        pltpu.VMEM((12 * 12 * 16, 2 * blocks), BF16),
        pltpu.VMEM((2, 12 * blocks_z // LANES, blocks_x * blocks_y * 12 * 16, LANES), BF16),
        pltpu.VMEM(tile_shape, F32),
    ]
    sizes = (blocks_x, blocks_y, blocks_z)
    cost = (300 * blocks * 512, 4 << 20)
    tile = call(
        functools.partial(deposit_kernel, *sizes, False), shape(*tile_shape), scratch, 32, *cost
    )(arrived[0], arrived_labels[0])
    middle, x_rims, y_rims = call(
        functools.partial(deposit_kernel, *sizes, True),
        (
            shape(rows_x, rows_y, cells_z), shape(2, 2, rows_y, cells_z),
            shape(2, rows_x + 4, 2, cells_z),
        ),
        scratch, 32, *cost,
    )(arrived[1], arrived_labels[1], tile)

    y_sides = send(y_rims[1], "py", 1), send(y_rims[0], "py", -1)
    x_rims = call(corner_kernel, shape(*x_rims.shape), [], 4, 8 * rows_y * cells_z, 1 << 17)(
        x_rims, *y_sides
    )
    x_sides = send(x_rims[1], "px", 1), send(x_rims[0], "px", -1)
    density = call(rim_kernel, shape(rows_x, rows_y, cells_z), [], 8, inner * cells_z, 2 << 20)(
        middle, *y_sides, *x_sides
    )
    return (displacement, density)


def solution(mesh):
    return jax.shard_map(
        per_device,
        mesh=mesh,
        in_specs=(P("px", "py", None), P("px", "py", None, None), P("px", "py", None)),
        out_specs=(P(None, "px", "py", None), P("px", "py", None)),
        check_vma=False,
    )
```

```python
import functools
import math

import jax
import jax.numpy as jnp
import numpy as np
from jax import lax
from jax.experimental import pallas as pl
from jax.experimental.pallas import tpu as pltpu
from jax.sharding import PartitionSpec as P

SECOND_ORDER = 3.0 / 7.0
F32 = jnp.float32
BF16 = jnp.bfloat16
LANES = 128
ROWS = 896
VMEM = pl.BlockSpec(memory_space=pltpu.VMEM)
SMEM = pl.BlockSpec(memory_space=pltpu.SMEM)
FAR = pl.BlockSpec(memory_space=pltpu.HBM)
NN = (((1,), (0,)), ((), ()))
NT = (((1,), (1,)), ((), ()))
TN = (((0,), (0,)), ((), ()))


def split(x, pieces):
    out = []
    for piece in range(pieces):
        part = x.astype(BF16)
        out.append(part)
        if piece < pieces - 1:
            x = x - part.astype(F32)
    return out


def dot(a, b, dims=NN):
    return lax.dot_general(a, b, dims, preferred_element_type=F32)


def dot3(a, b, dims=NN):
    return dot(a[0], b[0], dims) + (dot(a[0], b[1], dims) + dot(a[1], b[0], dims))


def swap_groups(rows, group):
    rows = list(rows)
    count = len(rows)
    axis = rows[0].ndim - 1
    lane = lax.broadcasted_iota(jnp.int32, rows[0].shape, axis) // group
    step = 1
    while step < count:
        low = (lane & step) == 0
        for k in range(count):
            if k & step:
                continue
            a, b = rows[k], rows[k + step]
            rows[k] = jnp.where(low, a, pltpu.roll(b, step * group, axis))
            rows[k + step] = jnp.where(low, pltpu.roll(a, LANES - step * group, axis), b)
        step *= 2
    return rows


def table_of(length):
    modes = np.arange(length)
    angle = (modes[:, None] * modes[None, :] % length) * (2.0 * math.pi / length)
    return (np.cos(angle) + np.sin(angle)).astype(np.float32)


def pieces_of(table):
    high = table.astype(jnp.bfloat16)
    low = (table - high.astype(np.float32)).astype(jnp.bfloat16)
    return np.asarray(high), np.asarray(low)


def laplace_of(length):
    return (2.0 * np.cos(np.arange(length) * (2.0 * math.pi / length)) - 2.0).astype(np.float32)


def call(body, outs, scratch, vmem, flops, moved, scalars=0):
    def run(*operands):
        return pl.pallas_call(
            body,
            out_shape=outs,
            in_specs=[SMEM] * scalars + [VMEM] * (len(operands) - scalars),
            out_specs=jax.tree.map(lambda _: VMEM, outs),
            scratch_shapes=scratch,
            compiler_params=pltpu.CompilerParams(vmem_limit_bytes=vmem << 20),
            cost_estimate=pl.CostEstimate(flops=flops, bytes_accessed=moved, transcendentals=0),
        )(*operands)

    return run


def shape(*dims, dtype=F32):
    return jax.ShapeDtypeStruct(dims, dtype)


def send(x, axis, step):
    size = lax.axis_size(axis)
    return lax.ppermute(x, axis, [(i, (i + step) % size) for i in range(size)])


def slot_kernel(half, start, owner_col, owner_row, window_row, slot_out, label_out):
    count = owner_row.shape[1]
    tiles = label_out.shape[0]
    later = lax.broadcasted_iota(jnp.int32, (count, count), 0) < lax.broadcasted_iota(
        jnp.int32, (count, count), 1
    )
    owners = owner_row[...]
    same = (owner_col[...] == owners) & later
    rank = jnp.sum(same.astype(F32), axis=0, keepdims=True).astype(jnp.int32)
    second = rank >= half
    place = owners * half + jnp.where(second, rank - half, rank)
    slot_out[...] = jnp.where(second, place + count, place)
    tile = lax.broadcasted_iota(jnp.int32, (tiles, count), 0)
    named = jnp.where(tile == owners, window_row[...] + 1, 0).astype(F32).astype(BF16)
    lane = lax.broadcasted_iota(jnp.int32, (LANES, count), 0)
    label_out[...] = dot(named, (lane == rank + start).astype(BF16), NT) - 1.0


def source_of(at, cells_z):
    def ahead(value):
        return pltpu.roll(value, cells_z - 1, 1)

    def behind(value):
        return pltpu.roll(value, 1, 1)

    here = at(0, 0)
    ahead_x, behind_x, ahead_y, behind_y = at(1, 0), at(-1, 0), at(0, 1), at(0, -1)
    xx = ahead_x - 2.0 * here + behind_x
    yy = ahead_y - 2.0 * here + behind_y
    zz = ahead(here) - 2.0 * here + behind(here)
    xy = (at(1, 1) - at(1, -1) - at(-1, 1) + at(-1, -1)) * 0.25
    across_x, across_y = ahead_x - behind_x, ahead_y - behind_y
    xz = (ahead(across_x) - behind(across_x)) * 0.25
    yz = (ahead(across_y) - behind(across_y)) * 0.25
    return xx * yy + xx * zz + yy * zz - xy * xy - xz * xz - yz * yz


def prepare_kernel(potential, core, y_last, y_first, sem):
    copy = pltpu.make_async_copy(potential, core, sem)
    copy.start()
    copy.wait()
    rows_x, rows_y, _ = core.shape
    for x in range(rows_x):
        y_last[x : x + 1, :] = core[x, rows_y - 1 : rows_y, :]
        y_first[x : x + 1, :] = core[x, 0:1, :]


def source_kernel(step, core, y_faces, high, low, table_high, table_low, pad):
    rows_x, rows_y, cells_z = core.shape
    coarse = cells_z // step

    def turns(count, stride):
        row = lax.broadcasted_iota(jnp.int32, (count, cells_z), 0) * stride
        col = lax.broadcasted_iota(jnp.int32, (count, cells_z), 1)
        angle = (row * col % cells_z).astype(F32) * (2.0 * math.pi / cells_z)
        return jnp.cos(angle), jnp.sin(angle)

    wide_cos, wide_sin = turns(coarse, step)
    fine_cos, fine_sin = turns(step, 1)
    fine, turned = fine_cos + fine_sin, fine_cos - fine_sin
    for k in range(coarse):
        rows = slice(k * step, (k + 1) * step)
        value = wide_cos[k : k + 1] * fine + wide_sin[k : k + 1] * turned
        table_high[rows, :], table_low[rows, :] = split(value, 2)
    pad[:, 8 : rows_y + 8, :] = core[...]
    for x in range(rows_x):
        pad[x, 7:8, :] = y_faces[0, x : x + 1, :]
        pad[x, rows_y + 8 : rows_y + 9, :] = y_faces[1, x : x + 1, :]

    @pl.loop(1, rows_x - 1, unroll=3)
    def _(x):
        def at(dx, dy):
            return pad[x + dx, 8 + dy : 8 + dy + rows_y, :]

        rows = pl.ds(pl.multiple_of(x * rows_y, rows_y), rows_y)
        high[rows, :], low[rows, :] = split(source_of(at, cells_z), 2)

    for x in (0, rows_x - 1):
        rows = slice(x * rows_y, (x + 1) * rows_y)
        high[rows, :] = jnp.zeros((rows_y, cells_z), BF16)
        low[rows, :] = jnp.zeros((rows_y, cells_z), BF16)


def spectrum_kernel(core, y_faces, x_faces, inner_high, inner_low, high, low, spectrum, pad, source_high, source_low):
    rows_x, rows_y, cells_z = core.shape
    source_high[...] = inner_high[...]
    source_low[...] = inner_low[...]
    for side in range(2):
        edge = side * (rows_x - 1)
        for line in range(3):
            x = edge + line - 1
            if 0 <= x < rows_x:
                pad[line, 8 : rows_y + 8, :] = core[x]
                pad[line, 7:8, :] = y_faces[0, x : x + 1, :]
                pad[line, rows_y + 8 : rows_y + 9, :] = y_faces[1, x : x + 1, :]
            else:
                pad[line, 7 : rows_y + 9, :] = x_faces[side]

        def at(dx, dy):
            return pad[1 + dx, 8 + dy : 8 + dy + rows_y, :]

        rows = slice(edge * rows_y, (edge + 1) * rows_y)
        source_high[rows, :], source_low[rows, :] = split(source_of(at, cells_z), 2)
    spectrum[...] = dot3((high[...], low[...]), (source_high[...], source_low[...]), NT)


def stacked(pieces):
    high, low = pieces
    return jnp.concatenate(
        [jnp.concatenate([high, low], 1), jnp.concatenate([high, jnp.zeros_like(high)], 1)], 0
    )


def joined(value):
    width = value.shape[1] // 2
    return value[:, :width] + value[:, width:]


def placed(pieces, choose):
    return dot(pieces[0], choose) + dot(pieces[1], choose) + dot(pieces[2], choose)


def iota(dims, axis):
    return lax.broadcasted_iota(jnp.int32, dims, axis)


def decay(w, length):
    grow = w + jnp.sqrt(w * (w + 2.0))
    rate = jnp.log(1.0 + grow)
    ratio = 1.0 / (1.0 + grow)
    both = (1.0 + grow) + jnp.exp(-rate * (length - 1.0))
    flat = w <= 0.0
    return rate, 2.0 * (1.0 + ratio) * both, 2.0 * jnp.where(flat, 1.0, grow * ratio * both), flat


def decay_kernel(length, first, lap_z, lap_x, even, odd, edge_even, edge_odd, spread):
    count = even.shape[0]
    dims = even.shape[1:]
    lane = iota(dims, 1)
    group = lane // length
    y = (lane % length).astype(F32)
    start = first[0]
    for q in range(count):
        along_z = jnp.where(group == 0, lap_z[start + q], lap_z[start + count + q])
        rate, plus, minus, flat = decay(-0.5 * (lap_x[...] + along_z), length)
        rise, fall = jnp.exp(-rate * y), jnp.exp(-rate * (length - 1.0 - y))
        even[q] = (rise + fall) / plus
        odd[q] = jnp.where(flat, 0.25 * (length - 1.0) - 0.5 * y, (rise - fall) / minus)
    along_z = jnp.zeros(dims, F32)
    for q in range(count):
        for g in range(2):
            along_z = jnp.where(lane // 2 == 2 * q + g, lap_z[start + g * count + q], along_z)
    rate, plus, minus, flat = decay(-0.5 * (lap_x[...] + along_z), length)
    last = jnp.exp(-rate * (length - 1.0))
    edge_even[...] = (1.0 + last) / plus
    edge_odd[...] = jnp.where(flat, 0.25 * (length - 1.0), (1.0 - last) / minus)
    dims = spread.shape
    col = iota(dims, 1)
    row = iota(dims, 0)
    hit = row // 2 == 2 * (col // (2 * LANES)) + col % LANES // length
    sign = jnp.where((col // LANES % 2 == 1) & (row % 2 == 0), -1.0, 1.0)
    spread[...] = jnp.where(hit, sign, 0.0).astype(BF16)


def half_kernel(
    tiles_x, tiles_y, rows_x, rows_y, scale, mark,
    first, lap_z, slab, labels, lap_xy, hx_high, hx_low, hy_high, hy_low,
    found, ends, sent, planes,
):
    grid_x = tiles_x * rows_x
    count = slab.shape[1] // 2
    length = tiles_y * rows_y
    per = LANES // rows_y
    along_y = stacked((hy_high[...], hy_low[...]))
    along_x = jnp.concatenate([hx_high[...], hx_low[...]], 1)

    def times_y(value):
        return joined(dot(jnp.concatenate(split(value, 2), 1), along_y))

    for i in range(tiles_x):
        for part in range(rows_x // per):
            lanes = slice(part * LANES, (part + 1) * LANES)
            rows = [
                slab[i * tiles_y + j, g * count : (g + 1) * count, lanes]
                for g in range(2)
                for j in range(tiles_y)
            ]
            x = (i * rows_x + part * per) * count
            planes[x : x + per * count, :] = times_y(jnp.concatenate(swap_groups(rows, rows_y), 0))
    dims = (grid_x, LANES)
    lane, row = iota(dims, 1), iota(dims, 0)
    block = jnp.zeros(dims, F32)
    for q in range(count):
        modes = joined(dot(along_x, stacked(split(planes[pl.ds(q, grid_x, stride=count), :], 2))))
        eigen = lap_xy[...] + jnp.where(lane < length, lap_z[first[0] + q], lap_z[first[0] + count + q])
        anchor = eigen == 0.0
        value = times_y(jnp.where(anchor, 0.0, scale / jnp.where(anchor, -1.0, eigen)) * modes)
        found[q] = value
        source = lane - 4 * q
        source = source // 2 * length + source % 2 * (length - 1)
        choose = (row == source) & (lane >= 4 * q) & (lane < 4 * q + 4)
        block = block + placed(split(value, 3), choose.astype(BF16))
        if q == 0:
            mean = pltpu.roll(modes * scale, 4 * count, 1)
            block = block + jnp.where((row == 0) & (lane == 4 * count), mean, 0.0)
    ends[...] = block
    tiles = labels.shape[0]
    ends[0:tiles, :] = jnp.where(lane[0:tiles] < mark, block[0:tiles], labels[...])
    turned = jnp.transpose(ends[...])
    used = 4 * count + 8
    sent[0:used, :] = turned[0:used]
    sent[used:, :] = turned[mark : mark + sent.shape[0] - used]


def join_kernel(
    tiles_x, tiles_y, rows_x, rows_y, places,
    first, half, found, ends, received, labels, even, odd, edge_even, edge_odd, spread, hx_high, hx_low,
    out, planes, faces, arrived,
):
    grid_x = tiles_x * rows_x
    count = found.shape[0]
    length = tiles_y * rows_y
    per = LANES // rows_y
    along_x = jnp.concatenate([hx_high[...], hx_low[...]], 1)

    def times_x(value):
        return joined(dot(along_x, stacked(split(value, 2))))

    dims = (grid_x, LANES)
    lane, row = iota(dims, 1), iota(dims, 0)
    used = 4 * count + 8
    mark = 2 * (rows_x + rows_y)
    gap = jnp.zeros((mark - used, LANES), F32)
    rest = jnp.zeros((LANES - mark - received.shape[0] + used, LANES), F32)
    arrived[...] = jnp.transpose(
        jnp.concatenate([received[0:used, :], gap, received[used:, :], rest], 0)
    )
    jump = jnp.where(lane < 4 * count + 1, arrived[...] - ends[...], 0.0)
    pieces = split(jump, 2)
    wide = dot(pieces[0], spread[...]) + dot(pieces[1], spread[...])
    mean = jnp.where(first[0] == 0, -0.5 * jump[0:1, 4 * count : 4 * count + 1], 0.0)
    y = lane.astype(F32)
    bend = jnp.where(
        (row == 0) & (lane < length),
        mean * (0.5 * y * y - 0.5 * (length - 1.0) * y - 0.25 * length),
        0.0,
    )
    target = iota((LANES, LANES), 1)
    source = iota((LANES, LANES), 0)
    side, j, group = target // 8 % 2, target // 2 % tiles_y, target % 2
    inside = ((side == 0) & (j > 0)) | ((side == 1) & (j < tiles_y - 1))
    wanted = group * length + jnp.where(side == 0, j * rows_y - 1, (j + 1) * rows_y)
    lines = jnp.zeros(dims, F32)
    for q in range(count):
        at = 2 * q * LANES
        value = found[q] + (wide[:, at : at + LANES] * even[q] + wide[:, at + LANES : at + 2 * LANES] * odd[q])
        if q == 0:
            value = value + bend
        choose = inside & (source == wanted) & (target // 16 == q)
        lines = lines + placed(split(value, 3), choose.astype(BF16))
        planes[pl.ds(q, grid_x, stride=count), :] = times_x(value)
    low = lane % 2 == 0
    other = jnp.where(low, pltpu.roll(jump, LANES - 1, 1), pltpu.roll(jump, 1, 1))
    change = (jump + other) * edge_even[...] + (other - jump) * edge_odd[...]
    change = change + jnp.where((row == 0) & (lane < 2), -0.25 * length * mean, 0.0)
    beyond = jnp.where(lane < 4 * count, arrived[...] - change, 0.0)
    first_side = source % 2 == 1
    goal = source // 4 * 16 + source // 2 % 2 + jnp.where(first_side, 0, 8 + 2 * (tiles_y - 1))
    choose = (target == goal) & (source < 4 * count)
    lines = lines + placed(split(beyond, 3), choose.astype(BF16))
    faces[...] = jnp.transpose(times_x(lines))

    def row_of(x):
        x = x % grid_x
        return planes[x * count : (x + 1) * count, :]

    lane = iota((count, LANES), 1)
    for i in range(tiles_x):
        for part in range(rows_x // per):
            lanes = slice(part * LANES, (part + 1) * LANES)
            rows = [row_of(i * rows_x + part * per + t) for t in range(per)]
            for k, item in enumerate(swap_groups(rows, rows_y)):
                g, j = k // tiles_y, k % tiles_y
                out[i * tiles_y + j, g * count : (g + 1) * count, lanes] = item
        before, after = row_of(i * rows_x - 1), row_of((i + 1) * rows_x)
        for k in range(per):
            g, j = k // tiles_y, k % tiles_y
            shift = (LANES - k * rows_y) % LANES
            line = pltpu.roll(before, shift, 1) if shift else before
            moved = pltpu.roll(after, (shift + rows_y) % LANES, 1)
            line = jnp.where(lane < rows_y, line, moved)
            for side in range(2):
                face = faces[pl.ds(side * 8 + j * 2 + g, count, stride=16), :]
                start = 2 * rows_y + side * rows_x
                move = (start - i * rows_x) % LANES
                face = pltpu.roll(face, move, 1) if move else face
                line = jnp.where(lane < start, line, face)
            start = 2 * (rows_x + rows_y)
            tile = (2 * i + half[0]) * tiles_y + j
            own, partner = labels[pl.ds(tile, 1), :], pltpu.roll(arrived[pl.ds(tile, 1), :], places, 1)
            line = jnp.where(lane < start, line, jnp.where(lane < start + places, own, partner))
            out[i * tiles_y + j, g * count : (g + 1) * count, rows_x * rows_y : rows_x * rows_y + LANES] = line


def solve_plain(slab, labels, rows_x, rows_y, cells_z, tiles_x, tiles_y, scale):
    high = lax.Precision.HIGHEST
    grid_x, grid_y = tiles_x * rows_x, tiles_y * rows_y
    count = slab.shape[1]
    hx, hy = jnp.asarray(table_of(grid_x)), jnp.asarray(table_of(grid_y))
    planes = slab.reshape(tiles_x, tiles_y, count, rows_x, rows_y).transpose(2, 0, 3, 1, 4)
    planes = planes.reshape(count, grid_x, grid_y)
    modes = jnp.einsum("qxy,xk,yl->qkl", planes, hx, hy, precision=high)
    first = lax.axis_index(("px", "py")) * count
    lap_z = lax.dynamic_slice_in_dim(jnp.asarray(laplace_of(cells_z)), first, count)
    eigen = (
        jnp.asarray(laplace_of(grid_x))[None, :, None]
        + jnp.asarray(laplace_of(grid_y))[None, None, :]
        + lap_z[:, None, None]
    )
    anchor = eigen == 0.0
    solved = jnp.where(anchor, 0.0, scale / jnp.where(anchor, -1.0, eigen)) * modes
    back = jnp.einsum("qkl,xk,yl->qxy", solved, hx, hy, precision=high)
    tiles = back.reshape(count, tiles_x, rows_x, tiles_y, rows_y).transpose(1, 3, 0, 2, 4)
    starts_x, starts_y = np.arange(tiles_x) * rows_x, np.arange(tiles_y) * rows_y
    faces = []
    for edge in (-1, rows_x):
        line = back[:, (starts_x + edge) % grid_x].reshape(count, tiles_x, tiles_y, rows_y)
        faces.append(line.transpose(1, 2, 0, 3))
    for edge in (-1, rows_y):
        line = back[:, :, (starts_y + edge) % grid_y].reshape(count, tiles_x, rows_x, tiles_y)
        faces.append(line.transpose(1, 3, 0, 2))
    tail = labels[:, 2 * (rows_x + rows_y) :].reshape(tiles_x, tiles_y, 1, -1)
    faces.append(jnp.broadcast_to(tail, (tiles_x, tiles_y, count, tail.shape[-1])))
    parts = [tiles.reshape(tiles_x, tiles_y, count, rows_x * rows_y)] + faces
    return jnp.concatenate(parts, -1).reshape(tiles_x * tiles_y, count, -1)


def combine(core, x_faces, y_faces, spectrum, high, low, cells):
    rows_x, rows_y, cells_z = core.shape
    inner = rows_x * rows_y
    cells[...] = dot3(split(spectrum[...], 2), (high[...], low[...]), TN)
    cells[0:inner, :] = cells[0:inner, :] + core[...].reshape(inner, cells_z)
    start = inner
    for faces, skip in ((x_faces, 1), (y_faces, 0)):
        for side in range(2):
            length = faces.shape[1] - 2 * skip
            rows = slice(start, start + length)
            cells[rows, :] = cells[rows, :] + faces[side, skip : skip + length, :]
            start += length
    return edges_of(rows_x, rows_y)


def displacement_kernel(core, x_faces, y_faces, spectrum, high, low, displacement, pad, cells):
    rows_x, rows_y, cells_z = core.shape
    x_edge, y_edge = combine(core, x_faces, y_faces, spectrum, high, low, cells)
    for x in range(rows_x):
        pad[x, 8 : rows_y + 8, :] = cells[x * rows_y : (x + 1) * rows_y, :]
        pad[x, 7:8, :] = cells[y_edge[0] + x : y_edge[0] + x + 1, :]
        pad[x, rows_y + 8 : rows_y + 9, :] = cells[y_edge[1] + x : y_edge[1] + x + 1, :]

    def line(x):
        if x < 0:
            return cells[x_edge[0] : x_edge[0] + rows_y, :]
        if x >= rows_x:
            return cells[x_edge[1] : x_edge[1] + rows_y, :]
        return cells[x * rows_y : (x + 1) * rows_y, :]

    for x in range(rows_x):
        here = line(x)
        displacement[0, x] = (line(x - 1) - line(x + 1)) * 0.5
        displacement[1, x] = (pad[x, 7 : rows_y + 7, :] - pad[x, 9 : rows_y + 9, :]) * 0.5
        displacement[2, x] = (pltpu.roll(here, 1, 1) - pltpu.roll(here, cells_z - 1, 1)) * 0.5


def edges_of(rows_x, rows_y):
    inner = rows_x * rows_y
    return [inner, inner + rows_y], [inner + 2 * rows_y, inner + 2 * rows_y + rows_x]


def sort_kernel(core, x_faces, y_faces, high, low, spread, sorted_high, sorted_low, cells):
    rows_x, rows_y, cells_z = core.shape
    blocks_z = cells_z // 8
    inner = rows_x * rows_y
    x_edge, y_edge = edges_of(rows_x, rows_y)
    cells[0:inner, :] = core[...].reshape(inner, cells_z)
    for side in range(2):
        cells[x_edge[side] : x_edge[side] + rows_y, :] = x_faces[side, 1 : rows_y + 1, :]
        cells[y_edge[side] : y_edge[side] + rows_x, :] = y_faces[side]
    used = y_edge[1] + rows_x
    cells[used:, :] = jnp.zeros((cells.shape[0] - used, cells_z), F32)
    width = sorted_high.shape[1]
    col = lax.broadcasted_iota(jnp.int32, (cells_z, width), 1)
    wanted = (8 * (col % blocks_z) + col // blocks_z + cells_z - 1) % cells_z
    choose = (wanted == lax.broadcasted_iota(jnp.int32, (cells_z, width), 0)).astype(BF16)
    pieces = split(cells[...], 3)
    moved = dot(pieces[0], choose) + dot(pieces[1], choose) + dot(pieces[2], choose)
    for quad in range(spread.shape[0]):
        spread[quad] = moved[:, quad * LANES : (quad + 1) * LANES]
    sorted_high[...] = dot(high[...], choose).astype(BF16)
    sorted_low[...] = dot(low[...], choose).astype(BF16)


def block_kernel(
    rows_x, rows_y, planes, half, tiles_y, span, own, potential, spectrum, high, low, slots,
    out, values, labels,
    spread,
):
    cells_z = spectrum.shape[0]
    inner = rows_x * rows_y
    blocks_x, blocks_y, blocks_z = rows_x // 8, rows_y // 8, cells_z // 8
    per = LANES // blocks_z
    x_edge, y_edge = edges_of(rows_x, rows_y)
    width = high.shape[1]
    second = dot3(split(spectrum[...], 2), (high[...], low[...]), TN)
    for quad in range(width // LANES):
        spread[quad] = potential[quad] + second[:, quad * LANES : (quad + 1) * LANES]

    def put(row, tiles):
        for quad in range(width // LANES):
            every = [tiles(b // blocks_y, b % blocks_y, quad) for b in range(blocks_x * blocks_y)]
            for block in range(0, len(every), per):
                for k, item in enumerate(swap_groups(every[block : block + per], blocks_z)):
                    where = row(quad * per + k - 1)
                    if where is not None:
                        start = block * blocks_z
                        values[where : where + 8, start : start + LANES] = item

    def x_tile(a):
        def tile(bx, by, quad):
            x = 8 * bx + a
            top = x_edge[0] if x < 0 else x_edge[1] if x >= rows_x else x * rows_y
            return spread[quad, top + 8 * by : top + 8 * by + 8, :]

        return tile

    for a in range(-1, 9):
        def row(e, a=a):
            if 0 <= e < 8:
                return ((a + 1) * 8 + e) * 8
            if e in (-1, 8) and 0 <= a < 8:
                return 640 + (64 if e == 8 else 0) + a * 8
            return None

        put(row, x_tile(a))
    for side, edge in enumerate((-1, 8)):
        def tile(bx, by, quad, edge=edge):
            y = 8 * by + edge
            if y < 0 or y >= rows_y:
                top = y_edge[0 if y < 0 else 1] + 8 * bx
                return spread[quad, top : top + 8, :]
            return spread[quad, pl.ds(8 * bx * rows_y + y, 8, stride=rows_y), :]

        put(lambda e, side=side: 768 + side * 64 + e * 8 if 0 <= e < 8 else None, tile)

    count = slots.shape[1]
    named = spectrum[:, inner : inner + LANES].astype(BF16)
    row = lax.broadcasted_iota(jnp.int32, (cells_z, count), 0)
    slot = lax.broadcasted_iota(jnp.int32, (cells_z, count), 1)
    tile = slot // half
    member = tile // tiles_y * span + tile % span
    source = (row % planes == 0) & (row // planes == member)
    by_lane = dot(named, source.astype(BF16), TN)
    dims = (LANES, count)
    slot = iota(dims, 1)
    moved = jnp.where(slot // half % tiles_y // span == own[0], 0, 2 * half)
    lane = iota(dims, 0) - 2 * (rows_x + rows_y) - moved
    place = slot % half
    for part in range(2):
        label = jnp.sum(jnp.where(lane == place + part * half, by_lane, 0.0), axis=0, keepdims=True)
        labels[part] = label.astype(jnp.int32)

    fill_slots(0, values, slots, out)


def fill_slots(part, values, slots, out):
    count = slots.shape[1]
    pieces = split(values[...], 3)
    number = lax.broadcasted_iota(jnp.int32, (count, count), 0) + part * count
    chosen = (slots[...] == number).astype(BF16)
    out[...] = dot(chosen, pieces[0], NT) + dot(chosen, pieces[1], NT) + dot(chosen, pieces[2], NT)


def spline(shift):
    g = jnp.abs(shift)
    h = 1.0 - g
    gg, hh = g * g, h * h
    near = (2.0 / 3.0) - gg + 0.5 * gg * g
    ahead = (2.0 / 3.0) - hh + 0.5 * hh * h
    back = hh * h * (1.0 / 6.0)
    far = gg * g * (1.0 / 6.0)
    up = shift >= 0.0
    zero = jnp.zeros_like(far)
    return (
        jnp.where(up, zero, far),
        jnp.where(up, back, ahead),
        near,
        jnp.where(up, ahead, back),
        jnp.where(up, far, zero),
    )


def deposit_kernel(blocks_x, blocks_y, blocks_z, last, blocks, labels, *refs):
    if last:
        before, core, x_rims, y_rims, turned, weights, pieces, grouped, tile = refs
    else:
        core, turned, weights, pieces, grouped, tile = refs
    slots = blocks.shape[0]
    cells_z = 8 * blocks_z
    per = LANES // blocks_z
    windows = blocks_x * blocks_y * blocks_z
    sub = lax.broadcasted_iota(jnp.int32, (8, LANES), 0)
    for g in range(slots // LANES):
        turned[g] = jnp.transpose(blocks[g * LANES : (g + 1) * LANES, :])

    @pl.loop(0, slots // LANES)
    def _(g):
        def rows(start):
            return turned[g, pl.ds(pl.multiple_of(start, 8), 8), :]

        @pl.loop(0, 8)
        def _(a):
            for e in range(8):
                here = rows((a + 1) * 64 + e * 8)
                x_diff = rows(a * 64 + e * 8) - rows((a + 2) * 64 + e * 8)
                z_low = rows((a + 1) * 64 + e * 8 - 8) if e > 0 else rows(640 + a * 8)
                z_top = rows((a + 1) * 64 + e * 8 + 8) if e < 7 else rows(704 + a * 8)
                y_low = jnp.where(
                    sub == 0, turned[g, pl.ds(768 + e * 8 + a, 1), :], pltpu.roll(here, 1, 0)
                )
                y_top = jnp.where(
                    sub == 7, turned[g, pl.ds(832 + e * 8 + a, 1), :], pltpu.roll(here, 7, 0)
                )
                for axis, diff in enumerate((x_diff, y_low - y_top, z_low - z_top)):
                    for k, weight in enumerate(spline(jnp.clip(diff * 0.5, -1.0, 1.0))):
                        if (axis, k) != (1, 2):
                            weights[g, axis * 5 + k, a * 8 + e] = weight

    def cell_row(g, s, depths):
        top_lanes = slice(g * LANES, (g + 1) * LANES)
        rest_lanes = slice(slots + g * LANES, slots + (g + 1) * LANES)
        sums = {}
        for a in range(8):
            for k in depths:
                at = a * 8 + (s - k)
                w_z = weights[g, 10 + k, at]
                w_y = [weights[g, 5 + j, at] if j != 2 else None for j in range(5)]
                for i in range(5):
                    plane = weights[g, i, at] * w_z
                    for j in range(5):
                        key = (a + i, j)
                        term = plane * w_y[j] if j != 2 else plane
                        sums[key] = sums[key] + term if key in sums else term
            for u in [a] if a < 7 else range(7, 12):
                rows = [sums[u, j] for j in range(5)]
                rows[2] = rows[2] - ((rows[0] + rows[1]) + (rows[3] + rows[4]))
                moved = [pltpu.roll(rows[j], j, 0) for j in range(1, 5)]
                every = rows[0] + ((moved[0] + moved[1]) + (moved[2] + moved[3]))
                past = [jnp.where(sub < j + 1, moved[j], 0.0) for j in range(4)]
                tail = (past[0] + past[1]) + (past[2] + past[3])
                top, rest = split(jnp.concatenate([every - tail, tail], 0), 2)
                out = slice((s * 12 + u) * 16, (s * 12 + u + 1) * 16)
                pieces[out, top_lanes] = top
                pieces[out, rest_lanes] = rest

    named = (labels[...] == lax.broadcasted_iota(jnp.int32, (windows, slots), 0)).astype(F32)
    named = jnp.transpose(named).astype(BF16)
    area = 12 * 16
    named = jnp.concatenate([named, named], 0)

    def gather(quad):
        summed = dot(pieces[quad * per * area : (quad + 1) * per * area, :], named)
        for wide in range(windows // LANES):
            lanes = slice(wide * LANES, (wide + 1) * LANES)
            part = [summed[k * area : (k + 1) * area, lanes] for k in range(per)]
            for t, item in enumerate(swap_groups(part, blocks_z)):
                rows = slice((wide * per + t) * area, (wide * per + t + 1) * area)
                grouped[0, quad, rows, :], grouped[1, quad, rows, :] = split(item, 2)

    for quad in range(12 // per):
        for s in range(quad * per, (quad + 1) * per):
            for g in range(slots // LANES):
                cell_row(g, s, [k for k in range(5) if 0 <= s - k < 8])
        if quad > 0:
            gather(quad - 1)
    gather(12 // per - 1)

    depth = 12 * blocks_z
    row = lax.broadcasted_iota(jnp.int32, (depth, cells_z), 0)
    wanted = (8 * (row % blocks_z) + row // blocks_z + cells_z - 2) % cells_z
    place = (wanted == lax.broadcasted_iota(jnp.int32, (depth, cells_z), 1)).astype(BF16)
    tile[...] = before[...] if last else jnp.zeros_like(tile)
    quads = depth // LANES
    left = jnp.concatenate([grouped[piece, quad] for piece in range(2) for quad in range(quads)], 1)
    total = dot(left, jnp.concatenate([place, place], 0))
    for bx in range(blocks_x):
        for by in range(blocks_y):
            at = (bx * blocks_y + by) * area
            rows = slice(bx * 8, bx * 8 + 12)
            cols = slice(by * 8, by * 8 + 16)
            tile[rows, cols, :] = tile[rows, cols, :] + total[at : at + area].reshape(12, 16, cells_z)

    if not last:
        core[...] = tile[...]
        return
    rows_x, rows_y = 8 * blocks_x, 8 * blocks_y
    core[...] = tile[2 : rows_x + 2, 2 : rows_y + 2, :]
    for side in range(2):
        x = side * (rows_x + 2)
        y = side * (rows_y + 2)
        x_rims[side] = tile[x : x + 2, 2 : rows_y + 2, :]
        y_rims[side] = tile[:, y : y + 2, :]


def corner_kernel(x_rims, y_low, y_top, out):
    rows_x, rows_y = y_low.shape[0] - 4, x_rims.shape[2]
    for side in range(2):
        x = side * (rows_x + 2)
        out[side] = x_rims[side]
        out[side, :, 0:2, :] = out[side, :, 0:2, :] + y_low[x : x + 2]
        out[side, :, rows_y - 2 :, :] = out[side, :, rows_y - 2 :, :] + y_top[x : x + 2]


def rim_kernel(core, y_low, y_top, x_low, x_top, out):
    rows_x, rows_y, _ = core.shape
    out[...] = core[...]
    for part, face in ((slice(0, 2), y_low), (slice(rows_y - 2, rows_y), y_top)):
        out[:, part, :] = out[:, part, :] + face[2 : rows_x + 2]
    for part, face in ((slice(0, 2), x_low), (slice(rows_x - 2, rows_x), x_top)):
        out[part] = out[part] + face[...]


def per_device(potential, owner, window):
    rows_x, rows_y, cells_z = potential.shape
    tiles_x, tiles_y = lax.axis_size("px"), lax.axis_size("py")
    tiles = tiles_x * tiles_y
    grid_x, grid_y = rows_x * tiles_x, rows_y * tiles_y
    planes = cells_z // tiles
    inner = rows_x * rows_y
    used = inner + -(-2 * (rows_x + rows_y) // LANES) * LANES
    blocks_x, blocks_y, blocks_z = rows_x // 8, rows_y // 8, cells_z // 8
    blocks = blocks_x * blocks_y * blocks_z
    half = max(2, 2 * blocks // tiles) // 2
    both = ("px", "py")

    def exchange(x):
        return lax.all_to_all(x, both, split_axis=0, concat_axis=0, tiled=True)

    slots, labels = call(
        functools.partial(slot_kernel, half, 2 * (rows_x + rows_y)),
        (shape(1, blocks, dtype=jnp.int32), shape(tiles, LANES)),
        [], 8, 2 * tiles * LANES * blocks, 8 * blocks,
    )(owner.reshape(blocks, 1), owner.reshape(1, blocks), window.reshape(1, blocks))

    line = shape(rows_x, cells_z)
    core, y_last, y_first = pl.pallas_call(
        prepare_kernel,
        out_shape=(shape(rows_x, rows_y, cells_z), line, line),
        in_specs=[FAR],
        out_specs=[VMEM] * 3,
        scratch_shapes=[pltpu.SemaphoreType.DMA],
        compiler_params=pltpu.CompilerParams(vmem_limit_bytes=8 << 20),
        cost_estimate=pl.CostEstimate(flops=0, bytes_accessed=2 << 20, transcendentals=0),
    )(potential)
    last_x = rows_x - 1
    y_faces = jnp.stack([send(y_last, "py", 1), send(y_first, "py", -1)])
    x_lines = [
        jnp.concatenate([y_faces[0, x : x + 1], core[x], y_faces[1, x : x + 1]])
        for x in (last_x, 0)
    ]
    x_faces = jnp.stack([send(x_lines[0], "px", 1), send(x_lines[1], "px", -1)])

    halves = shape(inner, cells_z, dtype=BF16)
    table = shape(cells_z, cells_z, dtype=BF16)
    step = 16
    *source, z_high, z_low = call(
        functools.partial(source_kernel, step), (halves, halves, table, table),
        [pltpu.VMEM((rows_x, rows_y + 16, cells_z), F32)],
        8, 60 * inner * cells_z, 2 << 20,
    )(core, y_faces)
    spectrum = call(
        spectrum_kernel, shape(cells_z, inner),
        [pltpu.VMEM((3, rows_y + 16, cells_z), F32)] + [pltpu.VMEM((inner, cells_z), BF16)] * 2,
        12, 6 * inner * cells_z**2, 2 << 20,
    )(core, y_faces, x_faces, *source, z_high, z_low)
    cells = pltpu.VMEM((used, cells_z), F32)
    width = -(-10 * blocks_z // LANES) * LANES
    sorted_table = shape(cells_z, width, dtype=BF16)
    *sorted_args, high, low = call(
        sort_kernel, (shape(width // LANES, used, LANES), sorted_table, sorted_table), [cells],
        10, 12 * used * cells_z**2, 2 << 20,
    )(core, x_faces, y_faces, z_high, z_low)
    sorted_tables = (high, low)

    span = tiles_y // 2
    length = span * rows_y
    halved = (
        2 * length == LANES and grid_x == LANES and planes == 8 and tiles_y == 8
        and 2 * (rows_x + rows_y) + 4 * half <= LANES
    )
    if halved:
        groups = [
            [i * tiles_y + g * span + j for i in range(tiles_x) for j in range(span)] for g in range(2)
        ]

        def exchange_half(x):
            return lax.all_to_all(x, both, 0, 0, axis_index_groups=groups, tiled=True)

        place_x, place_y = lax.axis_index("px"), lax.axis_index("py")
        own = (place_y // span).astype(jnp.int32).reshape(1)
        first = ((place_x * span + place_y % span) * 2 * planes).astype(jnp.int32).reshape(1)
        lap_z = laplace_of(cells_z)
        lap_x = np.broadcast_to(laplace_of(grid_x)[:, None], (grid_x, LANES))
        lap_xy = lap_x + np.tile(laplace_of(length), 2)[None, :]
        x_table = pieces_of(table_of(grid_x))
        y_table = pieces_of(np.kron(np.eye(2, dtype=np.float32), table_of(length)))
        square = shape(grid_x, LANES)
        cube = shape(planes, grid_x, LANES)
        slab = exchange_half(spectrum).reshape(tiles // 2, 2 * planes, inner)
        slab, *sorted_args, high, low = lax.optimization_barrier((slab, *sorted_args, high, low))
        sorted_tables = (high, low)
        tables = call(
            functools.partial(decay_kernel, length),
            (cube, cube, square, square, shape(LANES, 2 * planes * LANES, dtype=BF16)),
            [], 16, 100 * planes * grid_x * LANES, 2 << 20, 2,
        )(first, lap_z, lap_x)
        found, ends, sent_ends = call(
            functools.partial(
                half_kernel, tiles_x, span, rows_x, rows_y,
                SECOND_ORDER / (grid_x * length * cells_z), 2 * (rows_x + rows_y),
            ),
            (cube, square, shape(4 * planes + 8 + 2 * half, grid_x)),
            [pltpu.VMEM((grid_x * planes, LANES), F32)],
            12, 12 * planes * grid_x**2 * LANES, 2 << 20, 2,
        )(first, lap_z, slab, labels, lap_xy, *x_table, *y_table)
        arrived_ends = lax.ppermute(sent_ends, "py", [(j, (j + span) % tiles_y) for j in range(tiles_y)])
        returned = call(
            functools.partial(join_kernel, tiles_x, span, rows_x, rows_y, 2 * half),
            shape(tiles // 2, 2 * planes, used),
            [pltpu.VMEM((grid_x * planes, LANES), F32)] + [pltpu.VMEM((LANES, grid_x), F32)] * 2,
            12, 12 * planes * grid_x**2 * LANES, 2 << 20, 2,
        )(first, own, found, ends, arrived_ends, labels, *tables, *x_table)
        modes = exchange_half(returned.reshape(cells_z, used))
    else:
        span = tiles_y
        own = jnp.zeros((1,), jnp.int32)
        slab = exchange(spectrum).reshape(tiles, planes, inner)
        scale = SECOND_ORDER / (grid_x * grid_y * cells_z)
        returned = solve_plain(slab, labels, rows_x, rows_y, cells_z, tiles_x, tiles_y, scale)
        modes = exchange(returned.reshape(cells_z, used))

    tile_args = (core, x_faces, y_faces, modes, z_high, z_low)
    sent, values, arrived_labels = call(
        functools.partial(block_kernel, rows_x, rows_y, cells_z // (tiles_x * span), half, tiles_y, span),
        (shape(blocks, ROWS), shape(ROWS, blocks), shape(2, 1, blocks, dtype=jnp.int32)),
        [pltpu.VMEM((width // LANES, used, LANES), F32)],
        12, 20 * used * cells_z**2, 6 << 20, 1,
    )(own, *sorted_args, modes, *sorted_tables, slots)
    first = exchange(sent)
    later = call(functools.partial(fill_slots, 1), shape(blocks, ROWS), [], 16, 6 * ROWS * blocks**2, 4 << 20)(values, slots)
    displacement = call(
        displacement_kernel, shape(3, rows_x, rows_y, cells_z),
        [pltpu.VMEM((rows_x, rows_y + 16, cells_z), F32), cells],
        16, 6 * used * cells_z**2, 4 << 20,
    )(*tile_args)

    later, displacement = lax.optimization_barrier((later, displacement))
    arrived = first, exchange(later)
    tile_shape = (rows_x + 4, rows_y + 8, cells_z)
    scratch = [
        pltpu.VMEM((blocks // LANES, ROWS, LANES), F32),
        pltpu.VMEM((blocks // LANES, 15, 64, 8, LANES), F32),
        pltpu.VMEM((12 * 12 * 16, 2 * blocks), BF16),
        pltpu.VMEM((2, 12 * blocks_z // LANES, blocks_x * blocks_y * 12 * 16, LANES), BF16),
        pltpu.VMEM(tile_shape, F32),
    ]
    sizes = (blocks_x, blocks_y, blocks_z)
    cost = (300 * blocks * 512, 4 << 20)
    tile = call(
        functools.partial(deposit_kernel, *sizes, False), shape(*tile_shape), scratch, 32, *cost
    )(arrived[0], arrived_labels[0])
    middle, x_rims, y_rims = call(
        functools.partial(deposit_kernel, *sizes, True),
        (
            shape(rows_x, rows_y, cells_z), shape(2, 2, rows_y, cells_z),
            shape(2, rows_x + 4, 2, cells_z),
        ),
        scratch, 32, *cost,
    )(arrived[1], arrived_labels[1], tile)

    y_sides = send(y_rims[1], "py", 1), send(y_rims[0], "py", -1)
    x_rims = call(corner_kernel, shape(*x_rims.shape), [], 4, 8 * rows_y * cells_z, 1 << 17)(
        x_rims, *y_sides
    )
    x_sides = send(x_rims[1], "px", 1), send(x_rims[0], "px", -1)
    density = call(rim_kernel, shape(rows_x, rows_y, cells_z), [], 8, inner * cells_z, 2 << 20)(
        middle, *y_sides, *x_sides
    )
    return (displacement, density)


def solution(mesh):
    return jax.shard_map(
        per_device,
        mesh=mesh,
        in_specs=(P("px", "py", None), P("px", "py", None, None), P("px", "py", None)),
        out_specs=(P(None, "px", "py", None), P("px", "py", None)),
        check_vma=False,
    )
```

```python
import functools
import math

import jax
import jax.numpy as jnp
import numpy as np
from jax import lax
from jax.experimental import pallas as pl
from jax.experimental.pallas import tpu as pltpu
from jax.sharding import PartitionSpec as P

SECOND_ORDER = 3.0 / 7.0
F32 = jnp.float32
BF16 = jnp.bfloat16
LANES = 128
ROWS = 896
VMEM = pl.BlockSpec(memory_space=pltpu.VMEM)
SMEM = pl.BlockSpec(memory_space=pltpu.SMEM)
FAR = pl.BlockSpec(memory_space=pltpu.HBM)
NN = (((1,), (0,)), ((), ()))
NT = (((1,), (1,)), ((), ()))
TN = (((0,), (0,)), ((), ()))


def split(x, pieces):
    out = []
    for piece in range(pieces):
        part = x.astype(BF16)
        out.append(part)
        if piece < pieces - 1:
            x = x - part.astype(F32)
    return out


def dot(a, b, dims=NN):
    return lax.dot_general(a, b, dims, preferred_element_type=F32)


def dot3(a, b, dims=NN):
    return dot(a[0], b[0], dims) + (dot(a[0], b[1], dims) + dot(a[1], b[0], dims))


def swap_groups(rows, group):
    rows = list(rows)
    count = len(rows)
    axis = rows[0].ndim - 1
    lane = lax.broadcasted_iota(jnp.int32, rows[0].shape, axis) // group
    step = 1
    while step < count:
        low = (lane & step) == 0
        for k in range(count):
            if k & step:
                continue
            a, b = rows[k], rows[k + step]
            rows[k] = jnp.where(low, a, pltpu.roll(b, step * group, axis))
            rows[k + step] = jnp.where(low, pltpu.roll(a, LANES - step * group, axis), b)
        step *= 2
    return rows


def table_of(length):
    modes = np.arange(length)
    angle = (modes[:, None] * modes[None, :] % length) * (2.0 * math.pi / length)
    return (np.cos(angle) + np.sin(angle)).astype(np.float32)


def pieces_of(table):
    high = table.astype(jnp.bfloat16)
    low = (table - high.astype(np.float32)).astype(jnp.bfloat16)
    return np.asarray(high), np.asarray(low)


def laplace_of(length):
    return (2.0 * np.cos(np.arange(length) * (2.0 * math.pi / length)) - 2.0).astype(np.float32)


def call(body, outs, scratch, vmem, flops, moved, scalars=0):
    def run(*operands):
        return pl.pallas_call(
            body,
            out_shape=outs,
            in_specs=[SMEM] * scalars + [VMEM] * (len(operands) - scalars),
            out_specs=jax.tree.map(lambda _: VMEM, outs),
            scratch_shapes=scratch,
            compiler_params=pltpu.CompilerParams(vmem_limit_bytes=vmem << 20),
            cost_estimate=pl.CostEstimate(flops=flops, bytes_accessed=moved, transcendentals=0),
        )(*operands)

    return run


def shape(*dims, dtype=F32):
    return jax.ShapeDtypeStruct(dims, dtype)


def send(x, axis, step):
    size = lax.axis_size(axis)
    return lax.ppermute(x, axis, [(i, (i + step) % size) for i in range(size)])


def slot_kernel(half, start, owner_col, owner_row, window_row, slot_out, label_out):
    count = owner_row.shape[1]
    tiles = label_out.shape[0]
    later = lax.broadcasted_iota(jnp.int32, (count, count), 0) < lax.broadcasted_iota(
        jnp.int32, (count, count), 1
    )
    owners = owner_row[...]
    same = (owner_col[...] == owners) & later
    rank = jnp.sum(same.astype(F32), axis=0, keepdims=True).astype(jnp.int32)
    second = rank >= half
    place = owners * half + jnp.where(second, rank - half, rank)
    slot_out[...] = jnp.where(second, place + count, place)
    tile = lax.broadcasted_iota(jnp.int32, (tiles, count), 0)
    named = jnp.where(tile == owners, window_row[...] + 1, 0).astype(F32).astype(BF16)
    lane = lax.broadcasted_iota(jnp.int32, (LANES, count), 0)
    label_out[...] = dot(named, (lane == rank + start).astype(BF16), NT) - 1.0


def source_of(at, cells_z):
    def ahead(value):
        return pltpu.roll(value, cells_z - 1, 1)

    def behind(value):
        return pltpu.roll(value, 1, 1)

    here = at(0, 0)
    ahead_x, behind_x, ahead_y, behind_y = at(1, 0), at(-1, 0), at(0, 1), at(0, -1)
    xx = ahead_x - 2.0 * here + behind_x
    yy = ahead_y - 2.0 * here + behind_y
    zz = ahead(here) - 2.0 * here + behind(here)
    xy = (at(1, 1) - at(1, -1) - at(-1, 1) + at(-1, -1)) * 0.25
    across_x, across_y = ahead_x - behind_x, ahead_y - behind_y
    xz = (ahead(across_x) - behind(across_x)) * 0.25
    yz = (ahead(across_y) - behind(across_y)) * 0.25
    return xx * yy + xx * zz + yy * zz - xy * xy - xz * xz - yz * yz


def prepare_kernel(potential, core, y_last, y_first, sem):
    copy = pltpu.make_async_copy(potential, core, sem)
    copy.start()
    copy.wait()
    rows_x, rows_y, _ = core.shape
    for x in range(rows_x):
        y_last[x : x + 1, :] = core[x, rows_y - 1 : rows_y, :]
        y_first[x : x + 1, :] = core[x, 0:1, :]


def source_kernel(step, core, y_faces, high, low, table_high, table_low, pad):
    rows_x, rows_y, cells_z = core.shape
    coarse = cells_z // step

    def turns(count, stride):
        row = lax.broadcasted_iota(jnp.int32, (count, cells_z), 0) * stride
        col = lax.broadcasted_iota(jnp.int32, (count, cells_z), 1)
        angle = (row * col % cells_z).astype(F32) * (2.0 * math.pi / cells_z)
        return jnp.cos(angle), jnp.sin(angle)

    wide_cos, wide_sin = turns(coarse, step)
    fine_cos, fine_sin = turns(step, 1)
    fine, turned = fine_cos + fine_sin, fine_cos - fine_sin
    for k in range(coarse):
        rows = slice(k * step, (k + 1) * step)
        value = wide_cos[k : k + 1] * fine + wide_sin[k : k + 1] * turned
        table_high[rows, :], table_low[rows, :] = split(value, 2)
    pad[:, 8 : rows_y + 8, :] = core[...]
    for x in range(rows_x):
        pad[x, 7:8, :] = y_faces[0, x : x + 1, :]
        pad[x, rows_y + 8 : rows_y + 9, :] = y_faces[1, x : x + 1, :]

    @pl.loop(1, rows_x - 1, unroll=3)
    def _(x):
        def at(dx, dy):
            return pad[x + dx, 8 + dy : 8 + dy + rows_y, :]

        rows = pl.ds(pl.multiple_of(x * rows_y, rows_y), rows_y)
        high[rows, :], low[rows, :] = split(source_of(at, cells_z), 2)

    for x in (0, rows_x - 1):
        rows = slice(x * rows_y, (x + 1) * rows_y)
        high[rows, :] = jnp.zeros((rows_y, cells_z), BF16)
        low[rows, :] = jnp.zeros((rows_y, cells_z), BF16)


def spectrum_kernel(core, y_faces, x_faces, inner_high, inner_low, high, low, spectrum, pad, source_high, source_low):
    rows_x, rows_y, cells_z = core.shape
    source_high[...] = inner_high[...]
    source_low[...] = inner_low[...]
    for side in range(2):
        edge = side * (rows_x - 1)
        for line in range(3):
            x = edge + line - 1
            if 0 <= x < rows_x:
                pad[line, 8 : rows_y + 8, :] = core[x]
                pad[line, 7:8, :] = y_faces[0, x : x + 1, :]
                pad[line, rows_y + 8 : rows_y + 9, :] = y_faces[1, x : x + 1, :]
            else:
                pad[line, 7 : rows_y + 9, :] = x_faces[side]

        def at(dx, dy):
            return pad[1 + dx, 8 + dy : 8 + dy + rows_y, :]

        rows = slice(edge * rows_y, (edge + 1) * rows_y)
        source_high[rows, :], source_low[rows, :] = split(source_of(at, cells_z), 2)
    spectrum[...] = dot3((high[...], low[...]), (source_high[...], source_low[...]), NT)


def stacked(pieces):
    high, low = pieces
    return jnp.concatenate(
        [jnp.concatenate([high, low], 1), jnp.concatenate([high, jnp.zeros_like(high)], 1)], 0
    )


def joined(value):
    width = value.shape[1] // 2
    return value[:, :width] + value[:, width:]


def placed(pieces, choose):
    return dot(pieces[0], choose) + dot(pieces[1], choose) + dot(pieces[2], choose)


def gathered(planes, choose, step):
    count, rows, _ = planes.shape
    pieces = jnp.concatenate(split(planes[...].reshape(count * rows, LANES), 3), 1)
    choose = choose.astype(BF16)
    picked = dot(pieces, jnp.concatenate([choose] * 3, 0))
    total = picked[0:rows]
    for q in range(1, count):
        total = total + pltpu.roll(picked[q * rows : (q + 1) * rows], step * q, 1)
    return total


def iota(dims, axis):
    return lax.broadcasted_iota(jnp.int32, dims, axis)


def decay(w, length):
    grow = w + jnp.sqrt(w * (w + 2.0))
    rate = jnp.log(1.0 + grow)
    ratio = 1.0 / (1.0 + grow)
    both = (1.0 + grow) + jnp.exp(-rate * (length - 1.0))
    flat = w <= 0.0
    return rate, 2.0 * (1.0 + ratio) * both, 2.0 * jnp.where(flat, 1.0, grow * ratio * both), flat


def decay_kernel(length, first, lap_z, lap_x, even, odd, edge_even, edge_odd, spread):
    count = even.shape[0]
    dims = even.shape[1:]
    lane = iota(dims, 1)
    group = lane // length
    y = (lane % length).astype(F32)
    start = first[0]
    for q in range(count):
        along_z = jnp.where(group == 0, lap_z[start + q], lap_z[start + count + q])
        rate, plus, minus, flat = decay(-0.5 * (lap_x[...] + along_z), length)
        rise, fall = jnp.exp(-rate * y), jnp.exp(-rate * (length - 1.0 - y))
        even[q] = (rise + fall) / plus
        odd[q] = jnp.where(flat, 0.25 * (length - 1.0) - 0.5 * y, (rise - fall) / minus)
    along_z = jnp.zeros(dims, F32)
    for q in range(count):
        for g in range(2):
            along_z = jnp.where(lane // 2 == 2 * q + g, lap_z[start + g * count + q], along_z)
    rate, plus, minus, flat = decay(-0.5 * (lap_x[...] + along_z), length)
    last = jnp.exp(-rate * (length - 1.0))
    edge_even[...] = (1.0 + last) / plus
    edge_odd[...] = jnp.where(flat, 0.25 * (length - 1.0), (1.0 - last) / minus)
    dims = spread.shape
    col = iota(dims, 1)
    row = iota(dims, 0)
    hit = row // 2 == 2 * (col // (2 * LANES)) + col % LANES // length
    sign = jnp.where((col // LANES % 2 == 1) & (row % 2 == 0), -1.0, 1.0)
    spread[...] = jnp.where(hit, sign, 0.0).astype(BF16)


def half_kernel(
    tiles_x, tiles_y, rows_x, rows_y, scale, mark,
    first, lap_z, slab, labels, lap_xy, hx_high, hx_low, hy_high, hy_low,
    found, ends, sent, planes,
):
    grid_x = tiles_x * rows_x
    count = slab.shape[1] // 2
    length = tiles_y * rows_y
    per = LANES // rows_y
    along_y = stacked((hy_high[...], hy_low[...]))
    along_x = jnp.concatenate([hx_high[...], hx_low[...]], 1)

    def times_y(value):
        return joined(dot(jnp.concatenate(split(value, 2), 1), along_y))

    for i in range(tiles_x):
        for part in range(rows_x // per):
            lanes = slice(part * LANES, (part + 1) * LANES)
            rows = [
                slab[i * tiles_y + j, g * count : (g + 1) * count, lanes]
                for g in range(2)
                for j in range(tiles_y)
            ]
            x = (i * rows_x + part * per) * count
            planes[x : x + per * count, :] = times_y(jnp.concatenate(swap_groups(rows, rows_y), 0))
    dims = (grid_x, LANES)
    lane, row = iota(dims, 1), iota(dims, 0)
    block = jnp.zeros(dims, F32)
    for q in range(count):
        modes = joined(dot(along_x, stacked(split(planes[pl.ds(q, grid_x, stride=count), :], 2))))
        eigen = lap_xy[...] + jnp.where(lane < length, lap_z[first[0] + q], lap_z[first[0] + count + q])
        anchor = eigen == 0.0
        value = times_y(jnp.where(anchor, 0.0, scale / jnp.where(anchor, -1.0, eigen)) * modes)
        found[q] = value
        if q == 0:
            mean = pltpu.roll(modes * scale, 4 * count, 1)
            block = block + jnp.where((row == 0) & (lane == 4 * count), mean, 0.0)
    choose = (row == lane // 2 * length + lane % 2 * (length - 1)) & (lane < 4)
    block = block + gathered(found, choose, 4)
    ends[...] = block
    tiles = labels.shape[0]
    ends[0:tiles, :] = jnp.where(lane[0:tiles] < mark, block[0:tiles], labels[...])
    turned = jnp.transpose(ends[...])
    used = 4 * count + 8
    sent[0:used, :] = turned[0:used]
    sent[used:, :] = turned[mark : mark + sent.shape[0] - used]


def join_kernel(
    tiles_x, tiles_y, rows_x, rows_y, places,
    first, half, found, ends, received, labels, even, odd, edge_even, edge_odd, spread, hx_high, hx_low,
    out, planes, faces, arrived,
):
    grid_x = tiles_x * rows_x
    count = found.shape[0]
    length = tiles_y * rows_y
    per = LANES // rows_y
    along_x = jnp.concatenate([hx_high[...], hx_low[...]], 1)

    def times_x(value):
        return joined(dot(along_x, stacked(split(value, 2))))

    dims = (grid_x, LANES)
    lane, row = iota(dims, 1), iota(dims, 0)
    used = 4 * count + 8
    mark = 2 * (rows_x + rows_y)
    gap = jnp.zeros((mark - used, LANES), F32)
    rest = jnp.zeros((LANES - mark - received.shape[0] + used, LANES), F32)
    arrived[...] = jnp.transpose(
        jnp.concatenate([received[0:used, :], gap, received[used:, :], rest], 0)
    )
    jump = jnp.where(lane < 4 * count + 1, arrived[...] - ends[...], 0.0)
    pieces = split(jump, 2)
    wide = dot(pieces[0], spread[...]) + dot(pieces[1], spread[...])
    mean = jnp.where(first[0] == 0, -0.5 * jump[0:1, 4 * count : 4 * count + 1], 0.0)
    y = lane.astype(F32)
    bend = jnp.where(
        (row == 0) & (lane < length),
        mean * (0.5 * y * y - 0.5 * (length - 1.0) * y - 0.25 * length),
        0.0,
    )
    target = iota((LANES, LANES), 1)
    source = iota((LANES, LANES), 0)
    side, j, group = target // 8 % 2, target // 2 % tiles_y, target % 2
    inside = ((side == 0) & (j > 0)) | ((side == 1) & (j < tiles_y - 1))
    wanted = group * length + jnp.where(side == 0, j * rows_y - 1, (j + 1) * rows_y)
    lines = jnp.zeros(dims, F32)
    for q in range(count):
        at = 2 * q * LANES
        value = found[q] + (wide[:, at : at + LANES] * even[q] + wide[:, at + LANES : at + 2 * LANES] * odd[q])
        if q == 0:
            value = value + bend
        choose = inside & (source == wanted) & (target // 16 == q)
        lines = lines + placed(split(value, 3), choose.astype(BF16))
        planes[pl.ds(q, grid_x, stride=count), :] = times_x(value)
    low = lane % 2 == 0
    other = jnp.where(low, pltpu.roll(jump, LANES - 1, 1), pltpu.roll(jump, 1, 1))
    change = (jump + other) * edge_even[...] + (other - jump) * edge_odd[...]
    change = change + jnp.where((row == 0) & (lane < 2), -0.25 * length * mean, 0.0)
    beyond = jnp.where(lane < 4 * count, arrived[...] - change, 0.0)
    first_side = source % 2 == 1
    goal = source // 4 * 16 + source // 2 % 2 + jnp.where(first_side, 0, 8 + 2 * (tiles_y - 1))
    choose = (target == goal) & (source < 4 * count)
    lines = lines + placed(split(beyond, 3), choose.astype(BF16))
    faces[...] = jnp.transpose(times_x(lines))

    def row_of(x):
        x = x % grid_x
        return planes[x * count : (x + 1) * count, :]

    lane = iota((count, LANES), 1)
    for i in range(tiles_x):
        for part in range(rows_x // per):
            lanes = slice(part * LANES, (part + 1) * LANES)
            rows = [row_of(i * rows_x + part * per + t) for t in range(per)]
            for k, item in enumerate(swap_groups(rows, rows_y)):
                g, j = k // tiles_y, k % tiles_y
                out[i * tiles_y + j, g * count : (g + 1) * count, lanes] = item
        before, after = row_of(i * rows_x - 1), row_of((i + 1) * rows_x)
        for k in range(per):
            g, j = k // tiles_y, k % tiles_y
            shift = (LANES - k * rows_y) % LANES
            line = pltpu.roll(before, shift, 1) if shift else before
            moved = pltpu.roll(after, (shift + rows_y) % LANES, 1)
            line = jnp.where(lane < rows_y, line, moved)
            for side in range(2):
                face = faces[pl.ds(side * 8 + j * 2 + g, count, stride=16), :]
                start = 2 * rows_y + side * rows_x
                move = (start - i * rows_x) % LANES
                face = pltpu.roll(face, move, 1) if move else face
                line = jnp.where(lane < start, line, face)
            start = 2 * (rows_x + rows_y)
            tile = (2 * i + half[0]) * tiles_y + j
            own, partner = labels[pl.ds(tile, 1), :], pltpu.roll(arrived[pl.ds(tile, 1), :], places, 1)
            line = jnp.where(lane < start, line, jnp.where(lane < start + places, own, partner))
            out[i * tiles_y + j, g * count : (g + 1) * count, rows_x * rows_y : rows_x * rows_y + LANES] = line


def solve_plain(slab, labels, rows_x, rows_y, cells_z, tiles_x, tiles_y, scale):
    high = lax.Precision.HIGHEST
    grid_x, grid_y = tiles_x * rows_x, tiles_y * rows_y
    count = slab.shape[1]
    hx, hy = jnp.asarray(table_of(grid_x)), jnp.asarray(table_of(grid_y))
    planes = slab.reshape(tiles_x, tiles_y, count, rows_x, rows_y).transpose(2, 0, 3, 1, 4)
    planes = planes.reshape(count, grid_x, grid_y)
    modes = jnp.einsum("qxy,xk,yl->qkl", planes, hx, hy, precision=high)
    first = lax.axis_index(("px", "py")) * count
    lap_z = lax.dynamic_slice_in_dim(jnp.asarray(laplace_of(cells_z)), first, count)
    eigen = (
        jnp.asarray(laplace_of(grid_x))[None, :, None]
        + jnp.asarray(laplace_of(grid_y))[None, None, :]
        + lap_z[:, None, None]
    )
    anchor = eigen == 0.0
    solved = jnp.where(anchor, 0.0, scale / jnp.where(anchor, -1.0, eigen)) * modes
    back = jnp.einsum("qkl,xk,yl->qxy", solved, hx, hy, precision=high)
    tiles = back.reshape(count, tiles_x, rows_x, tiles_y, rows_y).transpose(1, 3, 0, 2, 4)
    starts_x, starts_y = np.arange(tiles_x) * rows_x, np.arange(tiles_y) * rows_y
    faces = []
    for edge in (-1, rows_x):
        line = back[:, (starts_x + edge) % grid_x].reshape(count, tiles_x, tiles_y, rows_y)
        faces.append(line.transpose(1, 2, 0, 3))
    for edge in (-1, rows_y):
        line = back[:, :, (starts_y + edge) % grid_y].reshape(count, tiles_x, rows_x, tiles_y)
        faces.append(line.transpose(1, 3, 0, 2))
    tail = labels[:, 2 * (rows_x + rows_y) :].reshape(tiles_x, tiles_y, 1, -1)
    faces.append(jnp.broadcast_to(tail, (tiles_x, tiles_y, count, tail.shape[-1])))
    parts = [tiles.reshape(tiles_x, tiles_y, count, rows_x * rows_y)] + faces
    return jnp.concatenate(parts, -1).reshape(tiles_x * tiles_y, count, -1)


def combine(core, x_faces, y_faces, spectrum, high, low, cells):
    rows_x, rows_y, cells_z = core.shape
    inner = rows_x * rows_y
    cells[...] = dot3(split(spectrum[...], 2), (high[...], low[...]), TN)
    cells[0:inner, :] = cells[0:inner, :] + core[...].reshape(inner, cells_z)
    start = inner
    for faces, skip in ((x_faces, 1), (y_faces, 0)):
        for side in range(2):
            length = faces.shape[1] - 2 * skip
            rows = slice(start, start + length)
            cells[rows, :] = cells[rows, :] + faces[side, skip : skip + length, :]
            start += length
    return edges_of(rows_x, rows_y)


def displacement_kernel(core, x_faces, y_faces, spectrum, high, low, displacement, pad, cells):
    rows_x, rows_y, cells_z = core.shape
    x_edge, y_edge = combine(core, x_faces, y_faces, spectrum, high, low, cells)
    for x in range(rows_x):
        pad[x, 8 : rows_y + 8, :] = cells[x * rows_y : (x + 1) * rows_y, :]
        pad[x, 7:8, :] = cells[y_edge[0] + x : y_edge[0] + x + 1, :]
        pad[x, rows_y + 8 : rows_y + 9, :] = cells[y_edge[1] + x : y_edge[1] + x + 1, :]

    def line(x):
        if x < 0:
            return cells[x_edge[0] : x_edge[0] + rows_y, :]
        if x >= rows_x:
            return cells[x_edge[1] : x_edge[1] + rows_y, :]
        return cells[x * rows_y : (x + 1) * rows_y, :]

    for x in range(rows_x):
        here = line(x)
        displacement[0, x] = (line(x - 1) - line(x + 1)) * 0.5
        displacement[1, x] = (pad[x, 7 : rows_y + 7, :] - pad[x, 9 : rows_y + 9, :]) * 0.5
        displacement[2, x] = (pltpu.roll(here, 1, 1) - pltpu.roll(here, cells_z - 1, 1)) * 0.5


def edges_of(rows_x, rows_y):
    inner = rows_x * rows_y
    return [inner, inner + rows_y], [inner + 2 * rows_y, inner + 2 * rows_y + rows_x]


def sort_kernel(core, x_faces, y_faces, high, low, spread, sorted_high, sorted_low, cells):
    rows_x, rows_y, cells_z = core.shape
    blocks_z = cells_z // 8
    inner = rows_x * rows_y
    x_edge, y_edge = edges_of(rows_x, rows_y)
    cells[0:inner, :] = core[...].reshape(inner, cells_z)
    for side in range(2):
        cells[x_edge[side] : x_edge[side] + rows_y, :] = x_faces[side, 1 : rows_y + 1, :]
        cells[y_edge[side] : y_edge[side] + rows_x, :] = y_faces[side]
    used = y_edge[1] + rows_x
    cells[used:, :] = jnp.zeros((cells.shape[0] - used, cells_z), F32)
    width = sorted_high.shape[1]
    col = lax.broadcasted_iota(jnp.int32, (cells_z, width), 1)
    wanted = (8 * (col % blocks_z) + col // blocks_z + cells_z - 1) % cells_z
    choose = (wanted == lax.broadcasted_iota(jnp.int32, (cells_z, width), 0)).astype(BF16)
    pieces = split(cells[...], 3)
    moved = dot(pieces[0], choose) + dot(pieces[1], choose) + dot(pieces[2], choose)
    for quad in range(spread.shape[0]):
        spread[quad] = moved[:, quad * LANES : (quad + 1) * LANES]
    sorted_high[...] = dot(high[...], choose).astype(BF16)
    sorted_low[...] = dot(low[...], choose).astype(BF16)


def block_kernel(
    rows_x, rows_y, planes, half, tiles_y, span, own, potential, spectrum, high, low, slots,
    out, values, labels,
    spread,
):
    cells_z = spectrum.shape[0]
    inner = rows_x * rows_y
    blocks_x, blocks_y, blocks_z = rows_x // 8, rows_y // 8, cells_z // 8
    per = LANES // blocks_z
    x_edge, y_edge = edges_of(rows_x, rows_y)
    width = high.shape[1]
    second = dot3(split(spectrum[...], 2), (high[...], low[...]), TN)
    for quad in range(width // LANES):
        spread[quad] = potential[quad] + second[:, quad * LANES : (quad + 1) * LANES]

    def put(row, tiles):
        for quad in range(width // LANES):
            every = [tiles(b // blocks_y, b % blocks_y, quad) for b in range(blocks_x * blocks_y)]
            for block in range(0, len(every), per):
                for k, item in enumerate(swap_groups(every[block : block + per], blocks_z)):
                    where = row(quad * per + k - 1)
                    if where is not None:
                        start = block * blocks_z
                        values[where : where + 8, start : start + LANES] = item

    def x_tile(a):
        def tile(bx, by, quad):
            x = 8 * bx + a
            top = x_edge[0] if x < 0 else x_edge[1] if x >= rows_x else x * rows_y
            return spread[quad, top + 8 * by : top + 8 * by + 8, :]

        return tile

    for a in range(-1, 9):
        def row(e, a=a):
            if 0 <= e < 8:
                return ((a + 1) * 8 + e) * 8
            if e in (-1, 8) and 0 <= a < 8:
                return 640 + (64 if e == 8 else 0) + a * 8
            return None

        put(row, x_tile(a))
    for side, edge in enumerate((-1, 8)):
        def tile(bx, by, quad, edge=edge):
            y = 8 * by + edge
            if y < 0 or y >= rows_y:
                top = y_edge[0 if y < 0 else 1] + 8 * bx
                return spread[quad, top : top + 8, :]
            return spread[quad, pl.ds(8 * bx * rows_y + y, 8, stride=rows_y), :]

        put(lambda e, side=side: 768 + side * 64 + e * 8 if 0 <= e < 8 else None, tile)

    count = slots.shape[1]
    named = spectrum[:, inner : inner + LANES].astype(BF16)
    row = lax.broadcasted_iota(jnp.int32, (cells_z, count), 0)
    slot = lax.broadcasted_iota(jnp.int32, (cells_z, count), 1)
    tile = slot // half
    member = tile // tiles_y * span + tile % span
    source = (row % planes == 0) & (row // planes == member)
    by_lane = dot(named, source.astype(BF16), TN)
    dims = (LANES, count)
    slot = iota(dims, 1)
    moved = jnp.where(slot // half % tiles_y // span == own[0], 0, 2 * half)
    lane = iota(dims, 0) - 2 * (rows_x + rows_y) - moved
    place = slot % half
    for part in range(2):
        label = jnp.sum(jnp.where(lane == place + part * half, by_lane, 0.0), axis=0, keepdims=True)
        labels[part] = label.astype(jnp.int32)

    fill_slots(0, values, slots, out)


def fill_slots(part, values, slots, out):
    count = slots.shape[1]
    pieces = split(values[...], 3)
    number = lax.broadcasted_iota(jnp.int32, (count, count), 0) + part * count
    chosen = (slots[...] == number).astype(BF16)
    out[...] = dot(chosen, pieces[0], NT) + dot(chosen, pieces[1], NT) + dot(chosen, pieces[2], NT)


def spline(shift):
    g = jnp.abs(shift)
    h = 1.0 - g
    gg, hh = g * g, h * h
    near = (2.0 / 3.0) - gg + 0.5 * gg * g
    ahead = (2.0 / 3.0) - hh + 0.5 * hh * h
    back = hh * h * (1.0 / 6.0)
    far = gg * g * (1.0 / 6.0)
    up = shift >= 0.0
    zero = jnp.zeros_like(far)
    return (
        jnp.where(up, zero, far),
        jnp.where(up, back, ahead),
        near,
        jnp.where(up, ahead, back),
        jnp.where(up, far, zero),
    )


def deposit_kernel(blocks_x, blocks_y, blocks_z, last, blocks, labels, *refs):
    if last:
        before, core, x_rims, y_rims, turned, weights, pieces, grouped, tile = refs
    else:
        core, turned, weights, pieces, grouped, tile = refs
    slots = blocks.shape[0]
    cells_z = 8 * blocks_z
    per = LANES // blocks_z
    windows = blocks_x * blocks_y * blocks_z
    sub = lax.broadcasted_iota(jnp.int32, (8, LANES), 0)
    for g in range(slots // LANES):
        turned[g] = jnp.transpose(blocks[g * LANES : (g + 1) * LANES, :])

    @pl.loop(0, slots // LANES)
    def _(g):
        def rows(start):
            return turned[g, pl.ds(pl.multiple_of(start, 8), 8), :]

        @pl.loop(0, 8)
        def _(a):
            for e in range(8):
                here = rows((a + 1) * 64 + e * 8)
                x_diff = rows(a * 64 + e * 8) - rows((a + 2) * 64 + e * 8)
                z_low = rows((a + 1) * 64 + e * 8 - 8) if e > 0 else rows(640 + a * 8)
                z_top = rows((a + 1) * 64 + e * 8 + 8) if e < 7 else rows(704 + a * 8)
                y_low = jnp.where(
                    sub == 0, turned[g, pl.ds(768 + e * 8 + a, 1), :], pltpu.roll(here, 1, 0)
                )
                y_top = jnp.where(
                    sub == 7, turned[g, pl.ds(832 + e * 8 + a, 1), :], pltpu.roll(here, 7, 0)
                )
                for axis, diff in enumerate((x_diff, y_low - y_top, z_low - z_top)):
                    for k, weight in enumerate(spline(jnp.clip(diff * 0.5, -1.0, 1.0))):
                        if (axis, k) != (1, 2):
                            weights[g, axis * 5 + k, a * 8 + e] = weight

    def cell_row(g, s, depths):
        top_lanes = slice(g * LANES, (g + 1) * LANES)
        rest_lanes = slice(slots + g * LANES, slots + (g + 1) * LANES)
        sums = {}
        for a in range(8):
            for k in depths:
                at = a * 8 + (s - k)
                w_z = weights[g, 10 + k, at]
                w_y = [weights[g, 5 + j, at] if j != 2 else None for j in range(5)]
                for i in range(5):
                    plane = weights[g, i, at] * w_z
                    for j in range(5):
                        key = (a + i, j)
                        term = plane * w_y[j] if j != 2 else plane
                        sums[key] = sums[key] + term if key in sums else term
            for u in [a] if a < 7 else range(7, 12):
                rows = [sums[u, j] for j in range(5)]
                rows[2] = rows[2] - ((rows[0] + rows[1]) + (rows[3] + rows[4]))
                moved = [pltpu.roll(rows[j], j, 0) for j in range(1, 5)]
                every = rows[0] + ((moved[0] + moved[1]) + (moved[2] + moved[3]))
                past = [jnp.where(sub < j + 1, moved[j], 0.0) for j in range(4)]
                tail = (past[0] + past[1]) + (past[2] + past[3])
                top, rest = split(jnp.concatenate([every - tail, tail], 0), 2)
                out = slice((s * 12 + u) * 16, (s * 12 + u + 1) * 16)
                pieces[out, top_lanes] = top
                pieces[out, rest_lanes] = rest

    named = (labels[...] == lax.broadcasted_iota(jnp.int32, (windows, slots), 0)).astype(F32)
    named = jnp.transpose(named).astype(BF16)
    area = 12 * 16
    named = jnp.concatenate([named, named], 0)

    def gather(quad):
        summed = dot(pieces[quad * per * area : (quad + 1) * per * area, :], named)
        for wide in range(windows // LANES):
            lanes = slice(wide * LANES, (wide + 1) * LANES)
            part = [summed[k * area : (k + 1) * area, lanes] for k in range(per)]
            for t, item in enumerate(swap_groups(part, blocks_z)):
                rows = slice((wide * per + t) * area, (wide * per + t + 1) * area)
                grouped[0, quad, rows, :], grouped[1, quad, rows, :] = split(item, 2)

    for quad in range(12 // per):
        for s in range(quad * per, (quad + 1) * per):
            for g in range(slots // LANES):
                cell_row(g, s, [k for k in range(5) if 0 <= s - k < 8])
        if quad > 0:
            gather(quad - 1)
    gather(12 // per - 1)

    depth = 12 * blocks_z
    row = lax.broadcasted_iota(jnp.int32, (depth, cells_z), 0)
    wanted = (8 * (row % blocks_z) + row // blocks_z + cells_z - 2) % cells_z
    place = (wanted == lax.broadcasted_iota(jnp.int32, (depth, cells_z), 1)).astype(BF16)
    tile[...] = before[...] if last else jnp.zeros_like(tile)
    quads = depth // LANES
    left = jnp.concatenate([grouped[piece, quad] for piece in range(2) for quad in range(quads)], 1)
    total = dot(left, jnp.concatenate([place, place], 0))
    for bx in range(blocks_x):
        for by in range(blocks_y):
            at = (bx * blocks_y + by) * area
            rows = slice(bx * 8, bx * 8 + 12)
            cols = slice(by * 8, by * 8 + 16)
            tile[rows, cols, :] = tile[rows, cols, :] + total[at : at + area].reshape(12, 16, cells_z)

    if not last:
        core[...] = tile[...]
        return
    rows_x, rows_y = 8 * blocks_x, 8 * blocks_y
    core[...] = tile[2 : rows_x + 2, 2 : rows_y + 2, :]
    for side in range(2):
        x = side * (rows_x + 2)
        y = side * (rows_y + 2)
        x_rims[side] = tile[x : x + 2, 2 : rows_y + 2, :]
        y_rims[side] = tile[:, y : y + 2, :]


def corner_kernel(x_rims, y_low, y_top, out):
    rows_x, rows_y = y_low.shape[0] - 4, x_rims.shape[2]
    for side in range(2):
        x = side * (rows_x + 2)
        out[side] = x_rims[side]
        out[side, :, 0:2, :] = out[side, :, 0:2, :] + y_low[x : x + 2]
        out[side, :, rows_y - 2 :, :] = out[side, :, rows_y - 2 :, :] + y_top[x : x + 2]


def rim_kernel(core, y_low, y_top, x_low, x_top, out):
    rows_x, rows_y, _ = core.shape
    out[...] = core[...]
    for part, face in ((slice(0, 2), y_low), (slice(rows_y - 2, rows_y), y_top)):
        out[:, part, :] = out[:, part, :] + face[2 : rows_x + 2]
    for part, face in ((slice(0, 2), x_low), (slice(rows_x - 2, rows_x), x_top)):
        out[part] = out[part] + face[...]


def per_device(potential, owner, window):
    rows_x, rows_y, cells_z = potential.shape
    tiles_x, tiles_y = lax.axis_size("px"), lax.axis_size("py")
    tiles = tiles_x * tiles_y
    grid_x, grid_y = rows_x * tiles_x, rows_y * tiles_y
    planes = cells_z // tiles
    inner = rows_x * rows_y
    used = inner + -(-2 * (rows_x + rows_y) // LANES) * LANES
    blocks_x, blocks_y, blocks_z = rows_x // 8, rows_y // 8, cells_z // 8
    blocks = blocks_x * blocks_y * blocks_z
    half = max(2, 2 * blocks // tiles) // 2
    both = ("px", "py")

    def exchange(x):
        return lax.all_to_all(x, both, split_axis=0, concat_axis=0, tiled=True)

    slots, labels = call(
        functools.partial(slot_kernel, half, 2 * (rows_x + rows_y)),
        (shape(1, blocks, dtype=jnp.int32), shape(tiles, LANES)),
        [], 8, 2 * tiles * LANES * blocks, 8 * blocks,
    )(owner.reshape(blocks, 1), owner.reshape(1, blocks), window.reshape(1, blocks))

    line = shape(rows_x, cells_z)
    core, y_last, y_first = pl.pallas_call(
        prepare_kernel,
        out_shape=(shape(rows_x, rows_y, cells_z), line, line),
        in_specs=[FAR],
        out_specs=[VMEM] * 3,
        scratch_shapes=[pltpu.SemaphoreType.DMA],
        compiler_params=pltpu.CompilerParams(vmem_limit_bytes=8 << 20),
        cost_estimate=pl.CostEstimate(flops=0, bytes_accessed=2 << 20, transcendentals=0),
    )(potential)
    last_x = rows_x - 1
    y_faces = jnp.stack([send(y_last, "py", 1), send(y_first, "py", -1)])
    x_lines = [
        jnp.concatenate([y_faces[0, x : x + 1], core[x], y_faces[1, x : x + 1]])
        for x in (last_x, 0)
    ]
    x_faces = jnp.stack([send(x_lines[0], "px", 1), send(x_lines[1], "px", -1)])

    halves = shape(inner, cells_z, dtype=BF16)
    table = shape(cells_z, cells_z, dtype=BF16)
    step = 16
    *source, z_high, z_low = call(
        functools.partial(source_kernel, step), (halves, halves, table, table),
        [pltpu.VMEM((rows_x, rows_y + 16, cells_z), F32)],
        8, 60 * inner * cells_z, 2 << 20,
    )(core, y_faces)
    spectrum = call(
        spectrum_kernel, shape(cells_z, inner),
        [pltpu.VMEM((3, rows_y + 16, cells_z), F32)] + [pltpu.VMEM((inner, cells_z), BF16)] * 2,
        12, 6 * inner * cells_z**2, 2 << 20,
    )(core, y_faces, x_faces, *source, z_high, z_low)
    cells = pltpu.VMEM((used, cells_z), F32)
    width = -(-10 * blocks_z // LANES) * LANES
    sorted_table = shape(cells_z, width, dtype=BF16)
    *sorted_args, high, low = call(
        sort_kernel, (shape(width // LANES, used, LANES), sorted_table, sorted_table), [cells],
        10, 12 * used * cells_z**2, 2 << 20,
    )(core, x_faces, y_faces, z_high, z_low)
    sorted_tables = (high, low)

    span = tiles_y // 2
    length = span * rows_y
    halved = (
        2 * length == LANES and grid_x == LANES and planes == 8 and tiles_y == 8
        and 2 * (rows_x + rows_y) + 4 * half <= LANES
    )
    if halved:
        groups = [
            [i * tiles_y + g * span + j for i in range(tiles_x) for j in range(span)] for g in range(2)
        ]

        def exchange_half(x):
            return lax.all_to_all(x, both, 0, 0, axis_index_groups=groups, tiled=True)

        place_x, place_y = lax.axis_index("px"), lax.axis_index("py")
        own = (place_y // span).astype(jnp.int32).reshape(1)
        first = ((place_x * span + place_y % span) * 2 * planes).astype(jnp.int32).reshape(1)
        lap_z = laplace_of(cells_z)
        lap_x = np.broadcast_to(laplace_of(grid_x)[:, None], (grid_x, LANES))
        lap_xy = lap_x + np.tile(laplace_of(length), 2)[None, :]
        x_table = pieces_of(table_of(grid_x))
        y_table = pieces_of(np.kron(np.eye(2, dtype=np.float32), table_of(length)))
        square = shape(grid_x, LANES)
        cube = shape(planes, grid_x, LANES)
        slab = exchange_half(spectrum).reshape(tiles // 2, 2 * planes, inner)
        slab, *sorted_args, high, low = lax.optimization_barrier((slab, *sorted_args, high, low))
        sorted_tables = (high, low)
        tables = call(
            functools.partial(decay_kernel, length),
            (cube, cube, square, square, shape(LANES, 2 * planes * LANES, dtype=BF16)),
            [], 16, 100 * planes * grid_x * LANES, 2 << 20, 2,
        )(first, lap_z, lap_x)
        found, ends, sent_ends = call(
            functools.partial(
                half_kernel, tiles_x, span, rows_x, rows_y,
                SECOND_ORDER / (grid_x * length * cells_z), 2 * (rows_x + rows_y),
            ),
            (cube, square, shape(4 * planes + 8 + 2 * half, grid_x)),
            [pltpu.VMEM((grid_x * planes, LANES), F32)],
            12, 12 * planes * grid_x**2 * LANES, 2 << 20, 2,
        )(first, lap_z, slab, labels, lap_xy, *x_table, *y_table)
        arrived_ends = lax.ppermute(sent_ends, "py", [(j, (j + span) % tiles_y) for j in range(tiles_y)])
        returned = call(
            functools.partial(join_kernel, tiles_x, span, rows_x, rows_y, 2 * half),
            shape(tiles // 2, 2 * planes, used),
            [pltpu.VMEM((grid_x * planes, LANES), F32)] + [pltpu.VMEM((LANES, grid_x), F32)] * 2,
            12, 12 * planes * grid_x**2 * LANES, 2 << 20, 2,
        )(first, own, found, ends, arrived_ends, labels, *tables, *x_table)
        modes = exchange_half(returned.reshape(cells_z, used))
    else:
        span = tiles_y
        own = jnp.zeros((1,), jnp.int32)
        slab = exchange(spectrum).reshape(tiles, planes, inner)
        scale = SECOND_ORDER / (grid_x * grid_y * cells_z)
        returned = solve_plain(slab, labels, rows_x, rows_y, cells_z, tiles_x, tiles_y, scale)
        modes = exchange(returned.reshape(cells_z, used))

    tile_args = (core, x_faces, y_faces, modes, z_high, z_low)
    sent, values, arrived_labels = call(
        functools.partial(block_kernel, rows_x, rows_y, cells_z // (tiles_x * span), half, tiles_y, span),
        (shape(blocks, ROWS), shape(ROWS, blocks), shape(2, 1, blocks, dtype=jnp.int32)),
        [pltpu.VMEM((width // LANES, used, LANES), F32)],
        12, 20 * used * cells_z**2, 6 << 20, 1,
    )(own, *sorted_args, modes, *sorted_tables, slots)
    first = exchange(sent)
    later = call(functools.partial(fill_slots, 1), shape(blocks, ROWS), [], 16, 6 * ROWS * blocks**2, 4 << 20)(values, slots)
    displacement = call(
        displacement_kernel, shape(3, rows_x, rows_y, cells_z),
        [pltpu.VMEM((rows_x, rows_y + 16, cells_z), F32), cells],
        16, 6 * used * cells_z**2, 4 << 20,
    )(*tile_args)

    later, displacement = lax.optimization_barrier((later, displacement))
    arrived = first, exchange(later)
    tile_shape = (rows_x + 4, rows_y + 8, cells_z)
    scratch = [
        pltpu.VMEM((blocks // LANES, ROWS, LANES), F32),
        pltpu.VMEM((blocks // LANES, 15, 64, 8, LANES), F32),
        pltpu.VMEM((12 * 12 * 16, 2 * blocks), BF16),
        pltpu.VMEM((2, 12 * blocks_z // LANES, blocks_x * blocks_y * 12 * 16, LANES), BF16),
        pltpu.VMEM(tile_shape, F32),
    ]
    sizes = (blocks_x, blocks_y, blocks_z)
    cost = (300 * blocks * 512, 4 << 20)
    tile = call(
        functools.partial(deposit_kernel, *sizes, False), shape(*tile_shape), scratch, 32, *cost
    )(arrived[0], arrived_labels[0])
    middle, x_rims, y_rims = call(
        functools.partial(deposit_kernel, *sizes, True),
        (
            shape(rows_x, rows_y, cells_z), shape(2, 2, rows_y, cells_z),
            shape(2, rows_x + 4, 2, cells_z),
        ),
        scratch, 32, *cost,
    )(arrived[1], arrived_labels[1], tile)

    y_sides = send(y_rims[1], "py", 1), send(y_rims[0], "py", -1)
    x_rims = call(corner_kernel, shape(*x_rims.shape), [], 4, 8 * rows_y * cells_z, 1 << 17)(
        x_rims, *y_sides
    )
    x_sides = send(x_rims[1], "px", 1), send(x_rims[0], "px", -1)
    density = call(rim_kernel, shape(rows_x, rows_y, cells_z), [], 8, inner * cells_z, 2 << 20)(
        middle, *y_sides, *x_sides
    )
    return (displacement, density)


def solution(mesh):
    return jax.shard_map(
        per_device,
        mesh=mesh,
        in_specs=(P("px", "py", None), P("px", "py", None, None), P("px", "py", None)),
        out_specs=(P(None, "px", "py", None), P("px", "py", None)),
        check_vma=False,
    )
```
